32 devices in a mesh: depth: 8 (over z, core), wave: 4 (over y, x).
Axes of the slice: x: 2, y: 2, z: 4, core: 2. Of those that a mesh axis runs over, the one named last changes fastest.
Arguments:
- rhs: float32 [2, 64, 32, 4096], P(None, 'depth', None, 'wave'), may hold values from -0.8 to 0.8
- cotangent: float32 [2, 64, 32, 4096], P(None, 'depth', None, 'wave'), may hold values from -0.8 to 0.8
- thickness: float32 [64], replicated, may hold values from 0.5 to 2
- ky_shift: float32 [32], replicated, may hold values from 1e-05 to 0.001
Outputs:
- pressure: float32 [2, 64, 32, 4096], P(None, 'depth', None, 'wave')
- adjoint_field: float32 [2, 64, 32, 4096], P(None, 'depth', None, 'wave')
The draws below stay inside these ranges and needn't reach their ends.
All inputs are finite; a program needn't handle non-finite values.
Results may differ from the reference program's by a relative error of at most 0.0003.
Values sent between devices are 32-bit elements; how exact they have to be, the bound alone decides.
No kernel may reach another device: no remote copies, remote signals or barrier semaphores. Data moves between devices by JAX's collectives and lax.ppermute only.
A program may use at most 192 MiB of HBM per device.

```python
import math
import jax
import jax.numpy as jnp
from jax import lax

NX = 4096
KY = 32
NZ = 64


def levels(own_key, shape, split, low, high):
    factor_of, own = 1.0, jax.random.fold_in(own_key, 6)
    for axis_at, parts in split:
        draws = jnp.exp(jax.random.uniform(jax.random.fold_in(own, axis_at), (parts,), jnp.float32, low / len(split), high / len(split)))
        factor_of = factor_of * jnp.repeat(draws, shape[axis_at] // parts).reshape([-1 if axis == axis_at else 1 for axis in range(len(shape))])
    return factor_of


def bell_draw(stream_key, dims, scale, reach, cuts=(), held_as=jnp.bfloat16):
    level = levels(stream_key, dims, cuts, -0.22, 0.18) if cuts else 1.0
    values = jax.random.normal(stream_key, dims, jnp.float32) * scale * level
    return jnp.minimum(jnp.maximum(values, -reach), reach).astype(held_as)


def setup_inputs(seed: int = 0) -> dict:
    keys = jax.random.split(jax.random.key(seed), 5)
    rhs = bell_draw(keys[0], (2, NZ, KY, NX), 0.1, 0.8, ((1, 8), (3, 4)), jnp.float32)
    cotangent = bell_draw(keys[1], (2, NZ, KY, NX), 0.1, 0.8, ((1, 8), (3, 4)), jnp.float32)
    thickness = jnp.clip(jnp.exp(jax.random.uniform(keys[2], (NZ,), jnp.float32, math.log(0.5), math.log(2.0))), 0.5, 2.0)
    ky_shift = jnp.clip(jnp.exp(jax.random.uniform(keys[3], (KY,), jnp.float32, math.log(9.999999747378752e-06), math.log(0.001))), 9.999999747378752e-06, 0.001)
    return dict(rhs=rhs, cotangent=cotangent, thickness=thickness, ky_shift=ky_shift)


aspect_ratio = 1.0

def level_terms(thickness):
    inner_face = 2.0 / (thickness[:-1] + thickness[1:])
    nothing = jnp.zeros((1,), jnp.float32)
    top_face = 2.0 / thickness[:1]
    below_face = jnp.concatenate([inner_face, nothing])
    above_face = jnp.concatenate([top_face, inner_face])
    lower_band = -jnp.concatenate([nothing, inner_face]) / thickness
    upper_band = -below_face / thickness
    centre = (above_face + below_face) / thickness
    return (lower_band, centre, upper_band)

def reference(rhs, cotangent, thickness, ky_shift):
    lower_band, centre, upper_band = level_terms(thickness)
    nothing = jnp.zeros((1,), jnp.float32)
    lower_transposed = jnp.concatenate([nothing, upper_band[:-1]])
    upper_transposed = jnp.concatenate([lower_band[1:], nothing])
    wavenumber = jnp.arange(NX).astype(jnp.float32)
    horizontal = aspect_ratio * 4.0 * jnp.sin(math.pi * wavenumber / NX) ** 2

    def solve_field(row_field, diagonal, lower_use, upper_use):
        spectrum = jnp.fft.fft(row_field[0] + 1j * row_field[1], axis=-1)
        stacked = jnp.stack([jnp.real(spectrum).T, jnp.imag(spectrum).T], -1)
        lower_wide = jnp.broadcast_to(lower_use[None, :], (NX, NZ))
        upper_wide = jnp.broadcast_to(upper_use[None, :], (NX, NZ))
        solution = lax.linalg.tridiagonal_solve(lower_wide, diagonal, upper_wide, stacked)
        physical = jnp.fft.ifft((solution[..., 0] + 1j * solution[..., 1]).T, axis=-1)
        return jnp.stack([jnp.real(physical), jnp.imag(physical)])[:, :, None, :]

    def solve_row(row_index, outputs):
        pressure_acc, adjoint_acc = outputs
        row_index = row_index.astype(jnp.int32)
        rhs_row = lax.dynamic_index_in_dim(rhs, row_index, 2, keepdims=False)
        cotangent_row = lax.dynamic_index_in_dim(cotangent, row_index, 2, keepdims=False)
        shift_value = lax.dynamic_index_in_dim(ky_shift, row_index, 0, keepdims=False)
        diagonal = centre[None, :] + shift_value + horizontal[:, None]
        pressure_row = solve_field(rhs_row, diagonal, lower_band, upper_band)
        adjoint_row = solve_field(cotangent_row, diagonal, lower_transposed, upper_transposed)
        zero_index = jnp.zeros((), jnp.int32)
        start = (zero_index, zero_index, row_index, zero_index)
        pressure_acc = lax.dynamic_update_slice(pressure_acc, pressure_row.astype(pressure_acc.dtype), start)
        adjoint_acc = lax.dynamic_update_slice(adjoint_acc, adjoint_row.astype(adjoint_acc.dtype), start)
        return (pressure_acc, adjoint_acc)
    initial = (jnp.zeros_like(rhs), jnp.zeros_like(cotangent))
    pressure, adjoint_field = lax.fori_loop(0, KY, solve_row, initial)
    return (pressure, adjoint_field)
```

```python
import functools
import math

import jax
import jax.numpy as jnp
import numpy as np
from jax import lax
from jax.experimental import pallas as pl
from jax.experimental.pallas import tpu as pltpu
from jax.sharding import PartitionSpec as P

aspect_ratio = 1.0
LANES = 128
ROWS = 8
VMEM_BYTES = 24 * 1024 * 1024
real_dot = functools.partial(jnp.dot, preferred_element_type=jnp.float32)


def butterflies(values, orient):
    size = len(values)
    if size == 1:
        return values
    even = butterflies(values[0::2], orient)
    odd = butterflies(values[1::2], orient)
    low, high = [], []
    half = size // 2
    for at in range(half):
        (er, ei), (re, im) = even[at], odd[at]
        if at == 0:
            tr, ti = re, im
        elif 4 * at == size:
            tr, ti = (-im, re) if orient > 0 else (im, -re)
        elif 8 * at == size:
            root = math.sqrt(0.5)
            tr, ti = root * (re - orient * im), root * (im + orient * re)
        elif 8 * at == 3 * size:
            root = math.sqrt(0.5)
            tr, ti = -root * (re + orient * im), root * (orient * re - im)
        else:
            angle = orient * 2.0 * math.pi * at / size
            c, s = math.cos(angle), math.sin(angle)
            tr, ti = c * re - s * im, s * re + c * im
        low.append((er + tr, ei + ti))
        high.append((er - tr, ei - ti))
    return low + high


def tables(outer, orient):
    full = outer * LANES
    angle = orient * 2.0 * np.pi * np.outer(np.arange(outer), np.arange(LANES)) / full
    wide = lambda a: np.broadcast_to(a[:, None, :], (outer, ROWS, LANES)).astype(np.float32)
    turn = orient * 2.0 * np.pi * (np.outer(np.arange(LANES), np.arange(LANES)) % LANES) / LANES
    c, s = np.cos(turn), np.sin(turn)
    matrix = np.block([[c, s], [-s, c]]).astype(np.float32)
    top = matrix.astype(jnp.bfloat16)
    rest = (matrix - top.astype(np.float32)).astype(jnp.bfloat16)
    return wide(np.cos(angle)), wide(np.sin(angle)), top, rest


def lane_dft(values, top, rest):
    high = values.astype(jnp.bfloat16)
    low = (values - high.astype(jnp.float32)).astype(jnp.bfloat16)
    return real_dot(high, top) + (real_dot(low, top) + real_dot(high, rest))


def coefficient_kernel(levels, total, group, place, thick, face, lam, q_out, p_out, r_out, m_out, end_out, down_out, up_out, r_all, m_all, n_all, u_all, f_all):
    rows = group * ROWS
    shift = lam[...].reshape(rows, LANES)
    zero = jnp.zeros((rows, LANES), jnp.float32)

    def step(j, state):
        f, r, phi, s = state
        m = face[j] * r
        f = shift * thick[j] + jnp.where(j == 0, face[0], m * f)
        r = 1.0 / (face[j + 1] + f)
        m_all[j] = jnp.where(j == 0, 0.0, m)
        r_all[j] = r
        f_all[j] = f
        i = total - 1 - j
        n = face[i + 1] * s
        u = n * phi
        phi = shift * thick[i] + u
        s = 1.0 / (face[i] + phi)
        n_all[i] = n
        u_all[i] = u
        return f, r, phi, s

    lax.fori_loop(0, total, step, (zero, zero, zero, zero))
    first = place[0] * levels
    wide = (group, ROWS, LANES)
    q = jnp.ones((rows, LANES), jnp.float32)
    p = q
    for i in range(levels):
        back = levels - 1 - i
        q_out[back] = q.reshape(wide)
        q = q * m_all[first + back]
        p_out[i] = p.reshape(wide)
        p = p * n_all[first + i]
        r_out[i] = r_all[first + i].reshape(wide)
        m_out[i] = m_all[first + i].reshape(wide)
    last = first + levels - 1
    end_out[0] = n_all[last].reshape(wide)
    end_out[1] = (1.0 / (f_all[last] + u_all[last])).reshape(wide)
    for block in range(total // levels):
        down = m_all[block * levels]
        up = n_all[block * levels]
        for i in range(1, levels):
            down = down * m_all[block * levels + i]
            up = up * n_all[block * levels + i]
        down_out[block] = down.reshape(wide)
        up_out[block] = up.reshape(wide)


def coefficients(place, thick, face, lam, levels):
    outer = lam.shape[0]
    total = thick.shape[0]
    count = total // levels
    group = min(8, outer)
    tall = lambda n: pl.BlockSpec((n, group, ROWS, LANES), lambda g: (0, g, 0, 0))
    shape = lambda n: jax.ShapeDtypeStruct((n, outer, ROWS, LANES), jnp.float32)
    smem = pl.BlockSpec(memory_space=pltpu.SMEM)
    sizes = (levels, levels, levels, levels, 2, count, count)
    return pl.pallas_call(
        functools.partial(coefficient_kernel, levels, total, group),
        grid=(outer // group,),
        in_specs=[smem, smem, smem, pl.BlockSpec((group, ROWS, LANES), lambda g: (g, 0, 0))],
        out_specs=[tall(n) for n in sizes],
        out_shape=[shape(n) for n in sizes],
        scratch_shapes=[pltpu.VMEM((total, group * ROWS, LANES), jnp.float32)] * 5,
        compiler_params=pltpu.CompilerParams(vmem_limit_bytes=2 * VMEM_BYTES),
        name="coefficients",
    )(place, thick, face, lam)


def forward_kernel(scale, x, tw_cos, tw_sin, top, rest, q, p, b_out, c_out, lhs):
    at = pl.program_id(0)
    waves, _, _, _, local = x.shape
    per = local // LANES
    outer = waves * per

    def piece(part, s):
        return x[s // per, part, 0, :, (s % per) * LANES:(s % per + 1) * LANES]

    turned = butterflies([(piece(0, s), piece(1, s)) for s in range(outer)], -1.0)
    for k, (re, im) in enumerate(turned):
        c, s = tw_cos[k], tw_sin[k]
        lhs[k * ROWS:(k + 1) * ROWS, :LANES] = re * c - im * s
        lhs[k * ROWS:(k + 1) * ROWS, LANES:] = re * s + im * c
    y = lane_dft(lhs[...], top[...], rest[...]) * scale[at]

    @pl.when(at == 0)
    def _():
        c_out[...] = jnp.zeros_like(c_out)

    for part in range(2):
        b = y[:, part * LANES:(part + 1) * LANES].reshape(outer, ROWS, LANES)
        b_out[part, 0] = b
        c_out[:, 0, part] += q[0] * b
        c_out[:, 1, part] += p[0] * b


def forward(x, scale, q, p):
    waves, _, levels, _, local = x.shape
    outer = waves * local // LANES
    consts = tables(outer, -1.0)
    whole = lambda a: pl.BlockSpec(a.shape, lambda l: (0,) * a.ndim)
    level = pl.BlockSpec((1, outer, ROWS, LANES), lambda l: (l, 0, 0, 0))
    return pl.pallas_call(
        forward_kernel,
        grid=(levels,),
        in_specs=[
            pl.BlockSpec(memory_space=pltpu.SMEM),
            pl.BlockSpec((waves, 2, 1, ROWS, local), lambda l: (0, 0, l, 0, 0)),
            *[whole(a) for a in consts],
            level,
            level,
        ],
        out_specs=[
            pl.BlockSpec((2, 1, outer, ROWS, LANES), lambda l: (0, l, 0, 0, 0)),
            pl.BlockSpec((outer, 2, 2, ROWS, LANES), lambda l: (0, 0, 0, 0, 0)),
        ],
        out_shape=[
            jax.ShapeDtypeStruct((2, levels, outer, ROWS, LANES), jnp.float32),
            jax.ShapeDtypeStruct((outer, 2, 2, ROWS, LANES), jnp.float32),
        ],
        scratch_shapes=[pltpu.VMEM((outer * ROWS, 2 * LANES), jnp.float32)],
        compiler_params=pltpu.CompilerParams(vmem_limit_bytes=VMEM_BYTES),
        name="forward",
    )(scale, x, *consts, q, p)


def join_kernel(c, down, up, out):
    count = c.shape[0]
    y = jnp.zeros(c.shape[1:2] + c.shape[3:], jnp.float32)
    z = y
    for block in range(count):
        out[block, :, 0] = y
        y = c[block, :, 0] + down[block][:, None] * y
        back = count - 1 - block
        out[back, :, 1] = z
        z = c[back, :, 1] + up[back][:, None] * z


def join(c, down, up):
    return pl.pallas_call(
        join_kernel,
        out_shape=jax.ShapeDtypeStruct(c.shape, jnp.float32),
        compiler_params=pltpu.CompilerParams(vmem_limit_bytes=VMEM_BYTES),
        name="join",
    )(c, down, up)


def backward_kernel(scale, b, ends, r, m, end, tw_cos, tw_sin, top, rest, out, y_all, now):
    at = pl.program_id(0)
    waves, _, _, _, local = out.shape
    per = local // LANES
    levels, outer = r.shape[:2]
    rows = outer * ROWS

    @pl.when(at == 0)
    def _():
        for part in range(2):
            y = ends[:, 0, part]
            for j in range(levels):
                y = b[part, j] + m[j] * y
                y_all[part, j] = y
            now[part] = (y + end[0] * ends[:, 1, part]) * end[1]

    level = levels - 1 - at

    @pl.when(at > 0)
    def _():
        for part in range(2):
            now[part] = r[level] * y_all[part, level] + m[level + 1] * now[part]

    spectrum = jnp.concatenate([now[0].reshape(rows, LANES), now[1].reshape(rows, LANES)], 1)
    z = lane_dft(spectrum, top[...], rest[...]) * scale[level]
    pairs = []
    for k in range(outer):
        re = z[k * ROWS:(k + 1) * ROWS, :LANES]
        im = z[k * ROWS:(k + 1) * ROWS, LANES:]
        c, s = tw_cos[k], tw_sin[k]
        pairs.append((re * c - im * s, re * s + im * c))
    for s, pair in enumerate(butterflies(pairs, 1.0)):
        for part in range(2):
            out[s // per, part, 0, :, (s % per) * LANES:(s % per + 1) * LANES] = pair[part]


def backward(b, ends, r, m, end, scale, waves):
    _, levels, outer, _, _ = b.shape
    local = outer * LANES // waves
    consts = tables(outer, 1.0)
    whole = lambda a: pl.BlockSpec(a.shape, lambda l: (0,) * a.ndim)
    return pl.pallas_call(
        backward_kernel,
        grid=(levels,),
        in_specs=[pl.BlockSpec(memory_space=pltpu.SMEM)] + [whole(a) for a in (b, ends, r, m, end, *consts)],
        out_specs=pl.BlockSpec((waves, 2, 1, ROWS, local), lambda l: (0, 0, levels - 1 - l, 0, 0)),
        out_shape=jax.ShapeDtypeStruct((waves, 2, levels, ROWS, local), jnp.float32),
        scratch_shapes=[
            pltpu.VMEM((2, levels, outer, ROWS, LANES), jnp.float32),
            pltpu.VMEM((2, outer, ROWS, LANES), jnp.float32),
        ],
        compiler_params=pltpu.CompilerParams(vmem_limit_bytes=VMEM_BYTES),
        name="backward",
    )(scale, b, ends, r, m, end, *consts)


def swap(a, axis):
    return lax.all_to_all(a, axis, split_axis=0, concat_axis=0, tiled=True)


def shards(rhs, cotangent, thickness, ky_shift):
    waves = lax.axis_size("wave")
    count = lax.axis_size("depth")
    depth_pos = lax.axis_index("depth")
    wave_pos = lax.axis_index("wave")
    _, levels, ky, local = rhs.shape
    full = waves * local
    ky_local = ky // waves
    spare = -ky_local % ROWS

    def pack(a):
        a = a.reshape(2, levels, waves, ky_local, local)
        return a.transpose(2, 0, 1, 3, 4)

    def unpack(a):
        return a.transpose(1, 2, 0, 3, 4).reshape(2, levels, ky, local)

    def pad(a):
        return jnp.pad(a, [(0, 0)] * 3 + [(0, spare), (0, 0)]) if spare else a

    def trim(a):
        return a[:, :, :, :ky_local] if spare else a

    rhs_in = swap(pack(rhs), "wave")
    rhs_in, cotangent = lax.optimization_barrier((rhs_in, cotangent))
    cotangent_in = swap(pack(cotangent), "wave")

    inner_face = 2.0 / (thickness[:-1] + thickness[1:])
    face = jnp.concatenate([2.0 / thickness[:1], inner_face, jnp.zeros((1,), jnp.float32)])
    outer = full // LANES
    wavenumber = np.arange(outer)[:, None] + outer * np.arange(LANES)[None, :]
    wavenumber = jnp.asarray(wavenumber, jnp.float32)
    horizontal = aspect_ratio * 4.0 * jnp.sin(math.pi * wavenumber / full) ** 2
    shifts = lax.dynamic_slice_in_dim(ky_shift, wave_pos * ky_local, ky_local)
    shifts = jnp.pad(shifts, (0, spare), constant_values=1.0)
    lam = shifts[None, :, None] + horizontal[:, None, :]
    place = depth_pos.astype(jnp.int32).reshape(1)
    q, p, r, m, end, down, up = coefficients(place, thickness, face, lam, levels)
    share = outer // count
    down = lax.dynamic_slice_in_dim(down, depth_pos * share, share, 1)
    up = lax.dynamic_slice_in_dim(up, depth_pos * share, share, 1)
    thick_here = lax.dynamic_slice_in_dim(thickness, depth_pos * levels, levels)
    even = jnp.ones_like(thick_here)

    def solve(field, before, after):
        b, c = forward(pad(field), before, q, p)
        c = swap(c.reshape((count, share) + c.shape[1:]), "depth")
        ends = swap(join(c, down, up), "depth").reshape((outer, 2, 2, ROWS, LANES))
        return trim(backward(b, ends, r, m, end, after / full, waves))

    pressure = swap(solve(rhs_in, thick_here, even), "wave")
    adjoint = solve(cotangent_in, even, thick_here)
    pressure, adjoint = lax.optimization_barrier((pressure, adjoint))
    adjoint = swap(adjoint, "wave")
    return unpack(pressure), unpack(adjoint)


def solution(mesh):
    spec = P(None, "depth", None, "wave")
    return jax.shard_map(shards, mesh=mesh, in_specs=(spec, spec, P(), P()), out_specs=(spec, spec), check_vma=False)
```

```python
import functools
import math

import jax
import jax.numpy as jnp
import numpy as np
from jax import lax
from jax.experimental import pallas as pl
from jax.experimental.pallas import tpu as pltpu
from jax.sharding import PartitionSpec as P

aspect_ratio = 1.0
LANES = 128
ROWS = 8
VMEM_BYTES = 56 * 1024 * 1024
real_dot = functools.partial(jnp.dot, preferred_element_type=jnp.float32)


def butterflies(values, orient):
    size = len(values)
    if size == 1:
        return values
    even = butterflies(values[0::2], orient)
    odd = butterflies(values[1::2], orient)
    low, high = [], []
    half = size // 2
    for at in range(half):
        (er, ei), (re, im) = even[at], odd[at]
        if at == 0:
            tr, ti = re, im
        elif 4 * at == size:
            tr, ti = (-im, re) if orient > 0 else (im, -re)
        elif 8 * at == size:
            root = math.sqrt(0.5)
            tr, ti = root * (re - orient * im), root * (im + orient * re)
        elif 8 * at == 3 * size:
            root = math.sqrt(0.5)
            tr, ti = -root * (re + orient * im), root * (orient * re - im)
        else:
            angle = orient * 2.0 * math.pi * at / size
            c, s = math.cos(angle), math.sin(angle)
            tr, ti = c * re - s * im, s * re + c * im
        low.append((er + tr, ei + ti))
        high.append((er - tr, ei - ti))
    return low + high


def tables(outer, orient):
    full = outer * LANES
    angle = orient * 2.0 * np.pi * np.outer(np.arange(outer), np.arange(LANES)) / full
    wide = lambda a: np.broadcast_to(a[:, None, :], (outer, ROWS, LANES)).astype(np.float32)
    turn = orient * 2.0 * np.pi * (np.outer(np.arange(LANES), np.arange(LANES)) % LANES) / LANES
    c, s = np.cos(turn), np.sin(turn)
    matrix = np.block([[c, s], [-s, c]]).astype(np.float32)
    top = matrix.astype(jnp.bfloat16)
    rest = (matrix - top.astype(np.float32)).astype(jnp.bfloat16)
    return wide(np.cos(angle)), wide(np.sin(angle)), top, rest


def lane_dft(values, top, rest):
    high = values.astype(jnp.bfloat16)
    low = (values - high.astype(jnp.float32)).astype(jnp.bfloat16)
    return real_dot(high, top) + (real_dot(low, top) + real_dot(high, rest))


def coefficient_kernel(levels, total, group, place, thick, face, lam, q_out, p_out, r_out, m_out, end_out, pair_out, far_out, r_all, m_all, n_all, u_all, f_all, down_all, up_all):
    rows = group * ROWS
    shift = lam[...].reshape(rows, LANES)
    zero = jnp.zeros((rows, LANES), jnp.float32)

    def step(j, state):
        f, r, phi, s = state
        m = face[j] * r
        f = shift * thick[j] + jnp.where(j == 0, face[0], m * f)
        r = 1.0 / (face[j + 1] + f)
        m_all[j] = jnp.where(j == 0, 0.0, m)
        r_all[j] = r
        f_all[j] = f
        i = total - 1 - j
        n = face[i + 1] * s
        u = n * phi
        phi = shift * thick[i] + u
        s = 1.0 / (face[i] + phi)
        n_all[i] = n
        u_all[i] = u
        return f, r, phi, s

    lax.fori_loop(0, total, step, (zero, zero, zero, zero))
    first = place[0] * levels
    wide = (group, ROWS, LANES)
    q = jnp.ones((rows, LANES), jnp.float32)
    p = q
    for i in range(levels):
        back = levels - 1 - i
        q_out[back] = q.reshape(wide)
        q = q * m_all[first + back]
        p_out[i] = p.reshape(wide)
        p = p * n_all[first + i]
        r_out[i] = r_all[first + i].reshape(wide)
        m_out[i] = m_all[first + i].reshape(wide)
    last = first + levels - 1
    end_out[0] = n_all[last].reshape(wide)
    end_out[1] = (1.0 / (f_all[last] + u_all[last])).reshape(wide)

    blocks = total // levels
    for block in range(blocks):
        down = m_all[block * levels]
        up = n_all[block * levels]
        for i in range(1, levels):
            down = down * m_all[block * levels + i]
            up = up * n_all[block * levels + i]
        down_all[block] = down
        up_all[block] = up

    chips = blocks // 2
    chip = place[0] // 2
    for core in range(2):
        pair_out[core] = down_all[2 * chip + core].reshape(wide)
        pair_out[2 + core] = up_all[2 * chip + core].reshape(wide)
    above, below = [jnp.ones((rows, LANES), jnp.float32)], [jnp.ones((rows, LANES), jnp.float32)]
    for apart in range(1, chips - 1):
        one = jnp.maximum(chip - apart, 0)
        above.append(above[-1] * down_all[2 * one] * down_all[2 * one + 1])
        one = jnp.minimum(chip + apart, chips - 1)
        below.append(below[-1] * up_all[2 * one] * up_all[2 * one + 1])
    for apart in range(1, chips):
        far_out[apart - 1] = jnp.where(chip >= apart, above[apart - 1], below[chips - apart - 1]).reshape(wide)


def coefficients(place, thick, face, lam, levels):
    outer = lam.shape[0]
    total = thick.shape[0]
    count = total // levels
    group = min(8, outer)
    tall = lambda n: pl.BlockSpec((n, group, ROWS, LANES), lambda g: (0, g, 0, 0))
    shape = lambda n: jax.ShapeDtypeStruct((n, outer, ROWS, LANES), jnp.float32)
    smem = pl.BlockSpec(memory_space=pltpu.SMEM)
    sizes = (levels, levels, levels, levels, 2, 4, count // 2 - 1)
    return pl.pallas_call(
        functools.partial(coefficient_kernel, levels, total, group),
        grid=(outer // group,),
        in_specs=[smem, smem, smem, pl.BlockSpec((group, ROWS, LANES), lambda g: (g, 0, 0))],
        out_specs=[tall(n) for n in sizes],
        out_shape=[shape(n) for n in sizes],
        scratch_shapes=[pltpu.VMEM((total, group * ROWS, LANES), jnp.float32)] * 5
        + [pltpu.VMEM((count, group * ROWS, LANES), jnp.float32)] * 2,
        compiler_params=pltpu.CompilerParams(vmem_limit_bytes=VMEM_BYTES),
        name="coefficients",
    )(place, thick, face, lam)


def forward_kernel(waves, place, scale, *refs):
    at = pl.program_id(0)
    blocks = refs[:waves]
    tw_cos, tw_sin, top, rest, q, p, b_out, keep_out, give_out, x, lhs, c_all = refs[waves:]
    local = x.shape[-1]
    per = local // LANES
    outer = waves * per
    half = outer // 2
    for s in range(waves):
        x[place[1] ^ s] = blocks[s][:, 0]

    def piece(part, s):
        return x[s // per, part, :, (s % per) * LANES:(s % per + 1) * LANES]

    turned = butterflies([(piece(0, s), piece(1, s)) for s in range(outer)], -1.0)
    for k, (re, im) in enumerate(turned):
        c, s = tw_cos[k], tw_sin[k]
        lhs[k * ROWS:(k + 1) * ROWS, :LANES] = re * c - im * s
        lhs[k * ROWS:(k + 1) * ROWS, LANES:] = re * s + im * c
    y = lane_dft(lhs[...], top[...], rest[...]) * scale[at]

    @pl.when(at == 0)
    def _():
        c_all[...] = jnp.zeros_like(c_all)

    for part in range(2):
        b = y[:, part * LANES:(part + 1) * LANES].reshape(outer, ROWS, LANES)
        b_out[part, 0] = b
        c_all[:, 0, part] += q[0] * b
        c_all[:, 1, part] += p[0] * b

    @pl.when(at == pl.num_programs(0) - 1)
    def _():
        core = place[0] % 2
        keep_out[...] = c_all[pl.ds(core * half, half)]
        give_out[...] = c_all[pl.ds((1 - core) * half, half)]


def forward(place, blocks, scale, q, p):
    waves = len(blocks)
    _, levels, _, local = blocks[0].shape
    outer = waves * local // LANES
    consts = tables(outer, -1.0)
    whole = lambda a: pl.BlockSpec(a.shape, lambda l: (0,) * a.ndim)
    level = pl.BlockSpec((1, outer, ROWS, LANES), lambda l: (l, 0, 0, 0))
    smem = pl.BlockSpec(memory_space=pltpu.SMEM)
    half = (outer // 2, 2, 2, ROWS, LANES)
    return pl.pallas_call(
        functools.partial(forward_kernel, waves),
        grid=(levels,),
        in_specs=[
            smem,
            smem,
            *[pl.BlockSpec((2, 1, ROWS, local), lambda l: (0, l, 0, 0))] * waves,
            *[whole(a) for a in consts],
            level,
            level,
        ],
        out_specs=[
            pl.BlockSpec((2, 1, outer, ROWS, LANES), lambda l: (0, l, 0, 0, 0)),
            *[pl.BlockSpec(half, lambda l: (0, 0, 0, 0, 0))] * 2,
        ],
        out_shape=[
            jax.ShapeDtypeStruct((2, levels, outer, ROWS, LANES), jnp.float32),
            *[jax.ShapeDtypeStruct(half, jnp.float32)] * 2,
        ],
        scratch_shapes=[
            pltpu.VMEM((waves, 2, ROWS, local), jnp.float32),
            pltpu.VMEM((outer * ROWS, 2 * LANES), jnp.float32),
            pltpu.VMEM((outer, 2, 2, ROWS, LANES), jnp.float32),
        ],
        compiler_params=pltpu.CompilerParams(vmem_limit_bytes=VMEM_BYTES),
        name="forward",
    )(place, scale, *blocks, *consts, q, p)


def chip_kernel(chips, place, keep, got, pair, *outs):
    chip = place[0] // 2
    upper = place[0] % 2 == 0
    above, below = keep[...], got[...]
    first, second = jnp.where(upper, above, below), jnp.where(upper, below, above)
    down = second[:, 0] + pair[1][:, None] * first[:, 0]
    up = first[:, 1] + pair[2][:, None] * second[:, 1]
    for apart in range(1, chips):
        outs[apart - 1][...] = jnp.where(chip + apart < chips, down, up)


def chip_sums(place, keep, got, pair, chips):
    half = keep.shape[0]
    full = pl.BlockSpec(keep.shape, lambda i, place: (0,) * keep.ndim)
    shape = (half, 2, ROWS, LANES)
    return pl.pallas_call(
        functools.partial(chip_kernel, chips),
        grid_spec=pltpu.PrefetchScalarGridSpec(
            num_scalar_prefetch=1,
            grid=(1,),
            in_specs=[full, full, pl.BlockSpec((4, half, ROWS, LANES), lambda i, place: (0, place[0] % 2, 0, 0))],
            out_specs=[pl.BlockSpec(shape, lambda i, place: (0, 0, 0, 0))] * (chips - 1),
        ),
        out_shape=[jax.ShapeDtypeStruct(shape, jnp.float32)] * (chips - 1),
        compiler_params=pltpu.CompilerParams(vmem_limit_bytes=VMEM_BYTES),
        name="chip_sums",
    )(place, keep, got, pair)


def join_kernel(chips, place, keep, got, pair, far, *refs):
    news = refs[:chips - 1]
    mine, theirs = refs[chips - 1:]
    chip = place[0] // 2
    upper = place[0] % 2 == 0
    first, second = jnp.where(upper, keep[...], got[...]), jnp.where(upper, got[...], keep[...])
    down = jnp.zeros(first.shape[:1] + first.shape[2:], jnp.float32)
    up = down
    for apart in range(1, chips):
        term = far[apart - 1][:, None] * news[apart - 1][...]
        down = down + jnp.where(chip >= apart, term, 0.0)
        up = up + jnp.where(chip >= apart, 0.0, term)
    inner_up = second[:, 1] + pair[3][:, None] * up
    inner_down = first[:, 0] + pair[0][:, None] * down
    mine[:, 0] = jnp.where(upper, down, inner_down)
    mine[:, 1] = jnp.where(upper, inner_up, up)
    theirs[:, 0] = jnp.where(upper, inner_down, down)
    theirs[:, 1] = jnp.where(upper, up, inner_up)


def join(place, keep, got, pair, far, news):
    half = keep.shape[0]
    chips = len(news) + 1
    full = lambda a: pl.BlockSpec(a.shape, lambda i, place: (0,) * a.ndim)
    part = lambda n: pl.BlockSpec((n, half, ROWS, LANES), lambda i, place: (0, place[0] % 2, 0, 0))
    return pl.pallas_call(
        functools.partial(join_kernel, chips),
        grid_spec=pltpu.PrefetchScalarGridSpec(
            num_scalar_prefetch=1,
            grid=(1,),
            in_specs=[full(keep), full(got), part(4), part(chips - 1), *[full(a) for a in news]],
            out_specs=[full(keep)] * 2,
        ),
        out_shape=[jax.ShapeDtypeStruct(keep.shape, jnp.float32)] * 2,
        compiler_params=pltpu.CompilerParams(vmem_limit_bytes=VMEM_BYTES),
        name="join",
    )(place, keep, got, pair, far, *news)


def backward_kernel(waves, place, scale, b, mine, theirs, r, m, end, tw_cos, tw_sin, top, rest, *refs):
    at = pl.program_id(0)
    outs = refs[:waves]
    y_all, now, x = refs[waves:]
    local = x.shape[-1]
    per = local // LANES
    levels, outer = r.shape[:2]
    rows = outer * ROWS
    half = outer // 2

    @pl.when(at == 0)
    def _():
        core = place[0] % 2
        for source, start in ((mine, core * half), (theirs, (1 - core) * half)):
            here = pl.ds(start, half)
            for part in range(2):
                y = source[:, 0, part]
                for j in range(levels):
                    y = b[part, j, here] + m[j, here] * y
                    y_all[part, j, here] = y
                now[part, here] = (y + end[0, here] * source[:, 1, part]) * end[1, here]

    level = levels - 1 - at

    @pl.when(at > 0)
    def _():
        for part in range(2):
            now[part] = r[level] * y_all[part, level] + m[level + 1] * now[part]

    spectrum = jnp.concatenate([now[0].reshape(rows, LANES), now[1].reshape(rows, LANES)], 1)
    z = lane_dft(spectrum, top[...], rest[...]) * scale[level]
    pairs = []
    for k in range(outer):
        re = z[k * ROWS:(k + 1) * ROWS, :LANES]
        im = z[k * ROWS:(k + 1) * ROWS, LANES:]
        c, s = tw_cos[k], tw_sin[k]
        pairs.append((re * c - im * s, re * s + im * c))
    for s, pair in enumerate(butterflies(pairs, 1.0)):
        for part in range(2):
            x[s // per, part, :, (s % per) * LANES:(s % per + 1) * LANES] = pair[part]
    for s in range(waves):
        outs[s][:, 0] = x[place[1] ^ s]


def backward(place, b, mine, theirs, r, m, end, scale, waves):
    _, levels, outer, _, _ = b.shape
    local = outer * LANES // waves
    consts = tables(outer, 1.0)
    whole = lambda a: pl.BlockSpec(a.shape, lambda l: (0,) * a.ndim)
    smem = pl.BlockSpec(memory_space=pltpu.SMEM)
    return pl.pallas_call(
        functools.partial(backward_kernel, waves),
        grid=(levels,),
        in_specs=[smem, smem] + [whole(a) for a in (b, mine, theirs, r, m, end, *consts)],
        out_specs=[pl.BlockSpec((2, 1, ROWS, local), lambda l: (0, levels - 1 - l, 0, 0))] * waves,
        out_shape=[jax.ShapeDtypeStruct((2, levels, ROWS, local), jnp.float32)] * waves,
        scratch_shapes=[
            pltpu.VMEM((2, levels, outer, ROWS, LANES), jnp.float32),
            pltpu.VMEM((2, outer, ROWS, LANES), jnp.float32),
            pltpu.VMEM((waves, 2, ROWS, local), jnp.float32),
        ],
        compiler_params=pltpu.CompilerParams(vmem_limit_bytes=VMEM_BYTES),
        name="backward",
    )(place, scale, b, mine, theirs, r, m, end, *consts)


def shards(rhs, cotangent, thickness, ky_shift):
    waves = lax.axis_size("wave")
    count = lax.axis_size("depth")
    depth_pos = lax.axis_index("depth")
    wave_pos = lax.axis_index("wave")
    _, levels, ky, local = rhs.shape
    full = waves * local
    ky_local = ky // waves
    spare = -ky_local % ROWS
    chips = count // 2
    place = jnp.stack([depth_pos, wave_pos]).astype(jnp.int32)

    def exchange(blocks):
        turns = [[(w, w ^ s) for w in range(waves)] for s in range(waves)]
        return [blocks[0]] + [lax.ppermute(blocks[s], "wave", turns[s]) for s in range(1, waves)]

    def cut(a):
        return [lax.dynamic_slice_in_dim(a, (wave_pos ^ s) * ky_local, ky_local, 2) for s in range(waves)]

    def glue(blocks):
        out = jnp.zeros((2, levels, ky, local), jnp.float32)
        for s in range(waves):
            out = lax.dynamic_update_slice_in_dim(out, blocks[s], (wave_pos ^ s) * ky_local, 2)
        return out

    def pad(a):
        return jnp.pad(a, [(0, 0)] * 2 + [(0, spare), (0, 0)]) if spare else a

    def trim(a):
        return a[:, :, :ky_local] if spare else a

    def across(a):
        return lax.ppermute(a, "depth", [(d, d ^ 1) for d in range(count)])

    def along(a, apart):
        return lax.ppermute(a, "depth", [(d, (d + 2 * apart) % count) for d in range(count)])

    rhs_in = exchange(cut(rhs))
    cotangent_in = exchange(cut(cotangent))

    inner_face = 2.0 / (thickness[:-1] + thickness[1:])
    face = jnp.concatenate([2.0 / thickness[:1], inner_face, jnp.zeros((1,), jnp.float32)])
    outer = full // LANES
    wavenumber = np.arange(outer)[:, None] + outer * np.arange(LANES)[None, :]
    wavenumber = jnp.asarray(wavenumber, jnp.float32)
    horizontal = aspect_ratio * 4.0 * jnp.sin(math.pi * wavenumber / full) ** 2
    shifts = lax.dynamic_slice_in_dim(ky_shift, wave_pos * ky_local, ky_local)
    shifts = jnp.pad(shifts, (0, spare), constant_values=1.0)
    lam = shifts[None, :, None] + horizontal[:, None, :]
    q, p, r, m, end, pair, far = coefficients(place, thickness, face, lam, levels)
    thick_here = lax.dynamic_slice_in_dim(thickness, depth_pos * levels, levels)
    even = jnp.ones_like(thick_here)

    def solve(blocks, before, after):
        b, keep, give = forward(place, [pad(a) for a in blocks], before, q, p)
        got = across(give)
        sums = chip_sums(place, keep, got, pair, chips)
        news = [along(sums[apart - 1], apart) for apart in range(1, chips)]
        mine, theirs = join(place, keep, got, pair, far, news)
        theirs = across(theirs)
        return [trim(a) for a in backward(place, b, mine, theirs, r, m, end, after / full, waves)]

    pressure = exchange(solve(rhs_in, thick_here, even))
    adjoint = exchange(solve(cotangent_in, even, thick_here))
    return glue(pressure), glue(adjoint)


def solution(mesh):
    spec = P(None, "depth", None, "wave")
    return jax.shard_map(shards, mesh=mesh, in_specs=(spec, spec, P(), P()), out_specs=(spec, spec), check_vma=False)
```

```python
import functools
import math

import jax
import jax.numpy as jnp
import numpy as np
from jax import lax
from jax.experimental import pallas as pl
from jax.experimental.pallas import tpu as pltpu
from jax.sharding import PartitionSpec as P

aspect_ratio = 1.0
LANES = 128
ROWS = 8
VMEM_BYTES = 40 * 1024 * 1024
real_dot = functools.partial(jnp.dot, preferred_element_type=jnp.float32)
exact_dot = functools.partial(lax.dot_general, precision=lax.Precision.HIGHEST, preferred_element_type=jnp.float32)
NN = (((1,), (0,)), ((), ()))
NT = (((1,), (1,)), ((), ()))
in_smem = pl.BlockSpec(memory_space=pltpu.SMEM)
in_vmem = pl.BlockSpec(memory_space=pltpu.VMEM)
params = pltpu.CompilerParams(vmem_limit_bytes=VMEM_BYTES)


def sine_matrix(size):
    turn = np.outer(np.arange(size), np.arange(size)) % (2 * size)
    matrix = np.sin(np.pi * turn / size)
    matrix[0] = 0.0
    matrix[:, 0] = 0.0
    matrix = matrix.astype(np.float32)
    top = matrix.astype(jnp.bfloat16)
    return top, (matrix - top.astype(np.float32)).astype(jnp.bfloat16)


def edge_signs(size):
    lane = np.arange(LANES)
    signs = np.zeros((ROWS, LANES), np.float32)
    signs[0] = 2.0 / size
    signs[1] = np.where(lane % 2 == 1, 2.0 / size, -2.0 / size)
    return signs


def spread_matrix(total):
    lane = np.arange(LANES)
    sign = np.where(lane % 2 == 1, 1.0, -1.0)
    matrix = np.zeros((2, total, total, LANES), np.float32)
    for j in range(total):
        matrix[0, j, j] = 1.0
        matrix[1, j, j] = sign
    return matrix.reshape(2 * total, total * LANES).astype(jnp.bfloat16)


def interface_matrix(waves, count, size):
    classes = waves // 2 + 1
    matrix = np.zeros((classes, waves, 2, 4, count, waves, 4, 2))
    for c in range(classes):
        weight = (1.0 if c in (0, waves // 2) else 2.0) / (size * waves)
        for w in range(waves):
            for e in range(2):
                for v in range(waves):
                    for g in range(2):
                        value = weight * math.cos(2.0 * math.pi * (c * (w + e - v - g) % waves) / waves)
                        for f in range(4):
                            matrix[c, w, e, f, :, v, f, g] = value
    return matrix.reshape(classes * waves * 8, count * waves * 8).astype(np.float32)


def three_parts(values):
    parts = []
    for _ in range(3):
        part = values.astype(jnp.bfloat16)
        values = values - part.astype(jnp.float32)
        parts.append(part)
    return parts


def sine_transform(values, top, rest):
    high = values.astype(jnp.bfloat16)
    low = (values - high.astype(jnp.float32)).astype(jnp.bfloat16)
    return real_dot(high, top) + (real_dot(low, top) + real_dot(high, rest))


def coefficient_kernel(levels, total, place, thick, face, lam, t_out, r_out, m_out, end_out, pair_out, far_out, m_chip, r_chip, f_chip, n_chip, u_chip, down_all, up_all):
    span = 2 * levels
    chips = total // span
    chip = place[0] // 2
    start = chip * span
    shift = lam[...]
    one = jnp.ones_like(shift)
    zero = jnp.zeros_like(shift)

    def down_step(j, f, r):
        m = face[j] * r
        f = shift * thick[j] + m * f
        return m, f, 1.0 / (face[j + 1] + f)

    def up_step(j, phi, s):
        n = face[j + 1] * s
        u = n * phi
        phi = shift * thick[j] + u
        return n, u, phi, 1.0 / (face[j] + phi)

    def down_chip(c, state):
        f, r = state
        product = one
        for i in range(span):
            m, f, r = down_step(c * span + i, f, r)
            t_out[c * span + i] = m
            product = product * m
        down_all[c] = product
        return f, r

    def up_chip(back, state):
        phi, s = state
        c = chips - 1 - back
        product = one
        for i in range(span - 1, -1, -1):
            n, _, phi, s = up_step(c * span + i, phi, s)
            t_out[c * span + i + 1] = n
            product = product * n
        up_all[c] = product
        return phi, s

    f, r = lax.fori_loop(0, chip, down_chip, (one, one))
    for i in range(span):
        m, f, r = down_step(start + i, f, r)
        m_chip[i], f_chip[i], r_chip[i] = m, f, r
    phi, s = lax.fori_loop(0, chips - 1 - chip, up_chip, (zero, zero))
    for i in range(span - 1, -1, -1):
        n, u, phi, s = up_step(start + i, phi, s)
        n_chip[i], u_chip[i] = n, u

    for i in range(levels):
        t_out[start + i] = m_chip[i]
        t_out[start + levels + 1 + i] = n_chip[levels + i]
    upper = place[0] % 2 == 0
    t_out[start + levels] = jnp.where(upper, n_chip[levels - 1], m_chip[levels])
    own = (place[0] % 2) * levels
    for i in range(levels):
        r_out[i] = r_chip[own + i]
        m_out[i] = m_chip[own + i]
    last = own + levels - 1
    end_out[0] = n_chip[last]
    end_out[1] = 1.0 / (f_chip[last] + u_chip[last])
    end_out[2] = f_chip[own] + u_chip[own]
    for core in range(2):
        down, up = m_chip[core * levels], n_chip[core * levels]
        for i in range(1, levels):
            down = down * m_chip[core * levels + i]
            up = up * n_chip[core * levels + i]
        pair_out[core] = down
        pair_out[2 + core] = up
    above, below = [one], [one]
    for apart in range(1, chips - 1):
        above.append(above[-1] * jnp.where(chip >= apart, down_all[jnp.maximum(chip - apart, 0)], one))
        below.append(below[-1] * jnp.where(chip + apart < chips, up_all[jnp.minimum(chip + apart, chips - 1)], one))
    for apart in range(1, chips):
        far_out[apart - 1] = jnp.where(chip >= apart, above[apart - 1], below[chips - apart - 1])


def coefficients(place, thick, face, lam, levels):
    ky, size = lam.shape
    total = thick.shape[0]
    chips = total // (2 * levels)
    group = min(2 * ROWS, ky)
    tall = lambda n: pl.BlockSpec((n, group, size), lambda g: (0, g, 0))
    sizes = (total + 1, levels, levels, 3, 4, chips - 1)
    scratch = lambda n: pltpu.VMEM((n, group, size), jnp.float32)
    return pl.pallas_call(
        functools.partial(coefficient_kernel, levels, total),
        grid=(ky // group,),
        in_specs=[in_smem, in_smem, in_smem, pl.BlockSpec((group, size), lambda g: (g, 0))],
        out_specs=[tall(n) for n in sizes],
        out_shape=[jax.ShapeDtypeStruct((n, ky, size), jnp.float32) for n in sizes],
        scratch_shapes=[scratch(2 * levels)] * 5 + [scratch(chips)] * 2,
        compiler_params=params,
        name="coefficients",
    )(place, thick, face, lam)


def lane_sum(values):
    tiles = [values[:, t * LANES:(t + 1) * LANES] for t in range(values.shape[1] // LANES)]
    while len(tiles) > 1:
        tiles = [a + b for a, b in zip(tiles[0::2], tiles[1::2])]
    return tiles[0]


def forward_kernel(total, place, before, share, x, top, rest, sines, signs, heights, t, r, m, end, b_out, keep_out, give_out, edge_out, c_all, z_all, sums):
    _, levels, ky, size = x.shape
    first = place[0] * levels
    half = ky // 2
    b = sine_transform(x[0].reshape(levels * ky, size), top[...], rest[...]).reshape(levels, ky, size)
    for j in range(levels):
        b_out[0, j] = b[j] * before[j]
    lane = lax.broadcasted_iota(jnp.int32, (ROWS, LANES), 1)
    spot = jnp.where((lane == 1) | (lane == 2), size / 4.0, 0.0)

    def tile(g, _):
        here = pl.ds(pl.multiple_of(g * ROWS, ROWS), ROWS)
        wave = sines[...]
        y = b_out[0, 0, here]
        ys = [y]
        for j in range(1, levels):
            y = b_out[0, j, here] + m[j, here] * y
            ys.append(y)
        c_all[0, here] = y
        value = y * end[1, here]
        z_all[1, here] = value * wave
        for j in range(levels - 1, -1, -1):
            if j < levels - 1:
                value = r[j, here] * ys[j] + m[j + 1, here] * value
            own = jnp.broadcast_to(x[0, j, here, 0:1], (ROWS, LANES)) * (spot * share[j])
            sums[pl.ds(g * ROWS * total + first + j, ROWS, stride=total), :] = lane_sum(value * wave) + own
        z_all[0, here] = value * wave
        c_all[1, here] = value * end[2, here]
        return 0

    lax.fori_loop(0, ky // ROWS, tile, 0)

    def reach_up(back, z):
        j = first - 1 - back
        z = t[j + 1] * z
        sums[pl.ds(j, ky, stride=total), :] = lane_sum(z)
        return z

    def reach_down(ahead, z):
        j = first + levels + ahead
        z = t[j] * z
        sums[pl.ds(j, ky, stride=total), :] = lane_sum(z)
        return z

    lax.fori_loop(0, first, reach_up, z_all[0])
    lax.fori_loop(0, total - levels - first, reach_down, z_all[1])
    edges = exact_dot(signs[...], sums[...], NT)
    edge_out[0] = (edges * heights[...])[:2]
    core = place[0] % 2
    keep_out[:, 0] = c_all[:, pl.ds(pl.multiple_of(core * half, ROWS), half)]
    give_out[:, 0] = c_all[:, pl.ds(pl.multiple_of((1 - core) * half, ROWS), half)]


def forward(place, x, before, share, heights, sines, t, r, m, end):
    _, levels, ky, size = x.shape
    total = t.shape[0] - 1
    top, rest = sine_matrix(size)
    half = (2, 2, ky // 2, size)
    half_spec = pl.BlockSpec((2, 1, ky // 2, size), lambda i: (0, i, 0, 0))
    field = pl.BlockSpec((1, levels, ky, size), lambda i: (i, 0, 0, 0))
    return pl.pallas_call(
        functools.partial(forward_kernel, total),
        grid=(2,),
        in_specs=[in_smem, in_smem, in_smem, field] + [in_vmem] * 9,
        out_specs=[field, half_spec, half_spec, pl.BlockSpec((1, 2, ky * total), lambda i: (i, 0, 0))],
        out_shape=[
            jax.ShapeDtypeStruct(x.shape, jnp.float32),
            jax.ShapeDtypeStruct(half, jnp.float32),
            jax.ShapeDtypeStruct(half, jnp.float32),
            jax.ShapeDtypeStruct((2, 2, ky * total), jnp.float32),
        ],
        scratch_shapes=[
            pltpu.VMEM((2, ky, size), jnp.float32),
            pltpu.VMEM((2, ky, size), jnp.float32),
            pltpu.VMEM((ky * total, LANES), jnp.float32),
        ],
        compiler_params=params,
        name="forward",
    )(place, before, share, x, top, rest, sines, edge_signs(size), heights, t, r, m, end)


def chip_kernel(chips, place, keep, got, pair, *outs):
    chip = place[0] // 2
    upper = place[0] % 2 == 0
    first, second = jnp.where(upper, keep[...], got[...]), jnp.where(upper, got[...], keep[...])
    down = second[0] + pair[1] * first[0]
    up = first[1] + pair[2] * second[1]
    for apart in range(1, chips):
        outs[apart - 1][...] = jnp.where(chip + apart < chips, down, up)


def chip_sums(place, keep, got, pair, chips):
    _, _, half, size = keep.shape
    full = pl.BlockSpec(keep.shape, lambda i, place: (0,) * keep.ndim)
    shape = (2, half, size)
    return pl.pallas_call(
        functools.partial(chip_kernel, chips),
        grid_spec=pltpu.PrefetchScalarGridSpec(
            num_scalar_prefetch=1,
            grid=(1,),
            in_specs=[full, full, pl.BlockSpec((4, half, size), lambda i, place: (0, place[0] % 2, 0))],
            out_specs=[pl.BlockSpec(shape, lambda i, place: (0, 0, 0))] * (chips - 1),
        ),
        out_shape=[jax.ShapeDtypeStruct(shape, jnp.float32)] * (chips - 1),
        compiler_params=params,
        name="chip_sums",
    )(place, keep, got, pair)


def join_kernel(chips, place, keep, got, pair, far, *refs):
    news = refs[:chips - 1]
    mine, theirs = refs[chips - 1:]
    chip = place[0] // 2
    upper = place[0] % 2 == 0
    first, second = jnp.where(upper, keep[...], got[...]), jnp.where(upper, got[...], keep[...])
    down = jnp.zeros(first.shape[1:], jnp.float32)
    up = down
    for apart in range(1, chips):
        term = far[apart - 1] * news[apart - 1][...]
        down = down + jnp.where(chip >= apart, term, 0.0)
        up = up + jnp.where(chip >= apart, 0.0, term)
    inner_up = second[1] + pair[3] * up
    inner_down = first[0] + pair[0] * down
    mine[0] = jnp.where(upper, down, inner_down)
    mine[1] = jnp.where(upper, inner_up, up)
    theirs[0] = jnp.where(upper, inner_down, down)
    theirs[1] = jnp.where(upper, up, inner_up)


def join(place, keep, got, pair, far, news):
    _, _, half, size = keep.shape
    chips = len(news) + 1
    full = lambda a: pl.BlockSpec(a.shape, lambda i, place: (0,) * a.ndim)
    part = lambda n: pl.BlockSpec((n, half, size), lambda i, place: (0, place[0] % 2, 0))
    return pl.pallas_call(
        functools.partial(join_kernel, chips),
        grid_spec=pltpu.PrefetchScalarGridSpec(
            num_scalar_prefetch=1,
            grid=(1,),
            in_specs=[full(keep), full(got), part(4), part(chips - 1), *[full(a) for a in news]],
            out_specs=[full(keep)] * 2,
        ),
        out_shape=[jax.ShapeDtypeStruct(keep.shape, jnp.float32)] * 2,
        compiler_params=params,
        name="join",
    )(place, keep, got, pair, far, *news)


def inverse_kernel(per, thick, face, lam, out, m_all, f_all, g_all):
    total = f_all.shape[0]
    rows = lam.shape[0]
    classes = out.shape[0]
    shift = lam[...]
    one = jnp.ones_like(shift)
    zero = jnp.zeros_like(shift)

    def step(j, state):
        f, r, phi, s = state
        m = face[j] * r
        f = shift * thick[j] + m * f
        r = 1.0 / (face[j + 1] + f)
        m_all[j] = m
        f_all[j] = f
        i = total - 1 - j
        u = face[i + 1] * s * phi
        phi = shift * thick[i] + u
        s = 1.0 / (face[i] + phi)
        g_all[i] = u
        return f, r, phi, s

    lax.fori_loop(0, total, step, (one, one, zero, zero))

    def centre(j, _):
        g_all[j] = 1.0 / (f_all[j] + g_all[j])
        return 0

    lax.fori_loop(0, total, centre, 0)
    wide = out.shape[2]
    sub = lax.broadcasted_iota(jnp.int32, (ROWS, LANES), 0)
    lane = lax.broadcasted_iota(jnp.int32, (ROWS, wide), 1)
    row = lax.broadcasted_iota(jnp.int32, (ROWS, wide), 0)
    line = lambda ref, j, t: jnp.broadcast_to(ref[j, t:t + 1, :], (ROWS, LANES))

    def put(j, z, sums):
        new = []
        for c in range(classes):
            tiles = z[c * per:(c + 1) * per]
            total_tile = tiles[0]
            for tile in tiles[1:]:
                total_tile = total_tile + tile
            value = jnp.sum(total_tile, axis=1, keepdims=True)
            new.append(jnp.where(lane == j, value, sums[c]))
        return new

    for base in range(0, total, ROWS):
        z = [jnp.zeros((ROWS, LANES), jnp.float32)] * (classes * per)
        sums = [jnp.zeros((ROWS, wide), jnp.float32)] * classes
        for i in range(ROWS - 1, -1, -1):
            j = base + i
            for t in range(classes * per):
                moved = z[t] * line(m_all, j + 1, t) if i < ROWS - 1 else z[t]
                z[t] = jnp.where(sub == i, line(g_all, j, t), moved)
            sums = put(j, z, sums)

        def above(back, state):
            z, sums = state
            j = base - 1 - back
            z = [z[t] * line(m_all, j + 1, t) for t in range(classes * per)]
            return z, put(j, z, sums)

        if base:
            z, sums = lax.fori_loop(0, base, above, (z, sums))
        for c in range(classes):
            out[c, base:base + ROWS, :] = sums[c] * jnp.where(lane == base + row, 0.5, 1.0)


def inverse_sums(thick, face, lam, per):
    total = thick.shape[0]
    classes = lam.shape[0] // per
    wide = -(-total // LANES) * LANES
    spare = -lam.shape[0] % ROWS
    lam = jnp.pad(lam, ((0, spare), (0, 0)), constant_values=1.0)
    return pl.pallas_call(
        functools.partial(inverse_kernel, per),
        in_specs=[in_smem, in_smem, in_vmem],
        out_shape=jax.ShapeDtypeStruct((classes, total, wide), jnp.float32),
        scratch_shapes=[pltpu.VMEM((total,) + lam.shape, jnp.float32)] * 3,
        compiler_params=params,
        name="inverse_sums",
    )(thick, face, lam)


def interface_kernel(matrix, edges, inverse, out):
    total = edges.shape[1]
    rows = out.shape[0]
    mixed = exact_dot(matrix[...], edges[...], NN)
    result = jnp.zeros((rows, total), jnp.float32)
    for c in range(inverse.shape[0]):
        part = mixed[c * rows:(c + 1) * rows]
        square = inverse[c][:, :total]
        result = result + (exact_dot(part, square, NN) + exact_dot(part, square, NT))
    out[...] = result


def interface(edges, inverse, waves, count, size):
    return pl.pallas_call(
        interface_kernel,
        in_specs=[in_vmem] * 3,
        out_shape=jax.ShapeDtypeStruct((waves * 8, edges.shape[1]), jnp.float32),
        compiler_params=params,
        name="interface",
    )(interface_matrix(waves, count, size), edges, inverse)


def backward_kernel(total, place, thick, after, b, edges, spread, mine, theirs, top, rest, sines, t, r, m, end, out, ends, u_all, q_all):
    _, levels, ky, size = b.shape
    first = place[0] * levels
    half = ky // 2
    core = place[0] % 2
    many = size // LANES
    ends[:, pl.ds(pl.multiple_of(core * half, ROWS), half)] = mine[:, 0]
    ends[:, pl.ds(pl.multiple_of((1 - core) * half, ROWS), half)] = theirs[:, 0]
    near = sum(real_dot(part, spread[...]) for part in three_parts(edges[0]))
    for j in range(total):
        u_all[j] = near[:, j * LANES:(j + 1) * LANES]

    def source(j):
        return jnp.concatenate([u_all[j] * thick[j]] * many, 1)

    def from_above(j, y):
        return t[j] * y + source(j)

    def from_below(back, y):
        j = total - 1 - back
        return t[j + 1] * y + source(j)

    zero = jnp.zeros((ky, size), jnp.float32)
    ends[0] += sines[...][:1] * lax.fori_loop(0, first, from_above, zero)
    ends[1] += sines[...][:1] * lax.fori_loop(0, total - levels - first, from_below, zero)

    def tile(g, _):
        here = pl.ds(pl.multiple_of(g * ROWS, ROWS), ROWS)
        wave = sines[...]
        y = ends[0, here]
        ys = []
        for j in range(levels):
            own = jnp.concatenate([u_all[first + j, here] * thick[first + j]] * many, 1)
            y = b[0, j, here] + wave * own + m[j, here] * y
            ys.append(y)
        value = (y + end[0, here] * ends[1, here]) * end[1, here]
        q_all[levels - 1, here] = value
        for j in range(levels - 2, -1, -1):
            value = r[j, here] * ys[j] + m[j + 1, here] * value
            q_all[j, here] = value
        return 0

    lax.fori_loop(0, ky // ROWS, tile, 0)
    field = sine_transform(q_all[...].reshape(levels * ky, size), top[...], rest[...]).reshape(levels, ky, size)
    lane = lax.broadcasted_iota(jnp.int32, (ky, LANES), 1)
    for j in range(levels):
        u = u_all[first + j]
        here = 0.5 * (u + pltpu.roll(u, 1, 1))
        value = field[j] * ((2.0 / size) * after[j])
        out[0, j] = value
        out[0, j, :, :LANES] = jnp.where(lane == 0, here * after[j], value[:, :LANES])


def backward(place, thick, after, b, edges, mine, theirs, sines, t, r, m, end):
    _, levels, ky, size = b.shape
    total = t.shape[0] - 1
    top, rest = sine_matrix(size)
    half_spec = pl.BlockSpec((2, 1, ky // 2, size), lambda i: (0, i, 0, 0))
    field = pl.BlockSpec((1, levels, ky, size), lambda i: (i, 0, 0, 0))
    return pl.pallas_call(
        functools.partial(backward_kernel, total),
        grid=(2,),
        in_specs=[in_smem, in_smem, in_smem, field, pl.BlockSpec((1, ky, 2 * total), lambda i: (i, 0, 0)), in_vmem, half_spec, half_spec]
        + [in_vmem] * 7,
        out_specs=field,
        out_shape=jax.ShapeDtypeStruct(b.shape, jnp.float32),
        scratch_shapes=[
            pltpu.VMEM((2, ky, size), jnp.float32),
            pltpu.VMEM((total, ky, LANES), jnp.float32),
            pltpu.VMEM((levels, ky, size), jnp.float32),
        ],
        compiler_params=params,
        name="backward",
    )(place, thick, after, b, edges, spread_matrix(total), mine, theirs, top, rest, sines, t, r, m, end)


def shards(rhs, cotangent, thickness, ky_shift):
    waves = lax.axis_size("wave")
    count = lax.axis_size("depth")
    depth_pos = lax.axis_index("depth")
    wave_pos = lax.axis_index("wave")
    _, levels, ky, size = rhs.shape
    total = thickness.shape[0]
    full = waves * size
    devices = waves * count
    chips = count // 2
    everyone = ("depth", "wave")
    place = depth_pos.astype(jnp.int32).reshape(1)

    def across(a):
        return lax.ppermute(a, "depth", [(d, d ^ 1) for d in range(count)])

    def along(a, apart):
        return lax.ppermute(a, "depth", [(d, (d + 2 * apart) % count) for d in range(count)])

    def everywhere(a):
        return lax.all_to_all(a, everyone, split_axis=0, concat_axis=0, tiled=True)

    def horizontal(wavenumber, length):
        return aspect_ratio * 4.0 * jnp.sin(math.pi * jnp.asarray(wavenumber, jnp.float32) / length) ** 2

    inner_face = 2.0 / (thickness[:-1] + thickness[1:])
    face = jnp.concatenate([2.0 / thickness[:1], inner_face, jnp.zeros((1,), jnp.float32)])
    lam = ky_shift[:, None] + horizontal(np.arange(size), 2 * size)[None, :]
    t, r, m, end, pair, far = coefficients(place, thickness, face, lam, levels)
    thick_here = lax.dynamic_slice_in_dim(thickness, depth_pos * levels, levels)
    even = jnp.ones_like(thick_here)
    sines = jnp.asarray(np.broadcast_to(np.sin(np.pi * np.arange(size) / size)[None, :], (ROWS, size)), jnp.float32)
    heights = jnp.tile(thickness, ky).reshape(1, ky * total)

    share = -(-ky // devices)
    padded = share * devices - ky
    classes = waves // 2 + 1
    wavenumber = (np.arange(classes)[:, None] + waves * np.arange(size)[None, :]).reshape(-1, LANES)
    my_shifts = lax.dynamic_slice_in_dim(
        jnp.pad(ky_shift, (0, padded), constant_values=1.0), (depth_pos * waves + wave_pos) * share, share
    )
    across_k = horizontal(wavenumber, full)

    def start(field, before, ratio):
        b, keep, give, edges = forward(place, field, before, ratio, heights, sines, t, r, m, end)
        return b, keep, across(give), edges

    def middle(keep, got):
        sums = chip_sums(place, keep, got, pair, chips)
        news = [along(sums[apart - 1], apart) for apart in range(1, chips)]
        mine, theirs = join(place, keep, got, pair, far, news)
        return mine, across(theirs)

    b0, keep0, got0, edges0 = start(rhs, thick_here, even)
    b1, keep1, got1, edges1 = start(cotangent, even, 1.0 / thick_here)
    edges = jnp.concatenate([edges0, edges1]).reshape(4, 2, ky, total).transpose(2, 0, 1, 3)
    edges = jnp.pad(edges, ((0, padded), (0, 0), (0, 0), (0, 0)))
    edges = everywhere(edges.reshape(devices, share, 8, total))
    inverse = [inverse_sums(thickness, face, my_shifts[a] + across_k, size // LANES) for a in range(share)]
    mine0, theirs0 = middle(keep0, got0)
    mine1, theirs1 = middle(keep1, got1)
    values = [interface(edges[:, a].reshape(devices * 8, total), inverse[a], waves, count, size) for a in range(share)]
    values = jnp.stack(values, 0).reshape(1, share, waves, 8, total).transpose(0, 2, 1, 3, 4)
    values = jnp.broadcast_to(values, (count, waves, share, 8, total)).reshape(devices, share, 8, total)
    values = everywhere(values).reshape(devices * share, 2, 4, total)[:ky]
    values = values.transpose(2, 0, 1, 3).reshape(4, ky, 2 * total)
    tables = (sines, t, r, m, end)
    pressure = backward(place, thickness, even, b0, values[:2], mine0, theirs0, *tables)
    adjoint = backward(place, thickness, thick_here, b1, values[2:], mine1, theirs1, *tables)
    return pressure, adjoint


def solution(mesh):
    spec = P(None, "depth", None, "wave")
    return jax.shard_map(shards, mesh=mesh, in_specs=(spec, spec, P(), P()), out_specs=(spec, spec), check_vma=False)
```

```python
import functools
import math

import jax
import jax.numpy as jnp
import numpy as np
from jax import lax
from jax.experimental import pallas as pl
from jax.experimental.pallas import tpu as pltpu
from jax.sharding import PartitionSpec as P

aspect_ratio = 1.0
LANES = 128
ROWS = 8
VMEM_BYTES = 24 * 1024 * 1024
real_dot = functools.partial(jnp.dot, preferred_element_type=jnp.float32)
exact_dot = functools.partial(lax.dot_general, precision=lax.Precision.HIGHEST, preferred_element_type=jnp.float32)
NN = (((1,), (0,)), ((), ()))
NT = (((1,), (1,)), ((), ()))
in_smem = pl.BlockSpec(memory_space=pltpu.SMEM)
in_vmem = pl.BlockSpec(memory_space=pltpu.VMEM)
params = pltpu.CompilerParams(vmem_limit_bytes=VMEM_BYTES)


def wave_order(size):
    return np.concatenate([np.arange(1, size, 2), np.arange(0, size, 2)])


def half_sines(size, back=False):
    half = size // 2
    place = np.arange(half)
    place[0] = half
    parts = []
    for waves in (np.arange(1, size, 2), np.arange(0, size, 2)):
        matrix = np.sin(np.pi * (np.outer(place, waves) % (2 * size)) / size)
        if waves[0] == 0:
            matrix[0] = 0.0
            matrix[:, 0] = 0.0
        matrix = (matrix.T if back else matrix).astype(np.float32)
        top = matrix.astype(jnp.bfloat16)
        parts += [top, (matrix - top.astype(np.float32)).astype(jnp.bfloat16)]
    return parts


def edge_signs(size):
    signs = np.zeros((2 * ROWS, LANES), np.float32)
    signs[0] = 2.0 / size
    signs[1] = np.where(np.arange(LANES) < LANES // 2, 2.0 / size, -2.0 / size)
    return signs.astype(jnp.bfloat16)


def interface_matrices(waves, size):
    classes = waves // 2 + 1
    matrix = np.zeros((2, classes, 2, waves, 4, waves, 4))
    for c in range(classes):
        weight = (1.0 if c in (0, waves // 2) else 2.0) / (size * waves)
        for w in range(waves):
            for e in range(2):
                for v in range(waves):
                    for g in range(2):
                        value = weight * math.cos(2.0 * math.pi * (c * (w + e - v - g) % waves) / waves)
                        for f in range(4):
                            matrix[g, c, e, w, f, v, f] = value
    return matrix.reshape(2, classes * 2 * waves * 4, waves * 4).astype(np.float32)


def split(values):
    high = values.astype(jnp.bfloat16)
    return high, (values - high.astype(jnp.float32)).astype(jnp.bfloat16)


def product(values, top, rest):
    high, low = split(values)
    return real_dot(high, top[...]) + (real_dot(low, top[...]) + real_dot(high, rest[...]))


def mirror(values):
    rows = values.shape[0]
    lane = lax.broadcasted_iota(jnp.int32, (rows, LANES), 1)
    back = (LANES - lane) % LANES
    tiles = [values[:, a * LANES:(a + 1) * LANES] for a in range(values.shape[1] // LANES)]
    many = len(tiles)
    out = []
    for a in range(many):
        turned = jnp.take_along_axis(tiles[many - 1 - a], back, axis=1)
        out.append(jnp.where(lane == 0, tiles[(many - a) % many], turned))
    return jnp.concatenate(out, 1) if many > 1 else out[0]


def to_waves(values, odd_top, odd_rest, even_top, even_rest):
    half = values.shape[1] // 2
    low, high = values[:, :half], mirror(values[:, half:])
    lane = lax.broadcasted_iota(jnp.int32, low.shape, 1)
    low = jnp.where(lane == 0, 0.0, low)
    return product(low + high, odd_top, odd_rest), product(low - high, even_top, even_rest)


def to_cells(odd, even, odd_top, odd_rest, even_top, even_rest):
    p, m = product(odd, odd_top, odd_rest), product(even, even_top, even_rest)
    return p + m, mirror(p - m)


def coefficient_kernel(levels, total, group, place, thick, face, shifts, across, t_out, r_out, m_out, end_out, pair_out, far_out, lam, m_chip, r_chip, f_chip, n_chip, u_chip, down_all, up_all):
    ky = t_out.shape[1]
    span = 2 * levels
    chips = total // span
    chip = place[0] // 2
    start = chip * span
    upper = place[0] % 2 == 0
    own = (place[0] % 2) * levels
    for row in range(ky):
        lam[row:row + 1, :] = across[...] + shifts[row]

    def down_step(shift, j, f, r):
        m = face[j] * r
        f = shift * thick[j] + m * f
        return m, f, 1.0 / (face[j + 1] + f)

    def up_step(shift, j, phi, s):
        n = face[j + 1] * s
        u = n * phi
        phi = shift * thick[j] + u
        return n, u, phi, 1.0 / (face[j] + phi)

    def part(g, _):
        here = pl.ds(pl.multiple_of(g * group, group), group)
        shift = lam[here]
        one = jnp.ones_like(shift)
        zero = jnp.zeros_like(shift)

        def down_chip(c, state):
            f, r = state
            product = one
            for i in range(span):
                m, f, r = down_step(shift, c * span + i, f, r)
                t_out[c * span + i, here] = m
                product = product * m
            down_all[c] = product
            return f, r

        def up_chip(back, state):
            phi, s = state
            c = chips - 1 - back
            product = one
            for i in range(span - 1, -1, -1):
                n, _, phi, s = up_step(shift, c * span + i, phi, s)
                t_out[c * span + i + 1, here] = n
                product = product * n
            up_all[c] = product
            return phi, s

        f, r = lax.fori_loop(0, chip, down_chip, (one, one))
        for i in range(span):
            m, f, r = down_step(shift, start + i, f, r)
            m_chip[i], f_chip[i], r_chip[i] = m, f, r
        phi, s = lax.fori_loop(0, chips - 1 - chip, up_chip, (zero, zero))
        for i in range(span - 1, -1, -1):
            n, u, phi, s = up_step(shift, start + i, phi, s)
            n_chip[i], u_chip[i] = n, u

        for i in range(levels):
            t_out[start + i, here] = m_chip[i]
            t_out[start + levels + 1 + i, here] = n_chip[levels + i]
        t_out[start + levels, here] = jnp.where(upper, n_chip[levels - 1], m_chip[levels])
        for i in range(levels):
            r_out[i, here] = r_chip[own + i]
            m_out[i, here] = m_chip[own + i]
        last = own + levels - 1
        end_out[0, here] = n_chip[last]
        end_out[1, here] = 1.0 / (f_chip[last] + u_chip[last])
        end_out[2, here] = f_chip[own] + u_chip[own]
        for core in range(2):
            down, up = m_chip[core * levels], n_chip[core * levels]
            for i in range(1, levels):
                down = down * m_chip[core * levels + i]
                up = up * n_chip[core * levels + i]
            pair_out[core, here] = down
            pair_out[2 + core, here] = up
        above, below = [one], [one]
        for apart in range(1, chips - 1):
            above.append(above[-1] * jnp.where(chip >= apart, down_all[jnp.maximum(chip - apart, 0)], one))
            below.append(below[-1] * jnp.where(chip + apart < chips, up_all[jnp.minimum(chip + apart, chips - 1)], one))
        for apart in range(1, chips):
            far_out[apart - 1, here] = jnp.where(chip >= apart, above[apart - 1], below[chips - apart - 1])
        return 0

    lax.fori_loop(0, ky // group, part, 0)


def coefficients(place, thick, face, shifts, across, levels):
    ky, size = shifts.shape[0], across.shape[1]
    total = thick.shape[0]
    chips = total // (2 * levels)
    group = min(2 * ROWS, ky)
    sizes = (total + 1, levels, levels, 3, 4, chips - 1)
    scratch = lambda n: pltpu.VMEM((n, group, size), jnp.float32)
    return pl.pallas_call(
        functools.partial(coefficient_kernel, levels, total, group),
        in_specs=[in_smem] * 4 + [in_vmem],
        out_specs=[in_vmem] * 6,
        out_shape=[jax.ShapeDtypeStruct((n, ky, size), jnp.float32) for n in sizes],
        scratch_shapes=[pltpu.VMEM((ky, size), jnp.float32)] + [scratch(2 * levels)] * 5 + [scratch(chips)] * 2,
        compiler_params=params,
        name="coefficients",
    )(place, thick, face, shifts, across)


def lane_sum(values):
    tiles = [values[:, t * LANES:(t + 1) * LANES] for t in range(values.shape[1] // LANES)]
    while len(tiles) > 1:
        tiles = [a + b for a, b in zip(tiles[0::2], tiles[1::2])] + tiles[len(tiles) // 2 * 2:]
    return tiles[0]


def two_sums(values):
    half = values.shape[1] // 2
    odd, even = lane_sum(values[:, :half]), lane_sum(values[:, half:])
    odd = odd + pltpu.roll(odd, LANES // 2, 1)
    even = even + pltpu.roll(even, LANES // 2, 1)
    return jnp.where(lax.broadcasted_iota(jnp.int32, odd.shape, 1) < LANES // 2, odd, even)


def forward_kernel(total, scaled, part, place, thick, x, odd_top, odd_rest, even_top, even_rest, sines, signs, t, r, m, end, *refs):
    b_out, keep_out, give_out, edge_out, c_all, z_all, sums = refs[-7:]
    _, levels, ky, size = x.shape
    first = place[0] * levels
    half = size // 2
    lane = lax.broadcasted_iota(jnp.int32, (ROWS, LANES), 1)
    spot = jnp.where((lane == 0) | (lane == LANES // 2), size / 4.0, 0.0)
    edge_out[...] = refs[0][...] if part else jnp.zeros_like(edge_out)
    odd, even = to_waves(x[...].reshape(2 * levels * ky, size), odd_top, odd_rest, even_top, even_rest)
    for ri in range(2):
        for j in range(levels):
            rows = slice((ri * levels + j) * ky, (ri * levels + j + 1) * ky)
            scale = thick[first + j] if scaled else 1.0
            b_out[ri, j, :, :half] = odd[rows] * scale
            b_out[ri, j, :, half:] = even[rows] * scale

    for ri in range(2):
        def tile(g, _):
            here = pl.ds(pl.multiple_of(g * ROWS, ROWS), ROWS)
            wave = sines[...]
            y = b_out[ri, 0, here]
            ys = [y]
            for j in range(1, levels):
                y = b_out[ri, j, here] + m[j, here] * y
                ys.append(y)
            c_all[0, here] = y
            value = y * end[1, here]
            z_all[1, here] = value * wave
            for j in range(levels - 1, -1, -1):
                if j < levels - 1:
                    value = r[j, here] * ys[j] + m[j + 1, here] * value
                height = thick[first + j]
                own = jnp.broadcast_to(x[ri, j, here, 0:1], (ROWS, LANES)) * (spot * height if scaled else spot)
                sums[pl.ds(g * ROWS * total + first + j, ROWS, stride=total), :] = two_sums(value * wave) * height + own
            z_all[0, here] = value * wave
            c_all[1, here] = value * end[2, here]
            return 0

        lax.fori_loop(0, ky // ROWS, tile, 0)

        def reach_up(back, z):
            j = first - 1 - back
            z = t[j + 1] * z
            sums[pl.ds(j, ky, stride=total), :] = two_sums(z) * thick[j]
            return z

        def reach_down(ahead, z):
            j = first + levels + ahead
            z = t[j] * z
            sums[pl.ds(j, ky, stride=total), :] = two_sums(z) * thick[j]
            return z

        lax.fori_loop(0, first, reach_up, z_all[0])
        lax.fori_loop(0, total - levels - first, reach_down, z_all[1])
        high, low = split(sums[...])
        edges = lax.dot_general(signs[...], high, NT, preferred_element_type=jnp.float32)
        edges = edges + lax.dot_general(signs[...], low, NT, preferred_element_type=jnp.float32)
        row = part * 2 + ri
        for i in range(ky):
            edge_out[i, row:row + 1, :total] = edges[0:1, i * total:(i + 1) * total]
            edge_out[i, row:row + 1, total:] = edges[1:2, i * total:(i + 1) * total]
        core = place[0] % 2
        keep_out[:, ri] = c_all[:, pl.ds(pl.multiple_of(core * (ky // 2), ROWS), ky // 2)]
        give_out[:, ri] = c_all[:, pl.ds(pl.multiple_of((1 - core) * (ky // 2), ROWS), ky // 2)]


def forward(place, thick, x, scaled, sines, t, r, m, end, devices, edges=None):
    _, levels, ky, size = x.shape
    total = t.shape[0] - 1
    part = 0 if edges is None else 1
    half = (2, 2, ky // 2, size)
    old = [] if edges is None else [edges]
    return pl.pallas_call(
        functools.partial(forward_kernel, total, scaled, part),
        in_specs=[in_smem, in_smem] + [in_vmem] * (11 + part),
        out_specs=[in_vmem] * 4,
        out_shape=[
            jax.ShapeDtypeStruct(x.shape, jnp.float32),
            jax.ShapeDtypeStruct(half, jnp.float32),
            jax.ShapeDtypeStruct(half, jnp.float32),
            jax.ShapeDtypeStruct((devices, 4, 2 * total), jnp.float32),
        ],
        scratch_shapes=[
            pltpu.VMEM((2, ky, size), jnp.float32),
            pltpu.VMEM((2, ky, size), jnp.float32),
            pltpu.VMEM((ky * total, LANES), jnp.float32),
        ],
        compiler_params=params,
        name="forward",
    )(place, thick, x, *half_sines(size), sines, edge_signs(size), t, r, m, end, *old)


def chip_kernel(chips, place, keep, got, pair, *outs):
    chip = place[0] // 2
    upper = place[0] % 2 == 0
    half = keep.shape[2]
    here = pl.ds(pl.multiple_of((place[0] % 2) * half, ROWS), half)
    first, second = jnp.where(upper, keep[...], got[...]), jnp.where(upper, got[...], keep[...])
    down = second[0] + pair[1, here] * first[0]
    up = first[1] + pair[2, here] * second[1]
    for apart in range(1, chips):
        outs[apart - 1][...] = jnp.where(chip + apart < chips, down, up)


def chip_sums(place, keep, got, pair, chips):
    return pl.pallas_call(
        functools.partial(chip_kernel, chips),
        in_specs=[in_smem] + [in_vmem] * 3,
        out_specs=[in_vmem] * (chips - 1),
        out_shape=[jax.ShapeDtypeStruct(keep.shape[1:], jnp.float32)] * (chips - 1),
        compiler_params=params,
        name="chip_sums",
    )(place, keep, got, pair)


def join_kernel(chips, place, keep, got, pair, far, *refs):
    news = refs[:chips - 1]
    mine, theirs = refs[chips - 1:]
    chip = place[0] // 2
    upper = place[0] % 2 == 0
    half = keep.shape[2]
    here = pl.ds(pl.multiple_of((place[0] % 2) * half, ROWS), half)
    first, second = jnp.where(upper, keep[...], got[...]), jnp.where(upper, got[...], keep[...])
    down = jnp.zeros(first.shape[1:], jnp.float32)
    up = down
    for apart in range(1, chips):
        term = far[apart - 1, here] * news[apart - 1][...]
        down = down + jnp.where(chip >= apart, term, 0.0)
        up = up + jnp.where(chip >= apart, 0.0, term)
    inner_up = second[1] + pair[3, here] * up
    inner_down = first[0] + pair[0, here] * down
    mine[0] = jnp.where(upper, down, inner_down)
    mine[1] = jnp.where(upper, inner_up, up)
    theirs[0] = jnp.where(upper, inner_down, down)
    theirs[1] = jnp.where(upper, up, inner_up)


def join(place, keep, got, pair, far, news):
    chips = len(news) + 1
    return pl.pallas_call(
        functools.partial(join_kernel, chips),
        in_specs=[in_smem] + [in_vmem] * (3 + chips),
        out_specs=[in_vmem] * 2,
        out_shape=[jax.ShapeDtypeStruct(keep.shape, jnp.float32)] * 2,
        compiler_params=params,
        name="join",
    )(place, keep, got, pair, far, *news)


def inverse_kernel(per, thick, face, lam, out, m_all, f_all, g_all):
    total = f_all.shape[0]
    rows = lam.shape[0]
    classes = out.shape[0]
    shift = lam[...]
    one = jnp.ones_like(shift)
    zero = jnp.zeros_like(shift)

    def step(j, state):
        f, r, phi, s = state
        m = face[j] * r
        f = shift * thick[j] + m * f
        r = 1.0 / (face[j + 1] + f)
        m_all[j] = m
        f_all[j] = f
        i = total - 1 - j
        u = face[i + 1] * s * phi
        phi = shift * thick[i] + u
        s = 1.0 / (face[i] + phi)
        g_all[i] = u
        return f, r, phi, s

    lax.fori_loop(0, total, step, (one, one, zero, zero))

    def centre(j, _):
        g_all[j] = 1.0 / (f_all[j] + g_all[j])
        return 0

    lax.fori_loop(0, total, centre, 0)
    wide = out.shape[2]
    sub = lax.broadcasted_iota(jnp.int32, (ROWS, LANES), 0)
    lane = lax.broadcasted_iota(jnp.int32, (ROWS, wide), 1)
    row = lax.broadcasted_iota(jnp.int32, (ROWS, wide), 0)
    line = lambda ref, j, t: jnp.broadcast_to(ref[j, t:t + 1, :], (ROWS, LANES))

    def put(j, z, sums):
        new = []
        for c in range(classes):
            tiles = z[c * per:(c + 1) * per]
            total_tile = tiles[0]
            for tile in tiles[1:]:
                total_tile = total_tile + tile
            value = jnp.sum(total_tile, axis=1, keepdims=True)
            new.append(jnp.where(lane == j, value, sums[c]))
        return new

    for base in range(0, total, ROWS):
        z = [jnp.zeros((ROWS, LANES), jnp.float32)] * (classes * per)
        sums = [jnp.zeros((ROWS, wide), jnp.float32)] * classes
        for i in range(ROWS - 1, -1, -1):
            j = base + i
            for t in range(classes * per):
                moved = z[t] * line(m_all, j + 1, t) if i < ROWS - 1 else z[t]
                z[t] = jnp.where(sub == i, line(g_all, j, t), moved)
            sums = put(j, z, sums)

        def above(back, state):
            z, sums = state
            for i in range(ROWS):
                j = base - 1 - back * ROWS - i
                z = [z[t] * line(m_all, j + 1, t) for t in range(classes * per)]
                sums = put(j, z, sums)
            return z, sums

        if base:
            z, sums = lax.fori_loop(0, base // ROWS, above, (z, sums))
        for c in range(classes):
            out[c, base:base + ROWS, :] = sums[c] * jnp.where(lane == base + row, 0.5, 1.0)


def inverse_sums(thick, face, lam, per):
    total = thick.shape[0]
    classes = lam.shape[0] // per
    wide = -(-total // LANES) * LANES
    spare = -lam.shape[0] % ROWS
    lam = jnp.pad(lam, ((0, spare), (0, 0)), constant_values=1.0) if spare else lam
    return pl.pallas_call(
        functools.partial(inverse_kernel, per),
        in_specs=[in_smem, in_smem, in_vmem],
        out_shape=jax.ShapeDtypeStruct((classes, total, wide), jnp.float32),
        scratch_shapes=[pltpu.VMEM((total,) + lam.shape, jnp.float32)] * 3,
        compiler_params=params,
        name="inverse_sums",
    )(thick, face, lam)


def interface_kernel(waves, matrices, edges, inverse, out):
    devices, _, wide = edges.shape
    total = wide // 2
    rows = 4 * waves
    lines = []
    for w in range(waves):
        line = edges[w]
        for d in range(1, devices // waves):
            line = line + edges[d * waves + w]
        lines.append(line)
    lines = jnp.concatenate(lines, 0)
    near, far = exact_dot(matrices[0], lines, NN), exact_dot(matrices[1], lines, NN)
    mixed = near[:, :total] + far[:, total:]
    result = jnp.zeros((2 * rows, total), jnp.float32)
    for c in range(inverse.shape[0]):
        part = mixed[c * 2 * rows:(c + 1) * 2 * rows]
        square = inverse[c][:, :total]
        result = result + (exact_dot(part, square, NN) + exact_dot(part, square, NT))
    result = jnp.concatenate([result[:rows], result[rows:]], 1)
    for w in range(waves):
        line = result[4 * w:4 * w + 4]
        for d in range(devices // waves):
            out[d * waves + w] = line


def interface(edges, inverse, waves, size):
    return pl.pallas_call(
        functools.partial(interface_kernel, waves),
        in_specs=[in_vmem] * 3,
        out_specs=in_vmem,
        out_shape=jax.ShapeDtypeStruct(edges.shape, jnp.float32),
        compiler_params=params,
        name="interface",
    )(interface_matrices(waves, size), edges, inverse)


def backward_kernel(total, scaled, part, place, thick, b, edges, mine, theirs, odd_top, odd_rest, even_top, even_rest, sines, t, r, m, end, out, ends, u_all, q_all):
    ri = pl.program_id(0)
    _, levels, ky, size = b.shape
    first = place[0] * levels
    half = size // 2
    many = half // LANES
    core = place[0] % 2
    ends[:, pl.ds(pl.multiple_of(core * (ky // 2), ROWS), ky // 2)] = mine[:, ri]
    ends[:, pl.ds(pl.multiple_of((1 - core) * (ky // 2), ROWS), ky // 2)] = theirs[:, ri]
    values = jnp.where(ri == 0, edges[:ky, 2 * part, :], edges[:ky, 2 * part + 1, :])
    near, far = values[:, :total], values[:, total:]
    plus, minus = near + far, near - far
    for j in range(total):
        u_all[0, j] = jnp.broadcast_to(plus[:, j:j + 1], (ky, LANES))
        u_all[1, j] = jnp.broadcast_to(minus[:, j:j + 1], (ky, LANES))

    def source(j, here=slice(None)):
        return jnp.concatenate([u_all[0, j, here] * thick[j]] * many + [u_all[1, j, here] * thick[j]] * many, 1)

    def from_above(j, y):
        return t[j] * y + source(j)

    def from_below(back, y):
        j = total - 1 - back
        return t[j + 1] * y + source(j)

    zero = jnp.zeros((ky, size), jnp.float32)
    ends[0] += sines[...][:1] * lax.fori_loop(0, first, from_above, zero)
    ends[1] += sines[...][:1] * lax.fori_loop(0, total - levels - first, from_below, zero)

    def tile(g, _):
        here = pl.ds(pl.multiple_of(g * ROWS, ROWS), ROWS)
        wave = sines[...]
        y = ends[0, here]
        ys = []
        for j in range(levels):
            y = b[ri, j, here] + wave * source(first + j, here) + m[j, here] * y
            ys.append(y)
        value = (y + end[0, here] * ends[1, here]) * end[1, here]
        q_all[levels - 1, here] = value
        for j in range(levels - 2, -1, -1):
            value = r[j, here] * ys[j] + m[j + 1, here] * value
            q_all[j, here] = value
        return 0

    lax.fori_loop(0, ky // ROWS, tile, 0)
    rows = levels * ky
    low, high = to_cells(
        q_all[:, :, :half].reshape(rows, half), q_all[:, :, half:].reshape(rows, half), odd_top, odd_rest, even_top, even_rest
    )
    lane = lax.broadcasted_iota(jnp.int32, (ky, LANES), 1)
    for j in range(levels):
        height = thick[first + j] if scaled else 1.0
        scale = (2.0 / size) * height
        here = slice(j * ky, (j + 1) * ky)
        u = (u_all[0, first + j] + u_all[1, first + j]) * (0.5 * height)
        if many > 1:
            out[0, j, :, LANES:half] = low[here, LANES:] * scale
        out[0, j, :, :LANES] = jnp.where(lane == 0, u, low[here, :LANES] * scale)
        out[0, j, :, half:] = high[here] * scale


def backward(place, thick, b, edges, mine, theirs, scaled, part, sines, t, r, m, end):
    _, levels, ky, size = b.shape
    total = t.shape[0] - 1
    return pl.pallas_call(
        functools.partial(backward_kernel, total, scaled, part),
        grid=(2,),
        in_specs=[in_smem, in_smem] + [in_vmem] * 13,
        out_specs=pl.BlockSpec((1, levels, ky, size), lambda i: (i, 0, 0, 0)),
        out_shape=jax.ShapeDtypeStruct(b.shape, jnp.float32),
        scratch_shapes=[
            pltpu.VMEM((2, ky, size), jnp.float32),
            pltpu.VMEM((2, total, ky, LANES), jnp.float32),
            pltpu.VMEM((levels, ky, size), jnp.float32),
        ],
        compiler_params=params,
        name="backward",
    )(place, thick, b, edges, mine, theirs, *half_sines(size, True), sines, t, r, m, end)


def shards(rhs, cotangent, thickness, ky_shift):
    waves = lax.axis_size("wave")
    count = lax.axis_size("depth")
    depth_pos = lax.axis_index("depth")
    wave_pos = lax.axis_index("wave")
    _, levels, ky, size = rhs.shape
    full = waves * size
    devices = waves * count
    chips = count // 2
    place = depth_pos.astype(jnp.int32).reshape(1)

    def across(a):
        return lax.ppermute(a, "depth", [(d, d ^ 1) for d in range(count)])

    def along(a, apart):
        return lax.ppermute(a, "depth", [(d, (d + 2 * apart) % count) for d in range(count)])

    def everywhere(a):
        return lax.all_to_all(a, ("depth", "wave"), split_axis=0, concat_axis=0, tiled=True)

    def horizontal(wavenumber, length):
        return (aspect_ratio * 4.0 * np.sin(math.pi * wavenumber / length) ** 2).astype(np.float32)

    inner_face = 2.0 / (thickness[:-1] + thickness[1:])
    face = jnp.concatenate([2.0 / thickness[:1], inner_face, jnp.zeros((1,), jnp.float32)])
    order = wave_order(size)
    t, r, m, end, pair, far = coefficients(place, thickness, face, ky_shift, horizontal(order, 2 * size)[None, :], levels)
    sines = jnp.asarray(np.broadcast_to(np.sin(np.pi * order / size)[None, :], (ROWS, size)), jnp.float32)
    tables = (sines, t, r, m, end)

    classes = waves // 2 + 1
    wavenumber = (np.arange(classes)[:, None] + waves * np.arange(size)[None, :]).reshape(-1, LANES)
    shifts = jnp.pad(ky_shift, (0, devices - ky), constant_values=1.0) if devices > ky else ky_shift
    my_shift = lax.dynamic_slice_in_dim(shifts, depth_pos * waves + wave_pos, 1)

    def middle(keep, give):
        got = across(give)
        sums = chip_sums(place, keep, got, pair, chips)
        news = [along(sums[apart - 1], apart) for apart in range(1, chips)]
        mine, theirs = join(place, keep, got, pair, far, news)
        return mine, across(theirs)

    b0, keep0, give0, edges = forward(place, thickness, rhs, True, *tables, devices)
    b1, keep1, give1, edges = forward(place, thickness, cotangent, False, *tables, devices, edges)
    edges = everywhere(edges)
    inverse = inverse_sums(thickness, face, my_shift + horizontal(wavenumber, full), size // LANES)
    mine0, theirs0 = middle(keep0, give0)
    mine1, theirs1 = middle(keep1, give1)
    values = everywhere(interface(edges, inverse, waves, size))
    pressure = backward(place, thickness, b0, values, mine0, theirs0, False, 0, *tables)
    adjoint = backward(place, thickness, b1, values, mine1, theirs1, True, 1, *tables)
    return pressure, adjoint


def solution(mesh):
    spec = P(None, "depth", None, "wave")
    return jax.shard_map(shards, mesh=mesh, in_specs=(spec, spec, P(), P()), out_specs=(spec, spec), check_vma=False)
```

```python
import functools
import math

import jax
import jax.numpy as jnp
import numpy as np
from jax import lax
from jax.experimental import pallas as pl
from jax.experimental.pallas import tpu as pltpu
from jax.sharding import PartitionSpec as P

aspect_ratio = 1.0
LANES = 128
ROWS = 8
VMEM_BYTES = 60 * 1024 * 1024
real_dot = functools.partial(jnp.dot, preferred_element_type=jnp.float32)
exact_dot = functools.partial(lax.dot_general, precision=lax.Precision.HIGHEST, preferred_element_type=jnp.float32)
NN = (((1,), (0,)), ((), ()))
NT = (((1,), (1,)), ((), ()))
in_smem = pl.BlockSpec(memory_space=pltpu.SMEM)
in_hbm = pl.BlockSpec(memory_space=pl.ANY)
in_vmem = pl.BlockSpec(memory_space=pltpu.VMEM)
params = pltpu.CompilerParams(vmem_limit_bytes=VMEM_BYTES)


def wave_order(size):
    return np.concatenate([np.arange(1, size, 2), np.arange(0, size, 2)])


def half_sines(size, back=False):
    half = size // 2
    place = np.arange(half)
    place[0] = half
    parts = []
    for waves in (np.arange(1, size, 2), np.arange(0, size, 2)):
        matrix = np.sin(np.pi * (np.outer(place, waves) % (2 * size)) / size)
        if waves[0] == 0:
            matrix[0] = 0.0
            matrix[:, 0] = 0.0
        matrix = (matrix.T if back else matrix).astype(np.float32)
        top = matrix.astype(jnp.bfloat16)
        parts += [top, (matrix - top.astype(np.float32)).astype(jnp.bfloat16)]
    return parts


def edge_matrix(size, total):
    matrix = np.full((2 * LANES, 2 * total), 2.0 / size, np.float32)
    matrix[LANES:, total:] = -2.0 / size
    return matrix.astype(jnp.bfloat16)


def spread_matrix(total):
    matrix = np.ones((2 * total, 2 * LANES), np.float32)
    matrix[total:, LANES:] = -1.0
    return matrix.astype(jnp.bfloat16)


def interface_matrices(waves, size):
    classes = waves // 2 + 1
    matrix = np.zeros((2, classes, 2, waves, 4, waves, 4))
    for c in range(classes):
        weight = (1.0 if c in (0, waves // 2) else 2.0) / (size * waves)
        for w in range(waves):
            for e in range(2):
                for v in range(waves):
                    for g in range(2):
                        value = weight * math.cos(2.0 * math.pi * (c * (w + e - v - g) % waves) / waves)
                        for f in range(4):
                            matrix[g, c, e, w, f, v, f] = value
    return matrix.reshape(2, classes * 2 * waves * 4, waves * 4).astype(np.float32)


def split(values):
    high = values.astype(jnp.bfloat16)
    return high, (values - high.astype(jnp.float32)).astype(jnp.bfloat16)


def product(values, top, rest):
    high, low = split(values)
    return real_dot(high, top[...]) + (real_dot(low, top[...]) + real_dot(high, rest[...]))


def mirror(values):
    rows = values.shape[0]
    lane = lax.broadcasted_iota(jnp.int32, (rows, LANES), 1)
    back = (LANES - lane) % LANES
    tiles = [values[:, a * LANES:(a + 1) * LANES] for a in range(values.shape[1] // LANES)]
    many = len(tiles)
    out = []
    for a in range(many):
        turned = jnp.take_along_axis(tiles[many - 1 - a], back, axis=1)
        out.append(jnp.where(lane == 0, tiles[(many - a) % many], turned))
    return jnp.concatenate(out, 1) if many > 1 else out[0]


def to_waves(values, odd_top, odd_rest, even_top, even_rest):
    half = values.shape[1] // 2
    low, high = values[:, :half], mirror(values[:, half:])
    lane = lax.broadcasted_iota(jnp.int32, low.shape, 1)
    low = jnp.where(lane == 0, 0.0, low)
    return product(low + high, odd_top, odd_rest), product(low - high, even_top, even_rest)


def to_cells(odd, even, odd_top, odd_rest, even_top, even_rest):
    p, m = product(odd, odd_top, odd_rest), product(even, even_top, even_rest)
    return p + m, mirror(p - m)


class Copies:
    def __init__(self, sems):
        self.sems, self.used = sems, 0

    def start(self, source, target):
        copy = pltpu.make_async_copy(source, target, self.sems.at[self.used])
        self.used += 1
        copy.start()
        return copy


def coefficients(levels, total, group, place, thick, face, shifts, across, t_out, r_out, m_out, end_out, pair_out, far_out, lam, m_chip, r_chip, f_chip, n_chip, u_chip, down_all, up_all):
    ky = lam.shape[0]
    span = 2 * levels
    chips = total // span
    chip = place[0] // 2
    start = chip * span
    upper = place[0] % 2 == 0
    own = (place[0] % 2) * levels
    for row in range(ky):
        lam[row:row + 1, :] = across[...] + shifts[row]

    def down_step(shift, j, f, r):
        m = face[j] * r
        f = shift * thick[j] + m * f
        return m, f, 1.0 / (face[j + 1] + f)

    def up_step(shift, j, phi, s):
        n = face[j + 1] * s
        u = n * phi
        phi = shift * thick[j] + u
        return n, u, phi, 1.0 / (face[j] + phi)

    def part(g, _):
        here = pl.ds(pl.multiple_of(g * group, group), group)
        shift = lam[here]
        one = jnp.ones_like(shift)
        zero = jnp.zeros_like(shift)

        def down_chip(c, state):
            f, r = state
            product = one
            for i in range(span):
                m, f, r = down_step(shift, c * span + i, f, r)
                t_out[c * span + i, here] = m
                product = product * m
            down_all[c] = product
            return f, r

        def up_chip(back, state):
            phi, s = state
            c = chips - 1 - back
            product = one
            for i in range(span - 1, -1, -1):
                n, _, phi, s = up_step(shift, c * span + i, phi, s)
                t_out[c * span + i + 1, here] = n
                product = product * n
            up_all[c] = product
            return phi, s

        f, r = lax.fori_loop(0, chip, down_chip, (one, one))
        for i in range(span):
            m, f, r = down_step(shift, start + i, f, r)
            m_chip[i], f_chip[i], r_chip[i] = m, f, r
        phi, s = lax.fori_loop(0, chips - 1 - chip, up_chip, (zero, zero))
        for i in range(span - 1, -1, -1):
            n, u, phi, s = up_step(shift, start + i, phi, s)
            n_chip[i], u_chip[i] = n, u

        for i in range(levels):
            t_out[start + i, here] = m_chip[i]
            t_out[start + levels + 1 + i, here] = n_chip[levels + i]
        t_out[start + levels, here] = jnp.where(upper, n_chip[levels - 1], m_chip[levels])
        for i in range(levels):
            r_out[i, here] = r_chip[own + i]
            m_out[i, here] = m_chip[own + i]
        last = own + levels - 1
        end_out[0, here] = n_chip[last]
        end_out[1, here] = 1.0 / (f_chip[last] + u_chip[last])
        end_out[2, here] = f_chip[own] + u_chip[own]
        for core in range(2):
            down, up = m_chip[core * levels], n_chip[core * levels]
            for i in range(1, levels):
                down = down * m_chip[core * levels + i]
                up = up * n_chip[core * levels + i]
            pair_out[core, here] = down
            pair_out[2 + core, here] = up
        above, below = [one], [one]
        for apart in range(1, chips - 1):
            above.append(above[-1] * jnp.where(chip >= apart, down_all[jnp.maximum(chip - apart, 0)], one))
            below.append(below[-1] * jnp.where(chip + apart < chips, up_all[jnp.minimum(chip + apart, chips - 1)], one))
        for apart in range(1, chips):
            far_out[apart - 1, here] = jnp.where(chip >= apart, above[apart - 1], below[chips - apart - 1])
        return 0

    lax.fori_loop(0, ky // group, part, 0)


def lane_sum(values):
    tiles = [values[:, t * LANES:(t + 1) * LANES] for t in range(values.shape[1] // LANES)]
    while len(tiles) > 1:
        tiles = [a + b for a, b in zip(tiles[0::2], tiles[1::2])] + tiles[len(tiles) // 2 * 2:]
    return tiles[0]


def front_kernel(levels, total, group, place, thick, face, shifts, across, sines, edge_mix, x0, x1, odd_top, odd_rest, even_top, even_rest, t_out, r_out, m_out, end_out, pair_out, far_out, b_out, keep_out, give_out, edge_out, sems, *scratch):
    across_v, sines_v, mix_v, x, ot, orest, et, er, t, r, m, end, pair, far, b, c_all, z_all, sums, edges, lam, *work = scratch
    _, _, _, ky, size = x.shape
    first = place[0] * levels
    half = size // 2
    copies = Copies(sems)
    early = [copies.start(across, across_v)]
    fields = [copies.start(x0, x.at[0])]
    mats = [copies.start(source, target) for source, target in ((odd_top, ot), (odd_rest, orest), (even_top, et), (even_rest, er))]
    mats += [copies.start(sines, sines_v)]
    fields += [copies.start(x1, x.at[1])]
    late = [copies.start(edge_mix, mix_v)]
    for copy in early:
        copy.wait()
    coefficients(levels, total, group, place, thick, face, shifts, across_v, t, r, m, end, pair, far, lam, *work)
    outs = [copies.start(source, target) for source, target in ((pair, pair_out), (far, far_out))]
    outs += [copies.start(source, target) for source, target in ((t, t_out), (r, r_out), (m, m_out), (end, end_out))]
    for copy in mats:
        copy.wait()
    lane = lax.broadcasted_iota(jnp.int32, (ROWS, LANES), 1)
    spot = jnp.where(lane == 0, size / 4.0, 0.0)
    core = place[0] % 2

    def put(f, rows, values, height, own=None):
        odd, even = lane_sum(values[:, :half]) * height, lane_sum(values[:, half:]) * height
        if own is not None:
            odd, even = odd + own, even + own
        sums[f, 0, rows, :] = odd
        sums[f, 1, rows, :] = even

    for a in range(2):
        fields[a].wait()
        odd, even = to_waves(x[a].reshape(2 * levels * ky, size), ot, orest, et, er)
        for ri in range(2):
            for j in range(levels):
                rows = slice((ri * levels + j) * ky, (ri * levels + j + 1) * ky)
                scale = thick[first + j] if a == 0 else 1.0
                b[a, ri, j, :, :half] = odd[rows] * scale
                b[a, ri, j, :, half:] = even[rows] * scale
        outs.append(copies.start(b.at[a], b_out.at[a]))
        for ri in range(2):
            f = 2 * a + ri

            def tile(g, _):
                here = pl.ds(pl.multiple_of(g * ROWS, ROWS), ROWS)
                wave = sines_v[...]
                y = b[a, ri, 0, here]
                ys = [y]
                for j in range(1, levels):
                    y = b[a, ri, j, here] + m[j, here] * y
                    ys.append(y)
                c_all[a, 0, ri, here] = y
                value = y * end[1, here]
                z_all[1, f, here] = value * wave
                for j in range(levels - 1, -1, -1):
                    if j < levels - 1:
                        value = r[j, here] * ys[j] + m[j + 1, here] * value
                    height = thick[first + j]
                    own = jnp.broadcast_to(x[a, ri, j, here, 0:1], (ROWS, LANES)) * (spot * height if a == 0 else spot)
                    put(f, pl.ds(g * ROWS * total + first + j, ROWS, stride=total), value * wave, height, own)
                z_all[0, f, here] = value * wave
                c_all[a, 1, ri, here] = value * end[2, here]
                return 0

            lax.fori_loop(0, ky // ROWS, tile, 0)
        for start, out in ((core, keep_out), (1 - core, give_out)):
            here = pl.ds(pl.multiple_of(start * (ky // 2), ROWS), ky // 2)
            outs.append(copies.start(c_all.at[a, :, :, here], out.at[a]))

    def reach(g, _):
        here = pl.ds(pl.multiple_of(g * ROWS, ROWS), ROWS)

        def up(block, z):
            for i in range(levels):
                j = first - 1 - block * levels - i
                step = t[j + 1, here]
                z = [step * one for one in z]
                for f in range(4):
                    put(f, pl.ds(g * ROWS * total + j, ROWS, stride=total), z[f], thick[j])
            return z

        def down(block, z):
            for i in range(levels):
                j = first + levels + block * levels + i
                step = t[j, here]
                z = [step * one for one in z]
                for f in range(4):
                    put(f, pl.ds(g * ROWS * total + j, ROWS, stride=total), z[f], thick[j])
            return z

        lax.fori_loop(0, place[0], up, [z_all[0, f, here] for f in range(4)])
        lax.fori_loop(0, total // levels - 1 - place[0], down, [z_all[1, f, here] for f in range(4)])
        return 0

    lax.fori_loop(0, ky // ROWS, reach, 0)
    for copy in late:
        copy.wait()
    if edges.shape[0] > ky:
        edges[...] = jnp.zeros_like(edges)
    wide = 2 * total
    row = lax.broadcasted_iota(jnp.int32, (ky, total, wide), 1)
    column = lax.broadcasted_iota(jnp.int32, (ky, total, wide), 2)
    diagonal = (row == column) | (row + total == column)
    for f in range(4):
        high, low = split(jnp.concatenate([sums[f, 0], sums[f, 1]], 1))
        spread = (real_dot(high, mix_v[...]) + real_dot(low, mix_v[...])).reshape(ky, total, wide)
        edges[:ky, f, :] = jnp.sum(jnp.where(diagonal, spread, 0.0), axis=1)
    outs.append(copies.start(edges, edge_out))
    for copy in outs:
        copy.wait()


def front(place, thick, face, shifts, across, sines, rhs, cotangent, devices):
    _, levels, ky, size = rhs.shape
    total = thick.shape[0]
    chips = total // (2 * levels)
    group = min(2 * ROWS, ky)
    half = size // 2
    wide = 2 * total
    single = lambda *shape: pltpu.VMEM(shape, jnp.float32)
    tables = [(n, ky, size) for n in (total + 1, levels, levels, 3, 4, chips - 1)]
    shapes = tables + [(2, 2, levels, ky, size), (2, 2, 2, ky // 2, size), (2, 2, 2, ky // 2, size), (devices, 4, wide)]
    return pl.pallas_call(
        functools.partial(front_kernel, levels, total, group),
        in_specs=[in_smem] * 4 + [in_hbm] * 9,
        out_specs=[in_hbm] * len(shapes),
        out_shape=[jax.ShapeDtypeStruct(shape, jnp.float32) for shape in shapes],
        scratch_shapes=[
            pltpu.SemaphoreType.DMA((22,)),
            single(1, size),
            single(ROWS, size),
            pltpu.VMEM((2 * LANES, wide), jnp.bfloat16),
            single(2, 2, levels, ky, size),
            *[pltpu.VMEM((half, half), jnp.bfloat16)] * 4,
            *[single(*shape) for shape in tables],
            single(2, 2, levels, ky, size),
            single(2, 2, 2, ky, size),
            single(2, 4, ky, size),
            single(4, 2, ky * total, LANES),
            single(devices, 4, wide),
            single(ky, size),
            *[single(2 * levels, group, size)] * 5,
            *[single(chips, group, size)] * 2,
        ],
        compiler_params=params,
        name="front",
    )(place, thick, face, shifts, across, sines, edge_matrix(size, total), rhs, cotangent, *half_sines(size))


def chip_kernel(chips, place, keep, got, pair, *refs):
    outs = refs[:chips - 1]
    sems, keep_v, got_v, pair_v, down_v, up_v = refs[chips - 1:]
    copies = Copies(sems)
    chip = place[0] // 2
    upper = place[0] % 2 == 0
    half = keep_v.shape[3]
    here = pl.ds(pl.multiple_of((place[0] % 2) * half, ROWS), half)
    for copy in [copies.start(keep, keep_v), copies.start(got, got_v), copies.start(pair.at[:, here], pair_v)]:
        copy.wait()
    for a in range(2):
        first, second = jnp.where(upper, keep_v[a], got_v[a]), jnp.where(upper, got_v[a], keep_v[a])
        down_v[a] = second[0] + pair_v[1] * first[0]
        up_v[a] = first[1] + pair_v[2] * second[1]
    for apart in range(1, chips):
        goes_down = chip + apart < chips
        sem = sems.at[2 + apart]

        @pl.when(goes_down)
        def _():
            pltpu.make_async_copy(down_v, outs[apart - 1], sem).start()

        @pl.when(jnp.logical_not(goes_down))
        def _():
            pltpu.make_async_copy(up_v, outs[apart - 1], sem).start()

    for apart in range(1, chips):
        pltpu.make_async_copy(down_v, outs[apart - 1], sems.at[2 + apart]).wait()


def chip_sums(place, keep, got, pair, chips):
    _, _, _, half, size = keep.shape
    single = lambda *shape: pltpu.VMEM(shape, jnp.float32)
    shape = (2, 2, half, size)
    return pl.pallas_call(
        functools.partial(chip_kernel, chips),
        in_specs=[in_smem] + [in_hbm] * 3,
        out_specs=[in_hbm] * (chips - 1),
        out_shape=[jax.ShapeDtypeStruct(shape, jnp.float32)] * (chips - 1),
        scratch_shapes=[
            pltpu.SemaphoreType.DMA((2 + chips,)),
            single(*keep.shape),
            single(*keep.shape),
            single(4, half, size),
            single(*shape),
            single(*shape),
        ],
        compiler_params=params,
        name="chip_sums",
    )(place, keep, got, pair)


def join_kernel(chips, place, keep, got, pair, far, *refs):
    news = refs[:chips - 1]
    mine, theirs, sems, keep_v, got_v, pair_v, far_v, news_v, mine_v, theirs_v = refs[chips - 1:]
    copies = Copies(sems)
    chip = place[0] // 2
    upper = place[0] % 2 == 0
    half = keep_v.shape[3]
    here = pl.ds(pl.multiple_of((place[0] % 2) * half, ROWS), half)
    ready = [copies.start(keep, keep_v), copies.start(got, got_v), copies.start(pair.at[:, here], pair_v), copies.start(far.at[:, here], far_v)]
    ready += [copies.start(news[i], news_v.at[i]) for i in range(chips - 1)]
    for copy in ready:
        copy.wait()
    for a in range(2):
        for ri in range(2):
            first, second = (keep_v, got_v), (got_v, keep_v)
            pick = lambda refs, way: jnp.where(upper, refs[0][a, way, ri], refs[1][a, way, ri])
            down = jnp.zeros((half, keep_v.shape[4]), jnp.float32)
            up = down
            for apart in range(1, chips):
                term = far_v[apart - 1] * news_v[apart - 1, a, ri]
                down = down + jnp.where(chip >= apart, term, 0.0)
                up = up + jnp.where(chip >= apart, 0.0, term)
            inner_up = pick(second, 1) + pair_v[3] * up
            inner_down = pick(first, 0) + pair_v[0] * down
            mine_v[a, 0, ri] = jnp.where(upper, down, inner_down)
            mine_v[a, 1, ri] = jnp.where(upper, inner_up, up)
            theirs_v[a, 0, ri] = jnp.where(upper, inner_down, down)
            theirs_v[a, 1, ri] = jnp.where(upper, up, inner_up)
    for copy in [copies.start(theirs_v, theirs), copies.start(mine_v, mine)]:
        copy.wait()


def join(place, keep, got, pair, far, news):
    chips = len(news) + 1
    _, _, _, half, size = keep.shape
    single = lambda *shape: pltpu.VMEM(shape, jnp.float32)
    return pl.pallas_call(
        functools.partial(join_kernel, chips),
        in_specs=[in_smem] + [in_hbm] * (3 + chips),
        out_specs=[in_hbm] * 2,
        out_shape=[jax.ShapeDtypeStruct(keep.shape, jnp.float32)] * 2,
        scratch_shapes=[
            pltpu.SemaphoreType.DMA((5 + chips,)),
            single(*keep.shape),
            single(*keep.shape),
            single(4, half, size),
            single(chips - 1, half, size),
            single(chips - 1, 2, 2, half, size),
            single(*keep.shape),
            single(*keep.shape),
        ],
        compiler_params=params,
        name="join",
    )(place, keep, got, pair, far, *news)


def inverse_kernel(per, thick, face, lam, out, m_all, f_all, g_all):
    total = f_all.shape[0]
    rows = lam.shape[0]
    classes = out.shape[0]
    shift = lam[...]
    one = jnp.ones_like(shift)
    zero = jnp.zeros_like(shift)

    def step(j, state):
        f, r, phi, s = state
        m = face[j] * r
        f = shift * thick[j] + m * f
        r = 1.0 / (face[j + 1] + f)
        m_all[j] = m
        f_all[j] = f
        i = total - 1 - j
        u = face[i + 1] * s * phi
        phi = shift * thick[i] + u
        s = 1.0 / (face[i] + phi)
        g_all[i] = u
        return f, r, phi, s

    lax.fori_loop(0, total, step, (one, one, zero, zero))

    def centre(j, _):
        g_all[j] = 1.0 / (f_all[j] + g_all[j])
        return 0

    lax.fori_loop(0, total, centre, 0)
    wide = out.shape[2]
    sub = lax.broadcasted_iota(jnp.int32, (ROWS, LANES), 0)
    lane = lax.broadcasted_iota(jnp.int32, (ROWS, wide), 1)
    row = lax.broadcasted_iota(jnp.int32, (ROWS, wide), 0)
    line = lambda ref, j, t: jnp.broadcast_to(ref[j, t:t + 1, :], (ROWS, LANES))

    def put(j, z, sums):
        new = []
        for c in range(classes):
            tiles = z[c * per:(c + 1) * per]
            total_tile = tiles[0]
            for tile in tiles[1:]:
                total_tile = total_tile + tile
            value = jnp.sum(total_tile, axis=1, keepdims=True)
            new.append(jnp.where(lane == j, value, sums[c]))
        return new

    for base in range(0, total, ROWS):
        z = [jnp.zeros((ROWS, LANES), jnp.float32)] * (classes * per)
        sums = [jnp.zeros((ROWS, wide), jnp.float32)] * classes
        for i in range(ROWS - 1, -1, -1):
            j = base + i
            for t in range(classes * per):
                moved = z[t] * line(m_all, j + 1, t) if i < ROWS - 1 else z[t]
                z[t] = jnp.where(sub == i, line(g_all, j, t), moved)
            sums = put(j, z, sums)

        def above(back, state):
            z, sums = state
            for i in range(ROWS):
                j = base - 1 - back * ROWS - i
                z = [z[t] * line(m_all, j + 1, t) for t in range(classes * per)]
                sums = put(j, z, sums)
            return z, sums

        if base:
            z, sums = lax.fori_loop(0, base // ROWS, above, (z, sums))
        for c in range(classes):
            out[c, base:base + ROWS, :] = sums[c] * jnp.where(lane == base + row, 0.5, 1.0)


def inverse_sums(thick, face, lam, per):
    total = thick.shape[0]
    classes = lam.shape[0] // per
    wide = -(-total // LANES) * LANES
    spare = -lam.shape[0] % ROWS
    lam = jnp.pad(lam, ((0, spare), (0, 0)), constant_values=1.0) if spare else lam
    return pl.pallas_call(
        functools.partial(inverse_kernel, per),
        in_specs=[in_smem, in_smem, in_vmem],
        out_shape=jax.ShapeDtypeStruct((classes, total, wide), jnp.float32),
        scratch_shapes=[pltpu.VMEM((total,) + lam.shape, jnp.float32)] * 3,
        compiler_params=params,
        name="inverse_sums",
    )(thick, face, lam)


def interface_kernel(waves, matrices, edges, inverse, out):
    devices, _, wide = edges.shape
    total = wide // 2
    rows = 4 * waves
    lines = []
    for w in range(waves):
        line = edges[w]
        for d in range(1, devices // waves):
            line = line + edges[d * waves + w]
        lines.append(line)
    lines = jnp.concatenate(lines, 0)
    near, far = exact_dot(matrices[0], lines, NN), exact_dot(matrices[1], lines, NN)
    mixed = near[:, :total] + far[:, total:]
    result = jnp.zeros((2 * rows, total), jnp.float32)
    for c in range(inverse.shape[0]):
        part = mixed[c * 2 * rows:(c + 1) * 2 * rows]
        square = inverse[c][:, :total]
        result = result + (exact_dot(part, square, NN) + exact_dot(part, square, NT))
    result = jnp.concatenate([result[:rows], result[rows:]], 1)
    for w in range(waves):
        line = result[4 * w:4 * w + 4]
        for d in range(devices // waves):
            out[d * waves + w] = line


def interface(edges, inverse, waves, size):
    return pl.pallas_call(
        functools.partial(interface_kernel, waves),
        in_specs=[in_vmem] * 3,
        out_specs=in_vmem,
        out_shape=jax.ShapeDtypeStruct(edges.shape, jnp.float32),
        compiler_params=params,
        name="interface",
    )(interface_matrices(waves, size), edges, inverse)


def back_kernel(levels, total, place, thick, values, spread, t, mine, theirs, sines, b, r, m, end, odd_top, odd_rest, even_top, even_rest, out0, out1, sems, values_v, spread_v, t_v, ends, sines_v, b_v, r_v, m_v, end_v, ot, orest, et, er, picked, u_all, q_all, out_v):
    _, _, _, ky, size = b_v.shape
    first = place[0] * levels
    half = size // 2
    many = half // LANES
    core = place[0] % 2
    copies = Copies(sems)
    early = [copies.start(values.at[pl.ds(0, ky)], values_v), copies.start(spread, spread_v)]
    table = copies.start(t, t_v)
    both = []
    for source, start in ((mine, core), (theirs, 1 - core)):
        here = pl.ds(pl.multiple_of(start * (ky // 2), ROWS), ky // 2)
        both.append(copies.start(source, ends.at[:, :, :, here]))
    both.append(copies.start(sines, sines_v))
    rest = [copies.start(source, target) for source, target in ((r, r_v), (m, m_v), (end, end_v), (b, b_v), (odd_top, ot), (odd_rest, orest), (even_top, et), (even_rest, er))]
    for copy in early:
        copy.wait()
    lane = lax.broadcasted_iota(jnp.int32, (ky, 2 * total), 1)
    for f in range(4):
        parts = [part.astype(jnp.float32) for part in split(values_v[:, f, :])]
        for j in range(total):
            spot = (lane == j) | (lane == total + j)
            for p in range(2):
                picked[p, j * ky:(j + 1) * ky, :] = jnp.where(spot, parts[p], 0.0).astype(jnp.bfloat16)
        u_all[f] = (real_dot(picked[0], spread_v[...]) + real_dot(picked[1], spread_v[...])).reshape(total, ky, 2 * LANES)
    table.wait()
    for copy in both:
        copy.wait()

    def source(f, j, here):
        pair = u_all[f, j, here] * thick[j]
        return jnp.concatenate([pair[:, :LANES]] * many + [pair[:, LANES:]] * many, 1)

    def sweep(g, _):
        here = pl.ds(pl.multiple_of(g * ROWS, ROWS), ROWS)

        def from_above(block, y):
            for i in range(levels):
                j = block * levels + i
                step = t_v[j, here]
                y = [step * y[f] + source(f, j, here) for f in range(4)]
            return y

        def from_below(block, y):
            for i in range(levels):
                j = total - 1 - block * levels - i
                step = t_v[j + 1, here]
                y = [step * y[f] + source(f, j, here) for f in range(4)]
            return y

        zero = [jnp.zeros((ROWS, size), jnp.float32)] * 4
        wave = sines_v[...]
        for way, y in (
            (0, lax.fori_loop(0, place[0], from_above, zero)),
            (1, lax.fori_loop(0, total // levels - 1 - place[0], from_below, zero)),
        ):
            for f in range(4):
                ends[f // 2, way, f % 2, here] += wave * y[f]
        return 0

    lax.fori_loop(0, ky // ROWS, sweep, 0)
    for copy in rest:
        copy.wait()
    rows = levels * ky
    lane = lax.broadcasted_iota(jnp.int32, (ky, LANES), 1)
    outs = []
    for f in range(4):
        a, ri = f // 2, f % 2

        def tile(g, _):
            here = pl.ds(pl.multiple_of(g * ROWS, ROWS), ROWS)
            wave = sines_v[...]
            y = ends[a, 0, ri, here]
            ys = []
            for j in range(levels):
                y = b_v[a, ri, j, here] + wave * source(f, first + j, here) + m_v[j, here] * y
                ys.append(y)
            value = (y + end_v[0, here] * ends[a, 1, ri, here]) * end_v[1, here]
            q_all[levels - 1, here] = value
            for j in range(levels - 2, -1, -1):
                value = r_v[j, here] * ys[j] + m_v[j + 1, here] * value
                q_all[j, here] = value
            return 0

        lax.fori_loop(0, ky // ROWS, tile, 0)
        low, high = to_cells(
            q_all[:, :, :half].reshape(rows, half), q_all[:, :, half:].reshape(rows, half), ot, orest, et, er
        )
        for j in range(levels):
            height = thick[first + j] if a else 1.0
            scale = (2.0 / size) * height
            here = slice(j * ky, (j + 1) * ky)
            u = (u_all[f, first + j, :, :LANES] + u_all[f, first + j, :, LANES:]) * (0.5 * height)
            if many > 1:
                out_v[f, j, :, LANES:half] = low[here, LANES:] * scale
            out_v[f, j, :, :LANES] = jnp.where(lane == 0, u, low[here, :LANES] * scale)
            out_v[f, j, :, half:] = high[here] * scale
        outs.append(copies.start(out_v.at[f], (out0, out1)[a].at[ri]))
    for copy in outs:
        copy.wait()


def back(place, thick, values, sines, t, r, m, end, b, mine, theirs):
    _, _, levels, ky, size = b.shape
    total = t.shape[0] - 1
    half = size // 2
    single = lambda *shape: pltpu.VMEM(shape, jnp.float32)
    return pl.pallas_call(
        functools.partial(back_kernel, levels, total),
        in_specs=[in_smem] * 2 + [in_hbm] * 14,
        out_specs=[in_hbm] * 2,
        out_shape=[jax.ShapeDtypeStruct((2, levels, ky, size), jnp.float32)] * 2,
        scratch_shapes=[
            pltpu.SemaphoreType.DMA((18,)),
            single(ky, 4, 2 * total),
            pltpu.VMEM((2 * total, 2 * LANES), jnp.bfloat16),
            single(*t.shape),
            single(2, 2, 2, ky, size),
            single(ROWS, size),
            single(*b.shape),
            single(*r.shape),
            single(*m.shape),
            single(*end.shape),
            *[pltpu.VMEM((half, half), jnp.bfloat16)] * 4,
            pltpu.VMEM((2, total * ky, 2 * total), jnp.bfloat16),
            single(4, total, ky, 2 * LANES),
            single(levels, ky, size),
            single(4, levels, ky, size),
        ],
        compiler_params=params,
        name="back",
    )(place, thick, values, spread_matrix(total), t, mine, theirs, sines, b, r, m, end, *half_sines(size, True))


def shards(rhs, cotangent, thickness, ky_shift):
    waves = lax.axis_size("wave")
    count = lax.axis_size("depth")
    depth_pos = lax.axis_index("depth")
    wave_pos = lax.axis_index("wave")
    _, levels, ky, size = rhs.shape
    full = waves * size
    devices = waves * count
    chips = count // 2
    place = depth_pos.astype(jnp.int32).reshape(1)

    def across(a):
        return lax.ppermute(a, "depth", [(d, d ^ 1) for d in range(count)])

    def along(a, apart):
        return lax.ppermute(a, "depth", [(d, (d + 2 * apart) % count) for d in range(count)])

    def everywhere(a):
        return lax.all_to_all(a, ("depth", "wave"), split_axis=0, concat_axis=0, tiled=True)

    def horizontal(wavenumber, length):
        return (aspect_ratio * 4.0 * np.sin(math.pi * wavenumber / length) ** 2).astype(np.float32)

    inner_face = 2.0 / (thickness[:-1] + thickness[1:])
    face = jnp.concatenate([2.0 / thickness[:1], inner_face, jnp.zeros((1,), jnp.float32)])
    order = wave_order(size)
    sines = np.broadcast_to(np.sin(np.pi * order / size)[None, :], (ROWS, size)).astype(np.float32)
    across_k = horizontal(order, 2 * size)[None, :]
    t, r, m, end, pair, far, b, keep, give, edges = front(
        place, thickness, face, ky_shift, across_k, sines, rhs, cotangent, devices
    )

    classes = waves // 2 + 1
    wavenumber = (np.arange(classes)[:, None] + waves * np.arange(size)[None, :]).reshape(-1, LANES)
    shifts = jnp.pad(ky_shift, (0, devices - ky), constant_values=1.0) if devices > ky else ky_shift
    my_shift = lax.dynamic_slice_in_dim(shifts, depth_pos * waves + wave_pos, 1)

    got = across(give)
    edges = everywhere(edges)
    sums = chip_sums(place, keep, got, pair, chips)
    news = [along(sums[apart - 1], apart) for apart in range(1, chips)]
    inverse = inverse_sums(thickness, face, my_shift + horizontal(wavenumber, full), size // LANES)
    values = everywhere(interface(edges, inverse, waves, size))
    mine, theirs = join(place, keep, got, pair, far, news)
    return back(place, thickness, values, sines, t, r, m, end, b, mine, across(theirs))


def solution(mesh):
    spec = P(None, "depth", None, "wave")
    return jax.shard_map(shards, mesh=mesh, in_specs=(spec, spec, P(), P()), out_specs=(spec, spec), check_vma=False)
```

```python
import functools
import math

import jax
import jax.numpy as jnp
import numpy as np
from jax import lax
from jax.experimental import pallas as pl
from jax.experimental.pallas import tpu as pltpu
from jax.sharding import PartitionSpec as P

aspect_ratio = 1.0
LANES = 128
ROWS = 8
VMEM_BYTES = 60 * 1024 * 1024
real_dot = functools.partial(jnp.dot, preferred_element_type=jnp.float32)
exact_dot = functools.partial(lax.dot_general, precision=lax.Precision.HIGHEST, preferred_element_type=jnp.float32)
NN = (((1,), (0,)), ((), ()))
NT = (((1,), (1,)), ((), ()))
in_smem = pl.BlockSpec(memory_space=pltpu.SMEM)
in_hbm = pl.BlockSpec(memory_space=pl.ANY)
in_vmem = pl.BlockSpec(memory_space=pltpu.VMEM)
params = pltpu.CompilerParams(vmem_limit_bytes=VMEM_BYTES)


def wave_order(size):
    return np.concatenate([np.arange(1, size, 2), np.arange(0, size, 2)])


def half_sines(size, back=False):
    half = size // 2
    place = np.arange(half)
    place[0] = half
    parts = []
    for waves in (np.arange(1, size, 2), np.arange(0, size, 2)):
        matrix = np.sin(np.pi * (np.outer(place, waves) % (2 * size)) / size)
        if waves[0] == 0:
            matrix[0] = 0.0
            matrix[:, 0] = 0.0
        matrix = (matrix.T if back else matrix).astype(np.float32)
        top = matrix.astype(jnp.bfloat16)
        parts += [top, (matrix - top.astype(np.float32)).astype(jnp.bfloat16)]
    return parts


def edge_matrix(size, total):
    matrix = np.full((2 * LANES, 2 * total), 2.0 / size, np.float32)
    matrix[LANES:, total:] = -2.0 / size
    return matrix.astype(jnp.bfloat16)


def spread_matrix(total):
    matrix = np.ones((2 * total, 2 * LANES), np.float32)
    matrix[total:, LANES:] = -1.0
    return matrix.astype(jnp.bfloat16)


def interface_matrices(waves, size):
    classes = waves // 2 + 1
    matrix = np.zeros((2, classes, 2, waves, 4, waves, 4))
    for c in range(classes):
        weight = (1.0 if c in (0, waves // 2) else 2.0) / (size * waves)
        for w in range(waves):
            for e in range(2):
                for v in range(waves):
                    for g in range(2):
                        value = weight * math.cos(2.0 * math.pi * (c * (w + e - v - g) % waves) / waves)
                        for f in range(4):
                            matrix[g, c, e, w, f, v, f] = value
    return matrix.reshape(2, classes * 2 * waves * 4, waves * 4).astype(np.float32)


def split(values):
    high = values.astype(jnp.bfloat16)
    return high, (values - high.astype(jnp.float32)).astype(jnp.bfloat16)


def product(values, top, rest):
    high, low = split(values)
    return real_dot(high, top[...]) + (real_dot(low, top[...]) + real_dot(high, rest[...]))


def mirror(values):
    rows = values.shape[0]
    lane = lax.broadcasted_iota(jnp.int32, (rows, LANES), 1)
    back = (LANES - lane) % LANES
    tiles = [values[:, a * LANES:(a + 1) * LANES] for a in range(values.shape[1] // LANES)]
    many = len(tiles)
    out = []
    for a in range(many):
        turned = jnp.take_along_axis(tiles[many - 1 - a], back, axis=1)
        out.append(jnp.where(lane == 0, tiles[(many - a) % many], turned))
    return jnp.concatenate(out, 1) if many > 1 else out[0]


def to_waves(values, odd_top, odd_rest, even_top, even_rest):
    half = values.shape[1] // 2
    low, high = values[:, :half], mirror(values[:, half:])
    lane = lax.broadcasted_iota(jnp.int32, low.shape, 1)
    low = jnp.where(lane == 0, 0.0, low)
    return product(low + high, odd_top, odd_rest), product(low - high, even_top, even_rest)


def to_cells(odd, even, odd_top, odd_rest, even_top, even_rest):
    p, m = product(odd, odd_top, odd_rest), product(even, even_top, even_rest)
    return p + m, mirror(p - m)


class Copies:
    def __init__(self, sems):
        self.sems, self.used = sems, 0

    def start(self, source, target):
        copy = pltpu.make_async_copy(source, target, self.sems.at[self.used])
        self.used += 1
        copy.start()
        return copy


def coefficients(levels, total, group, place, thick, face, shifts, across, t_out, r_out, m_out, end_out, pair_out, far_out, lam, m_chip, r_chip, f_chip, n_chip, u_chip, down_all, up_all):
    ky = lam.shape[0]
    span = 2 * levels
    chips = total // span
    chip = place[0] // 2
    start = chip * span
    upper = place[0] % 2 == 0
    own = (place[0] % 2) * levels
    for row in range(ky):
        lam[row:row + 1, :] = across[...] + shifts[row]

    def down_step(shift, j, f, r):
        m = face[j] * r
        f = shift * thick[j] + m * f
        return m, f, 1.0 / (face[j + 1] + f)

    def up_step(shift, j, phi, s):
        n = face[j + 1] * s
        u = n * phi
        phi = shift * thick[j] + u
        return n, u, phi, 1.0 / (face[j] + phi)

    def part(g, _):
        here = pl.ds(pl.multiple_of(g * group, group), group)
        shift = lam[here]
        one = jnp.ones_like(shift)
        zero = jnp.zeros_like(shift)

        def down_chip(c, state):
            f, r = state
            product = one
            for i in range(span):
                m, f, r = down_step(shift, c * span + i, f, r)
                t_out[c * span + i, here] = m
                product = product * m
            down_all[c] = product
            return f, r

        def up_chip(back, state):
            phi, s = state
            c = chips - 1 - back
            product = one
            for i in range(span - 1, -1, -1):
                n, _, phi, s = up_step(shift, c * span + i, phi, s)
                t_out[c * span + i + 1, here] = n
                product = product * n
            up_all[c] = product
            return phi, s

        f, r = lax.fori_loop(0, chip, down_chip, (one, one))
        for i in range(span):
            m, f, r = down_step(shift, start + i, f, r)
            m_chip[i], f_chip[i], r_chip[i] = m, f, r
        phi, s = lax.fori_loop(0, chips - 1 - chip, up_chip, (zero, zero))
        for i in range(span - 1, -1, -1):
            n, u, phi, s = up_step(shift, start + i, phi, s)
            n_chip[i], u_chip[i] = n, u

        for i in range(levels):
            t_out[start + i, here] = m_chip[i]
            t_out[start + levels + 1 + i, here] = n_chip[levels + i]
        t_out[start + levels, here] = jnp.where(upper, n_chip[levels - 1], m_chip[levels])
        for i in range(levels):
            r_out[i, here] = r_chip[own + i]
            m_out[i, here] = m_chip[own + i]
        last = own + levels - 1
        end_out[0, here] = n_chip[last]
        end_out[1, here] = 1.0 / (f_chip[last] + u_chip[last])
        end_out[2, here] = f_chip[own] + u_chip[own]
        for core in range(2):
            down, up = m_chip[core * levels], n_chip[core * levels]
            for i in range(1, levels):
                down = down * m_chip[core * levels + i]
                up = up * n_chip[core * levels + i]
            pair_out[core, here] = down
            pair_out[2 + core, here] = up
        above, below = [one], [one]
        for apart in range(1, chips - 1):
            above.append(above[-1] * jnp.where(chip >= apart, down_all[jnp.maximum(chip - apart, 0)], one))
            below.append(below[-1] * jnp.where(chip + apart < chips, up_all[jnp.minimum(chip + apart, chips - 1)], one))
        for apart in range(1, chips):
            far_out[apart - 1, here] = jnp.where(chip >= apart, above[apart - 1], below[chips - apart - 1])
        return 0

    lax.fori_loop(0, ky // group, part, 0)


def lane_sum(values):
    tiles = [values[:, t * LANES:(t + 1) * LANES] for t in range(values.shape[1] // LANES)]
    while len(tiles) > 1:
        tiles = [a + b for a, b in zip(tiles[0::2], tiles[1::2])] + tiles[len(tiles) // 2 * 2:]
    return tiles[0]


def front_kernel(levels, total, group, place, thick, face, shifts, across, sines, edge_mix, x0, x1, odd_top, odd_rest, even_top, even_rest, t_out, r_out, m_out, end_out, pair_out, far_out, b_out, keep_out, give_out, edge_out, sems, *scratch):
    across_v, sines_v, mix_v, x, ot, orest, et, er, t, r, m, end, pair, far, b, c_all, z_all, sums, edges, lam, *work = scratch
    _, _, _, ky, size = x.shape
    first = place[0] * levels
    half = size // 2
    copies = Copies(sems)
    early = [copies.start(across, across_v)]
    fields = [copies.start(x0, x.at[0])]
    mats = [copies.start(source, target) for source, target in ((odd_top, ot), (odd_rest, orest), (even_top, et), (even_rest, er))]
    mats += [copies.start(sines, sines_v)]
    fields += [copies.start(x1, x.at[1])]
    late = [copies.start(edge_mix, mix_v)]
    for copy in early:
        copy.wait()
    coefficients(levels, total, group, place, thick, face, shifts, across_v, t, r, m, end, pair, far, lam, *work)
    outs = [copies.start(source, target) for source, target in ((pair, pair_out), (far, far_out))]
    outs += [copies.start(source, target) for source, target in ((t, t_out), (r, r_out), (m, m_out), (end, end_out))]
    for copy in mats:
        copy.wait()
    lane = lax.broadcasted_iota(jnp.int32, (ROWS, LANES), 1)
    spot = jnp.where(lane == 0, size / 4.0, 0.0)
    core = place[0] % 2

    def put(f, rows, values, height, own=None):
        odd, even = lane_sum(values[:, :half]) * height, lane_sum(values[:, half:]) * height
        if own is not None:
            odd, even = odd + own, even + own
        sums[f, 0, rows, :] = odd
        sums[f, 1, rows, :] = even

    for a in range(2):
        fields[a].wait()
        odd, even = to_waves(x[a].reshape(2 * levels * ky, size), ot, orest, et, er)
        for ri in range(2):
            for j in range(levels):
                rows = slice((ri * levels + j) * ky, (ri * levels + j + 1) * ky)
                scale = thick[first + j] if a == 0 else 1.0
                b[a, ri, j, :, :half] = odd[rows] * scale
                b[a, ri, j, :, half:] = even[rows] * scale
        outs.append(copies.start(b.at[a], b_out.at[a]))
        for ri in range(2):
            f = 2 * a + ri

            def tile(g, _):
                here = pl.ds(pl.multiple_of(g * ROWS, ROWS), ROWS)
                wave = sines_v[...]
                y = b[a, ri, 0, here]
                ys = [y]
                for j in range(1, levels):
                    y = b[a, ri, j, here] + m[j, here] * y
                    ys.append(y)
                c_all[a, 0, ri, here] = y
                value = y * end[1, here]
                z_all[1, f, here] = value * wave
                for j in range(levels - 1, -1, -1):
                    if j < levels - 1:
                        value = r[j, here] * ys[j] + m[j + 1, here] * value
                    height = thick[first + j]
                    own = jnp.broadcast_to(x[a, ri, j, here, 0:1], (ROWS, LANES)) * (spot * height if a == 0 else spot)
                    put(f, pl.ds(g * ROWS * total + first + j, ROWS, stride=total), value * wave, height, own)
                z_all[0, f, here] = value * wave
                c_all[a, 1, ri, here] = value * end[2, here]
                return 0

            lax.fori_loop(0, ky // ROWS, tile, 0)
        for start, out in ((core, keep_out), (1 - core, give_out)):
            here = pl.ds(pl.multiple_of(start * (ky // 2), ROWS), ky // 2)
            outs.append(copies.start(c_all.at[a, :, :, here], out.at[a]))

    def reach(g, _):
        here = pl.ds(pl.multiple_of(g * ROWS, ROWS), ROWS)

        def up(block, z):
            for i in range(levels):
                j = first - 1 - block * levels - i
                step = t[j + 1, here]
                z = [step * one for one in z]
                for f in range(4):
                    put(f, pl.ds(g * ROWS * total + j, ROWS, stride=total), z[f], thick[j])
            return z

        def down(block, z):
            for i in range(levels):
                j = first + levels + block * levels + i
                step = t[j, here]
                z = [step * one for one in z]
                for f in range(4):
                    put(f, pl.ds(g * ROWS * total + j, ROWS, stride=total), z[f], thick[j])
            return z

        lax.fori_loop(0, place[0], up, [z_all[0, f, here] for f in range(4)])
        lax.fori_loop(0, total // levels - 1 - place[0], down, [z_all[1, f, here] for f in range(4)])
        return 0

    lax.fori_loop(0, ky // ROWS, reach, 0)
    for copy in late:
        copy.wait()
    if edges.shape[0] > ky:
        edges[...] = jnp.zeros_like(edges)
    wide = 2 * total
    row = lax.broadcasted_iota(jnp.int32, (ky, total, wide), 1)
    column = lax.broadcasted_iota(jnp.int32, (ky, total, wide), 2)
    diagonal = (row == column) | (row + total == column)
    for f in range(4):
        high, low = split(jnp.concatenate([sums[f, 0], sums[f, 1]], 1))
        spread = (real_dot(high, mix_v[...]) + real_dot(low, mix_v[...])).reshape(ky, total, wide)
        edges[:ky, f, :] = jnp.sum(jnp.where(diagonal, spread, 0.0), axis=1)
    outs.append(copies.start(edges, edge_out))
    for copy in outs:
        copy.wait()


def front(place, thick, face, shifts, across, sines, rhs, cotangent, devices):
    _, levels, ky, size = rhs.shape
    total = thick.shape[0]
    chips = total // (2 * levels)
    group = min(2 * ROWS, ky)
    half = size // 2
    wide = 2 * total
    single = lambda *shape: pltpu.VMEM(shape, jnp.float32)
    tables = [(n, ky, size) for n in (total + 1, levels, levels, 3, 4, chips - 1)]
    shapes = tables + [(2, 2, levels, ky, size), (2, 2, 2, ky // 2, size), (2, 2, 2, ky // 2, size), (devices, 4, wide)]
    return pl.pallas_call(
        functools.partial(front_kernel, levels, total, group),
        in_specs=[in_smem] * 4 + [in_hbm] * 9,
        out_specs=[in_hbm] * len(shapes),
        out_shape=[jax.ShapeDtypeStruct(shape, jnp.float32) for shape in shapes],
        scratch_shapes=[
            pltpu.SemaphoreType.DMA((22,)),
            single(1, size),
            single(ROWS, size),
            pltpu.VMEM((2 * LANES, wide), jnp.bfloat16),
            single(2, 2, levels, ky, size),
            *[pltpu.VMEM((half, half), jnp.bfloat16)] * 4,
            *[single(*shape) for shape in tables],
            single(2, 2, levels, ky, size),
            single(2, 2, 2, ky, size),
            single(2, 4, ky, size),
            single(4, 2, ky * total, LANES),
            single(devices, 4, wide),
            single(ky, size),
            *[single(2 * levels, group, size)] * 5,
            *[single(chips, group, size)] * 2,
        ],
        compiler_params=params,
        name="front",
    )(place, thick, face, shifts, across, sines, edge_matrix(size, total), rhs, cotangent, *half_sines(size))


def chip_kernel(chips, place, keep, got, pair, *refs):
    outs = refs[:chips - 1]
    sems, keep_v, got_v, pair_v, down_v, up_v = refs[chips - 1:]
    copies = Copies(sems)
    chip = place[0] // 2
    upper = place[0] % 2 == 0
    half = keep_v.shape[3]
    here = pl.ds(pl.multiple_of((place[0] % 2) * half, ROWS), half)
    for copy in [copies.start(keep, keep_v), copies.start(got, got_v), copies.start(pair.at[:, here], pair_v)]:
        copy.wait()
    for a in range(2):
        first, second = jnp.where(upper, keep_v[a], got_v[a]), jnp.where(upper, got_v[a], keep_v[a])
        down_v[a] = second[0] + pair_v[1] * first[0]
        up_v[a] = first[1] + pair_v[2] * second[1]
    for apart in range(1, chips):
        goes_down = chip + apart < chips
        sem = sems.at[2 + apart]

        @pl.when(goes_down)
        def _():
            pltpu.make_async_copy(down_v, outs[apart - 1], sem).start()

        @pl.when(jnp.logical_not(goes_down))
        def _():
            pltpu.make_async_copy(up_v, outs[apart - 1], sem).start()

    for apart in range(1, chips):
        pltpu.make_async_copy(down_v, outs[apart - 1], sems.at[2 + apart]).wait()


def chip_sums(place, keep, got, pair, chips):
    _, _, _, half, size = keep.shape
    single = lambda *shape: pltpu.VMEM(shape, jnp.float32)
    shape = (2, 2, half, size)
    return pl.pallas_call(
        functools.partial(chip_kernel, chips),
        in_specs=[in_smem] + [in_hbm] * 3,
        out_specs=[in_hbm] * (chips - 1),
        out_shape=[jax.ShapeDtypeStruct(shape, jnp.float32)] * (chips - 1),
        scratch_shapes=[
            pltpu.SemaphoreType.DMA((2 + chips,)),
            single(*keep.shape),
            single(*keep.shape),
            single(4, half, size),
            single(*shape),
            single(*shape),
        ],
        compiler_params=params,
        name="chip_sums",
    )(place, keep, got, pair)


def join_kernel(chips, place, keep, got, pair, far, *refs):
    news = refs[:chips - 1]
    mine, theirs, sems, keep_v, got_v, pair_v, far_v, news_v, mine_v, theirs_v = refs[chips - 1:]
    copies = Copies(sems)
    chip = place[0] // 2
    upper = place[0] % 2 == 0
    half = keep_v.shape[3]
    here = pl.ds(pl.multiple_of((place[0] % 2) * half, ROWS), half)
    ready = [copies.start(keep, keep_v), copies.start(got, got_v), copies.start(pair.at[:, here], pair_v), copies.start(far.at[:, here], far_v)]
    ready += [copies.start(news[i], news_v.at[i]) for i in range(chips - 1)]
    for copy in ready:
        copy.wait()
    for a in range(2):
        for ri in range(2):
            first, second = (keep_v, got_v), (got_v, keep_v)
            pick = lambda refs, way: jnp.where(upper, refs[0][a, way, ri], refs[1][a, way, ri])
            down = jnp.zeros((half, keep_v.shape[4]), jnp.float32)
            up = down
            for apart in range(1, chips):
                term = far_v[apart - 1] * news_v[apart - 1, a, ri]
                down = down + jnp.where(chip >= apart, term, 0.0)
                up = up + jnp.where(chip >= apart, 0.0, term)
            inner_up = pick(second, 1) + pair_v[3] * up
            inner_down = pick(first, 0) + pair_v[0] * down
            mine_v[a, 0, ri] = jnp.where(upper, down, inner_down)
            mine_v[a, 1, ri] = jnp.where(upper, inner_up, up)
            theirs_v[a, 0, ri] = jnp.where(upper, inner_down, down)
            theirs_v[a, 1, ri] = jnp.where(upper, up, inner_up)
    for copy in [copies.start(theirs_v, theirs), copies.start(mine_v, mine)]:
        copy.wait()


def join(place, keep, got, pair, far, news):
    chips = len(news) + 1
    _, _, _, half, size = keep.shape
    single = lambda *shape: pltpu.VMEM(shape, jnp.float32)
    return pl.pallas_call(
        functools.partial(join_kernel, chips),
        in_specs=[in_smem] + [in_hbm] * (3 + chips),
        out_specs=[in_hbm] * 2,
        out_shape=[jax.ShapeDtypeStruct(keep.shape, jnp.float32)] * 2,
        scratch_shapes=[
            pltpu.SemaphoreType.DMA((5 + chips,)),
            single(*keep.shape),
            single(*keep.shape),
            single(4, half, size),
            single(chips - 1, half, size),
            single(chips - 1, 2, 2, half, size),
            single(*keep.shape),
            single(*keep.shape),
        ],
        compiler_params=params,
        name="join",
    )(place, keep, got, pair, far, *news)


def inverse_kernel(per, thick, face, lam, out, m_all, f_all, g_all):
    total = f_all.shape[0]
    rows = lam.shape[0]
    classes = out.shape[0]
    shift = lam[...]
    one = jnp.ones_like(shift)
    zero = jnp.zeros_like(shift)

    def step(j, state):
        f, r, phi, s = state
        m = face[j] * r
        f = shift * thick[j] + m * f
        r = 1.0 / (face[j + 1] + f)
        m_all[j] = m
        f_all[j] = f
        i = total - 1 - j
        u = face[i + 1] * s * phi
        phi = shift * thick[i] + u
        s = 1.0 / (face[i] + phi)
        g_all[i] = u
        return f, r, phi, s

    lax.fori_loop(0, total, step, (one, one, zero, zero))

    def centre(j, _):
        g_all[j] = 1.0 / (f_all[j] + g_all[j])
        return 0

    lax.fori_loop(0, total, centre, 0)
    wide = out.shape[2]
    sub = lax.broadcasted_iota(jnp.int32, (ROWS, LANES), 0)
    lane = lax.broadcasted_iota(jnp.int32, (ROWS, wide), 1)
    row = lax.broadcasted_iota(jnp.int32, (ROWS, wide), 0)
    line = lambda ref, j, t: jnp.broadcast_to(ref[j, t:t + 1, :], (ROWS, LANES))

    def put(j, z, sums):
        new = []
        for c in range(classes):
            tiles = z[c * per:(c + 1) * per]
            total_tile = tiles[0]
            for tile in tiles[1:]:
                total_tile = total_tile + tile
            value = jnp.sum(total_tile, axis=1, keepdims=True)
            new.append(jnp.where(lane == j, value, sums[c]))
        return new

    for base in range(0, total, ROWS):
        z = [jnp.zeros((ROWS, LANES), jnp.float32)] * (classes * per)
        sums = [jnp.zeros((ROWS, wide), jnp.float32)] * classes
        for i in range(ROWS - 1, -1, -1):
            j = base + i
            for t in range(classes * per):
                moved = z[t] * line(m_all, j + 1, t) if i < ROWS - 1 else z[t]
                z[t] = jnp.where(sub == i, line(g_all, j, t), moved)
            sums = put(j, z, sums)

        def above(back, state):
            z, sums = state
            for i in range(ROWS):
                j = base - 1 - back * ROWS - i
                z = [z[t] * line(m_all, j + 1, t) for t in range(classes * per)]
                sums = put(j, z, sums)
            return z, sums

        if base:
            z, sums = lax.fori_loop(0, base // ROWS, above, (z, sums))
        for c in range(classes):
            out[c, base:base + ROWS, :] = sums[c] * jnp.where(lane == base + row, 0.5, 1.0)


def inverse_sums(thick, face, lam, per):
    total = thick.shape[0]
    classes = lam.shape[0] // per
    wide = -(-total // LANES) * LANES
    spare = -lam.shape[0] % ROWS
    lam = jnp.pad(lam, ((0, spare), (0, 0)), constant_values=1.0) if spare else lam
    return pl.pallas_call(
        functools.partial(inverse_kernel, per),
        in_specs=[in_smem, in_smem, in_vmem],
        out_shape=jax.ShapeDtypeStruct((classes, total, wide), jnp.float32),
        scratch_shapes=[pltpu.VMEM((total,) + lam.shape, jnp.float32)] * 3,
        compiler_params=params,
        name="inverse_sums",
    )(thick, face, lam)


def interface_kernel(waves, matrices, edges, inverse, out):
    devices, _, wide = edges.shape
    total = wide // 2
    rows = 4 * waves
    lines = []
    for w in range(waves):
        line = edges[w]
        for d in range(1, devices // waves):
            line = line + edges[d * waves + w]
        lines.append(line)
    lines = jnp.concatenate(lines, 0)
    near, far = exact_dot(matrices[0], lines, NN), exact_dot(matrices[1], lines, NN)
    mixed = near[:, :total] + far[:, total:]
    result = jnp.zeros((2 * rows, total), jnp.float32)
    for c in range(inverse.shape[0]):
        part = mixed[c * 2 * rows:(c + 1) * 2 * rows]
        square = inverse[c][:, :total]
        result = result + (exact_dot(part, square, NN) + exact_dot(part, square, NT))
    result = jnp.concatenate([result[:rows], result[rows:]], 1)
    for w in range(waves):
        line = result[4 * w:4 * w + 4]
        for d in range(devices // waves):
            out[d * waves + w] = line


def interface(edges, inverse, waves, size):
    return pl.pallas_call(
        functools.partial(interface_kernel, waves),
        in_specs=[in_vmem] * 3,
        out_specs=in_vmem,
        out_shape=jax.ShapeDtypeStruct(edges.shape, jnp.float32),
        compiler_params=params,
        name="interface",
    )(interface_matrices(waves, size), edges, inverse)


def back_kernel(levels, total, place, thick, values, spread, t, mine, theirs, sines, b, r, m, end, odd_top, odd_rest, even_top, even_rest, out0, out1, sems, values_v, spread_v, t_v, ends, sines_v, b_v, r_v, m_v, end_v, ot, orest, et, er, picked, u_all, q_all, out_v):
    _, _, _, ky, size = b_v.shape
    first = place[0] * levels
    half = size // 2
    many = half // LANES
    core = place[0] % 2
    copies = Copies(sems)
    early = [copies.start(values.at[pl.ds(0, ky)], values_v), copies.start(spread, spread_v)]
    table = copies.start(t, t_v)
    both = []
    for source, start in ((mine, core), (theirs, 1 - core)):
        here = pl.ds(pl.multiple_of(start * (ky // 2), ROWS), ky // 2)
        both.append(copies.start(source, ends.at[:, :, :, here]))
    both.append(copies.start(sines, sines_v))
    rest = [copies.start(source, target) for source, target in ((r, r_v), (m, m_v), (end, end_v), (b, b_v), (odd_top, ot), (odd_rest, orest), (even_top, et), (even_rest, er))]
    for copy in early:
        copy.wait()
    lane = lax.broadcasted_iota(jnp.int32, (ky, 2 * total), 1)
    for f in range(4):
        parts = [part.astype(jnp.float32) for part in split(values_v[:, f, :])]
        for j in range(total):
            spot = (lane == j) | (lane == total + j)
            for p in range(2):
                picked[p, j * ky:(j + 1) * ky, :] = jnp.where(spot, parts[p], 0.0).astype(jnp.bfloat16)
        u_all[f] = (real_dot(picked[0], spread_v[...]) + real_dot(picked[1], spread_v[...])).reshape(total, ky, 2 * LANES)
    table.wait()
    for copy in both:
        copy.wait()

    def source(f, j, here):
        pair = u_all[f, j, here] * thick[j]
        return jnp.concatenate([pair[:, :LANES]] * many + [pair[:, LANES:]] * many, 1)

    def sweep(g, _):
        here = pl.ds(pl.multiple_of(g * ROWS, ROWS), ROWS)

        def from_above(block, y):
            for i in range(levels):
                j = block * levels + i
                step = t_v[j, here]
                y = [step * y[f] + source(f, j, here) for f in range(4)]
            return y

        def from_below(block, y):
            for i in range(levels):
                j = total - 1 - block * levels - i
                step = t_v[j + 1, here]
                y = [step * y[f] + source(f, j, here) for f in range(4)]
            return y

        zero = [jnp.zeros((ROWS, size), jnp.float32)] * 4
        wave = sines_v[...]
        for way, y in (
            (0, lax.fori_loop(0, place[0], from_above, zero)),
            (1, lax.fori_loop(0, total // levels - 1 - place[0], from_below, zero)),
        ):
            for f in range(4):
                ends[f // 2, way, f % 2, here] += wave * y[f]
        return 0

    lax.fori_loop(0, ky // ROWS, sweep, 0)
    for copy in rest:
        copy.wait()
    rows = levels * ky
    lane = lax.broadcasted_iota(jnp.int32, (ky, LANES), 1)
    outs = []
    for f in range(4):
        a, ri = f // 2, f % 2

        def tile(g, _):
            here = pl.ds(pl.multiple_of(g * ROWS, ROWS), ROWS)
            wave = sines_v[...]
            y = ends[a, 0, ri, here]
            ys = []
            for j in range(levels):
                y = b_v[a, ri, j, here] + wave * source(f, first + j, here) + m_v[j, here] * y
                ys.append(y)
            value = (y + end_v[0, here] * ends[a, 1, ri, here]) * end_v[1, here]
            q_all[levels - 1, here] = value
            for j in range(levels - 2, -1, -1):
                value = r_v[j, here] * ys[j] + m_v[j + 1, here] * value
                q_all[j, here] = value
            return 0

        lax.fori_loop(0, ky // ROWS, tile, 0)
        low, high = to_cells(
            q_all[:, :, :half].reshape(rows, half), q_all[:, :, half:].reshape(rows, half), ot, orest, et, er
        )
        for j in range(levels):
            height = thick[first + j] if a else 1.0
            scale = (2.0 / size) * height
            here = slice(j * ky, (j + 1) * ky)
            u = (u_all[f, first + j, :, :LANES] + u_all[f, first + j, :, LANES:]) * (0.5 * height)
            if many > 1:
                out_v[f, j, :, LANES:half] = low[here, LANES:] * scale
            out_v[f, j, :, :LANES] = jnp.where(lane == 0, u, low[here, :LANES] * scale)
            out_v[f, j, :, half:] = high[here] * scale
        outs.append(copies.start(out_v.at[f], (out0, out1)[a].at[ri]))
    for copy in outs:
        copy.wait()


def back(place, thick, values, sines, t, r, m, end, b, mine, theirs):
    _, _, levels, ky, size = b.shape
    total = t.shape[0] - 1
    half = size // 2
    single = lambda *shape: pltpu.VMEM(shape, jnp.float32)
    return pl.pallas_call(
        functools.partial(back_kernel, levels, total),
        in_specs=[in_smem] * 2 + [in_hbm] * 14,
        out_specs=[in_hbm] * 2,
        out_shape=[jax.ShapeDtypeStruct((2, levels, ky, size), jnp.float32)] * 2,
        scratch_shapes=[
            pltpu.SemaphoreType.DMA((18,)),
            single(ky, 4, 2 * total),
            pltpu.VMEM((2 * total, 2 * LANES), jnp.bfloat16),
            single(*t.shape),
            single(2, 2, 2, ky, size),
            single(ROWS, size),
            single(*b.shape),
            single(*r.shape),
            single(*m.shape),
            single(*end.shape),
            *[pltpu.VMEM((half, half), jnp.bfloat16)] * 4,
            pltpu.VMEM((2, total * ky, 2 * total), jnp.bfloat16),
            single(4, total, ky, 2 * LANES),
            single(levels, ky, size),
            single(4, levels, ky, size),
        ],
        compiler_params=params,
        name="back",
    )(place, thick, values, spread_matrix(total), t, mine, theirs, sines, b, r, m, end, *half_sines(size, True))


def shards(rhs, cotangent, thickness, ky_shift):
    waves = lax.axis_size("wave")
    count = lax.axis_size("depth")
    depth_pos = lax.axis_index("depth")
    wave_pos = lax.axis_index("wave")
    _, levels, ky, size = rhs.shape
    full = waves * size
    devices = waves * count
    chips = count // 2
    place = depth_pos.astype(jnp.int32).reshape(1)

    def across(a):
        return lax.ppermute(a, "depth", [(d, d ^ 1) for d in range(count)])

    def along(a, apart):
        return lax.ppermute(a, "depth", [(d, (d + 2 * apart) % count) for d in range(count)])

    def everywhere(a):
        return lax.all_to_all(a, ("depth", "wave"), split_axis=0, concat_axis=0, tiled=True)

    def horizontal(wavenumber, length):
        return (aspect_ratio * 4.0 * np.sin(math.pi * wavenumber / length) ** 2).astype(np.float32)

    inner_face = 2.0 / (thickness[:-1] + thickness[1:])
    face = jnp.concatenate([2.0 / thickness[:1], inner_face, jnp.zeros((1,), jnp.float32)])
    order = wave_order(size)
    sines = np.broadcast_to(np.sin(np.pi * order / size)[None, :], (ROWS, size)).astype(np.float32)
    across_k = horizontal(order, 2 * size)[None, :]
    t, r, m, end, pair, far, b, keep, give, edges = front(
        place, thickness, face, ky_shift, across_k, sines, rhs, cotangent, devices
    )

    classes = waves // 2 + 1
    wavenumber = (np.arange(classes)[:, None] + waves * np.arange(size)[None, :]).reshape(-1, LANES)
    shifts = jnp.pad(ky_shift, (0, devices - ky), constant_values=1.0) if devices > ky else ky_shift
    my_shift = lax.dynamic_slice_in_dim(shifts, depth_pos * waves + wave_pos, 1)

    got = across(give)
    edges = everywhere(edges)
    sums = chip_sums(place, keep, got, pair, chips)
    news = [along(sums[apart - 1], apart) for apart in range(1, chips)]
    inverse = inverse_sums(thickness, face, my_shift + horizontal(wavenumber, full), size // LANES)
    values = interface(edges, inverse, waves, size)
    news, values = lax.optimization_barrier((news, values))
    values = everywhere(values)
    mine, theirs = join(place, keep, got, pair, far, news)
    return back(place, thickness, values, sines, t, r, m, end, b, mine, across(theirs))


def solution(mesh):
    spec = P(None, "depth", None, "wave")
    return jax.shard_map(shards, mesh=mesh, in_specs=(spec, spec, P(), P()), out_specs=(spec, spec), check_vma=False)
```

```python
import functools
import math

import jax
import jax.numpy as jnp
import numpy as np
from jax import lax
from jax.experimental import pallas as pl
from jax.experimental.pallas import tpu as pltpu
from jax.sharding import PartitionSpec as P

aspect_ratio = 1.0
LANES = 128
ROWS = 8
VMEM_BYTES = 60 * 1024 * 1024
real_dot = functools.partial(jnp.dot, preferred_element_type=jnp.float32)
exact_dot = functools.partial(lax.dot_general, precision=lax.Precision.HIGHEST, preferred_element_type=jnp.float32)
NN = (((1,), (0,)), ((), ()))
NT = (((1,), (1,)), ((), ()))
in_smem = pl.BlockSpec(memory_space=pltpu.SMEM)
in_hbm = pl.BlockSpec(memory_space=pl.ANY)
in_vmem = pl.BlockSpec(memory_space=pltpu.VMEM)
params = pltpu.CompilerParams(vmem_limit_bytes=VMEM_BYTES)
brief = pl.CostEstimate(flops=1, bytes_accessed=1, transcendentals=0)
lengthy = pl.CostEstimate(flops=20_000_000_000, bytes_accessed=40_000_000, transcendentals=0)


def wave_order(size):
    return np.concatenate([np.arange(1, size, 2), np.arange(0, size, 2)])


def half_sines(size, back=False):
    half = size // 2
    place = np.arange(half)
    place[0] = half
    parts = []
    for waves in (np.arange(1, size, 2), np.arange(0, size, 2)):
        matrix = np.sin(np.pi * (np.outer(place, waves) % (2 * size)) / size)
        if waves[0] == 0:
            matrix[0] = 0.0
            matrix[:, 0] = 0.0
        matrix = (matrix.T if back else matrix).astype(np.float32)
        top = matrix.astype(jnp.bfloat16)
        parts += [top, (matrix - top.astype(np.float32)).astype(jnp.bfloat16)]
    return parts


def edge_matrix(size, total):
    matrix = np.full((2 * LANES, 2 * total), 2.0 / size, np.float32)
    matrix[LANES:, total:] = -2.0 / size
    return matrix.astype(jnp.bfloat16)


def spread_matrix(total):
    matrix = np.ones((2 * total, 2 * LANES), np.float32)
    matrix[total:, LANES:] = -1.0
    return matrix.astype(jnp.bfloat16)


def interface_matrices(waves, size):
    classes = waves // 2 + 1
    matrix = np.zeros((2, classes, 2, waves, 4, waves, 4))
    for c in range(classes):
        weight = (1.0 if c in (0, waves // 2) else 2.0) / (size * waves)
        for w in range(waves):
            for e in range(2):
                for v in range(waves):
                    for g in range(2):
                        value = weight * math.cos(2.0 * math.pi * (c * (w + e - v - g) % waves) / waves)
                        for f in range(4):
                            matrix[g, c, e, w, f, v, f] = value
    return matrix.reshape(2, classes * 2 * waves * 4, waves * 4).astype(np.float32)


def split(values):
    high = values.astype(jnp.bfloat16)
    return high, (values - high.astype(jnp.float32)).astype(jnp.bfloat16)


def product(values, top, rest):
    high, low = split(values)
    return real_dot(high, top[...]) + (real_dot(low, top[...]) + real_dot(high, rest[...]))


def mirror(values):
    rows = values.shape[0]
    lane = lax.broadcasted_iota(jnp.int32, (rows, LANES), 1)
    back = (LANES - lane) % LANES
    tiles = [values[:, a * LANES:(a + 1) * LANES] for a in range(values.shape[1] // LANES)]
    many = len(tiles)
    out = []
    for a in range(many):
        turned = jnp.take_along_axis(tiles[many - 1 - a], back, axis=1)
        out.append(jnp.where(lane == 0, tiles[(many - a) % many], turned))
    return jnp.concatenate(out, 1) if many > 1 else out[0]


def to_waves(values, odd_top, odd_rest, even_top, even_rest):
    half = values.shape[1] // 2
    low, high = values[:, :half], mirror(values[:, half:])
    lane = lax.broadcasted_iota(jnp.int32, low.shape, 1)
    low = jnp.where(lane == 0, 0.0, low)
    return product(low + high, odd_top, odd_rest), product(low - high, even_top, even_rest)


def to_cells(odd, even, odd_top, odd_rest, even_top, even_rest):
    p, m = product(odd, odd_top, odd_rest), product(even, even_top, even_rest)
    return p + m, mirror(p - m)


class Copies:
    def __init__(self, sems):
        self.sems, self.used = sems, 0

    def start(self, source, target):
        copy = pltpu.make_async_copy(source, target, self.sems.at[self.used])
        self.used += 1
        copy.start()
        return copy


def coefficients(levels, total, group, place, thick, face, shifts, across, t_out, r_out, m_out, end_out, pair_out, far_out, lam, m_chip, r_chip, f_chip, n_chip, u_chip, down_all, up_all):
    ky = lam.shape[0]
    span = 2 * levels
    chips = total // span
    chip = place[0] // 2
    start = chip * span
    upper = place[0] % 2 == 0
    own = (place[0] % 2) * levels
    for row in range(ky):
        lam[row:row + 1, :] = across[...] + shifts[row]

    def down_step(shift, j, f, r):
        m = face[j] * r
        f = shift * thick[j] + m * f
        return m, f, 1.0 / (face[j + 1] + f)

    def up_step(shift, j, phi, s):
        n = face[j + 1] * s
        u = n * phi
        phi = shift * thick[j] + u
        return n, u, phi, 1.0 / (face[j] + phi)

    def part(g, _):
        here = pl.ds(pl.multiple_of(g * group, group), group)
        shift = lam[here]
        one = jnp.ones_like(shift)
        zero = jnp.zeros_like(shift)

        def down_chip(c, state):
            f, r = state
            product = one
            for i in range(span):
                m, f, r = down_step(shift, c * span + i, f, r)
                t_out[c * span + i, here] = m
                product = product * m
            down_all[c] = product
            return f, r

        def up_chip(back, state):
            phi, s = state
            c = chips - 1 - back
            product = one
            for i in range(span - 1, -1, -1):
                n, _, phi, s = up_step(shift, c * span + i, phi, s)
                t_out[c * span + i + 1, here] = n
                product = product * n
            up_all[c] = product
            return phi, s

        f, r = lax.fori_loop(0, chip, down_chip, (one, one))
        for i in range(span):
            m, f, r = down_step(shift, start + i, f, r)
            m_chip[i], f_chip[i], r_chip[i] = m, f, r
        phi, s = lax.fori_loop(0, chips - 1 - chip, up_chip, (zero, zero))
        for i in range(span - 1, -1, -1):
            n, u, phi, s = up_step(shift, start + i, phi, s)
            n_chip[i], u_chip[i] = n, u

        for i in range(levels):
            t_out[start + i, here] = m_chip[i]
            t_out[start + levels + 1 + i, here] = n_chip[levels + i]
        t_out[start + levels, here] = jnp.where(upper, n_chip[levels - 1], m_chip[levels])
        for i in range(levels):
            r_out[i, here] = r_chip[own + i]
            m_out[i, here] = m_chip[own + i]
        last = own + levels - 1
        end_out[0, here] = n_chip[last]
        end_out[1, here] = 1.0 / (f_chip[last] + u_chip[last])
        end_out[2, here] = f_chip[own] + u_chip[own]
        for core in range(2):
            down, up = m_chip[core * levels], n_chip[core * levels]
            for i in range(1, levels):
                down = down * m_chip[core * levels + i]
                up = up * n_chip[core * levels + i]
            pair_out[core, here] = down
            pair_out[2 + core, here] = up
        above, below = [one], [one]
        for apart in range(1, chips - 1):
            above.append(above[-1] * jnp.where(chip >= apart, down_all[jnp.maximum(chip - apart, 0)], one))
            below.append(below[-1] * jnp.where(chip + apart < chips, up_all[jnp.minimum(chip + apart, chips - 1)], one))
        for apart in range(1, chips):
            far_out[apart - 1, here] = jnp.where(chip >= apart, above[apart - 1], below[chips - apart - 1])
        return 0

    lax.fori_loop(0, ky // group, part, 0)


def lane_sum(values):
    tiles = [values[:, t * LANES:(t + 1) * LANES] for t in range(values.shape[1] // LANES)]
    while len(tiles) > 1:
        tiles = [a + b for a, b in zip(tiles[0::2], tiles[1::2])] + tiles[len(tiles) // 2 * 2:]
    return tiles[0]


def front_kernel(levels, total, group, place, thick, face, shifts, across, sines, edge_mix, x0, x1, odd_top, odd_rest, even_top, even_rest, t_out, r_out, m_out, end_out, pair_out, far_out, b_out, keep_out, give_out, edge_out, sems, *scratch):
    across_v, sines_v, mix_v, x, ot, orest, et, er, t, r, m, end, pair, far, b, c_all, z_all, sums, edges, lam, *work = scratch
    _, _, _, ky, size = x.shape
    first = place[0] * levels
    half = size // 2
    copies = Copies(sems)
    early = [copies.start(across, across_v)]
    fields = [copies.start(x0, x.at[0])]
    mats = [copies.start(source, target) for source, target in ((odd_top, ot), (odd_rest, orest), (even_top, et), (even_rest, er))]
    mats += [copies.start(sines, sines_v)]
    fields += [copies.start(x1, x.at[1])]
    late = [copies.start(edge_mix, mix_v)]
    for copy in early:
        copy.wait()
    coefficients(levels, total, group, place, thick, face, shifts, across_v, t, r, m, end, pair, far, lam, *work)
    outs = [copies.start(source, target) for source, target in ((pair, pair_out), (far, far_out))]
    outs += [copies.start(source, target) for source, target in ((t, t_out), (r, r_out), (m, m_out), (end, end_out))]
    for copy in mats:
        copy.wait()
    lane = lax.broadcasted_iota(jnp.int32, (ROWS, LANES), 1)
    spot = jnp.where(lane == 0, size / 4.0, 0.0)
    core = place[0] % 2

    def put(f, rows, values, height, own=None):
        odd, even = lane_sum(values[:, :half]) * height, lane_sum(values[:, half:]) * height
        if own is not None:
            odd, even = odd + own, even + own
        sums[f, 0, rows, :] = odd
        sums[f, 1, rows, :] = even

    for a in range(2):
        fields[a].wait()
        odd, even = to_waves(x[a].reshape(2 * levels * ky, size), ot, orest, et, er)
        for ri in range(2):
            for j in range(levels):
                rows = slice((ri * levels + j) * ky, (ri * levels + j + 1) * ky)
                scale = thick[first + j] if a == 0 else 1.0
                b[a, ri, j, :, :half] = odd[rows] * scale
                b[a, ri, j, :, half:] = even[rows] * scale
        outs.append(copies.start(b.at[a], b_out.at[a]))
        for ri in range(2):
            f = 2 * a + ri

            def tile(g, _):
                here = pl.ds(pl.multiple_of(g * ROWS, ROWS), ROWS)
                wave = sines_v[...]
                y = b[a, ri, 0, here]
                ys = [y]
                for j in range(1, levels):
                    y = b[a, ri, j, here] + m[j, here] * y
                    ys.append(y)
                c_all[a, 0, ri, here] = y
                value = y * end[1, here]
                z_all[1, f, here] = value * wave
                for j in range(levels - 1, -1, -1):
                    if j < levels - 1:
                        value = r[j, here] * ys[j] + m[j + 1, here] * value
                    height = thick[first + j]
                    own = jnp.broadcast_to(x[a, ri, j, here, 0:1], (ROWS, LANES)) * (spot * height if a == 0 else spot)
                    put(f, pl.ds(g * ROWS * total + first + j, ROWS, stride=total), value * wave, height, own)
                z_all[0, f, here] = value * wave
                c_all[a, 1, ri, here] = value * end[2, here]
                return 0

            lax.fori_loop(0, ky // ROWS, tile, 0)
        for start, out in ((core, keep_out), (1 - core, give_out)):
            here = pl.ds(pl.multiple_of(start * (ky // 2), ROWS), ky // 2)
            outs.append(copies.start(c_all.at[a, :, :, here], out.at[a]))

    def reach(g, _):
        here = pl.ds(pl.multiple_of(g * ROWS, ROWS), ROWS)

        def up(block, z):
            for i in range(levels):
                j = first - 1 - block * levels - i
                step = t[j + 1, here]
                z = [step * one for one in z]
                for f in range(4):
                    put(f, pl.ds(g * ROWS * total + j, ROWS, stride=total), z[f], thick[j])
            return z

        def down(block, z):
            for i in range(levels):
                j = first + levels + block * levels + i
                step = t[j, here]
                z = [step * one for one in z]
                for f in range(4):
                    put(f, pl.ds(g * ROWS * total + j, ROWS, stride=total), z[f], thick[j])
            return z

        lax.fori_loop(0, place[0], up, [z_all[0, f, here] for f in range(4)])
        lax.fori_loop(0, total // levels - 1 - place[0], down, [z_all[1, f, here] for f in range(4)])
        return 0

    lax.fori_loop(0, ky // ROWS, reach, 0)
    for copy in late:
        copy.wait()
    if edges.shape[0] > ky:
        edges[...] = jnp.zeros_like(edges)
    wide = 2 * total
    row = lax.broadcasted_iota(jnp.int32, (ky, total, wide), 1)
    column = lax.broadcasted_iota(jnp.int32, (ky, total, wide), 2)
    diagonal = (row == column) | (row + total == column)
    for f in range(4):
        high, low = split(jnp.concatenate([sums[f, 0], sums[f, 1]], 1))
        spread = (real_dot(high, mix_v[...]) + real_dot(low, mix_v[...])).reshape(ky, total, wide)
        edges[:ky, f, :] = jnp.sum(jnp.where(diagonal, spread, 0.0), axis=1)
    outs.append(copies.start(edges, edge_out))
    for copy in outs:
        copy.wait()


def front(place, thick, face, shifts, across, sines, rhs, cotangent, devices):
    _, levels, ky, size = rhs.shape
    total = thick.shape[0]
    chips = total // (2 * levels)
    group = min(2 * ROWS, ky)
    half = size // 2
    wide = 2 * total
    single = lambda *shape: pltpu.VMEM(shape, jnp.float32)
    tables = [(n, ky, size) for n in (total + 1, levels, levels, 3, 4, chips - 1)]
    shapes = tables + [(2, 2, levels, ky, size), (2, 2, 2, ky // 2, size), (2, 2, 2, ky // 2, size), (devices, 4, wide)]
    return pl.pallas_call(
        functools.partial(front_kernel, levels, total, group),
        in_specs=[in_smem] * 4 + [in_hbm] * 9,
        out_specs=[in_hbm] * len(shapes),
        out_shape=[jax.ShapeDtypeStruct(shape, jnp.float32) for shape in shapes],
        scratch_shapes=[
            pltpu.SemaphoreType.DMA((22,)),
            single(1, size),
            single(ROWS, size),
            pltpu.VMEM((2 * LANES, wide), jnp.bfloat16),
            single(2, 2, levels, ky, size),
            *[pltpu.VMEM((half, half), jnp.bfloat16)] * 4,
            *[single(*shape) for shape in tables],
            single(2, 2, levels, ky, size),
            single(2, 2, 2, ky, size),
            single(2, 4, ky, size),
            single(4, 2, ky * total, LANES),
            single(devices, 4, wide),
            single(ky, size),
            *[single(2 * levels, group, size)] * 5,
            *[single(chips, group, size)] * 2,
        ],
        compiler_params=params,
        name="front",
    )(place, thick, face, shifts, across, sines, edge_matrix(size, total), rhs, cotangent, *half_sines(size))


def chip_kernel(chips, place, keep, got, pair, *refs):
    outs = refs[:chips - 1]
    sems, keep_v, got_v, pair_v, down_v, up_v = refs[chips - 1:]
    copies = Copies(sems)
    chip = place[0] // 2
    upper = place[0] % 2 == 0
    half = keep_v.shape[3]
    here = pl.ds(pl.multiple_of((place[0] % 2) * half, ROWS), half)
    for copy in [copies.start(keep, keep_v), copies.start(got, got_v), copies.start(pair.at[:, here], pair_v)]:
        copy.wait()
    for a in range(2):
        first, second = jnp.where(upper, keep_v[a], got_v[a]), jnp.where(upper, got_v[a], keep_v[a])
        down_v[a] = second[0] + pair_v[1] * first[0]
        up_v[a] = first[1] + pair_v[2] * second[1]
    for apart in range(1, chips):
        goes_down = chip + apart < chips
        sem = sems.at[2 + apart]

        @pl.when(goes_down)
        def _():
            pltpu.make_async_copy(down_v, outs[apart - 1], sem).start()

        @pl.when(jnp.logical_not(goes_down))
        def _():
            pltpu.make_async_copy(up_v, outs[apart - 1], sem).start()

    for apart in range(1, chips):
        pltpu.make_async_copy(down_v, outs[apart - 1], sems.at[2 + apart]).wait()


def chip_sums(place, keep, got, pair, chips):
    _, _, _, half, size = keep.shape
    single = lambda *shape: pltpu.VMEM(shape, jnp.float32)
    shape = (2, 2, half, size)
    return pl.pallas_call(
        functools.partial(chip_kernel, chips),
        in_specs=[in_smem] + [in_hbm] * 3,
        out_specs=[in_hbm] * (chips - 1),
        out_shape=[jax.ShapeDtypeStruct(shape, jnp.float32)] * (chips - 1),
        scratch_shapes=[
            pltpu.SemaphoreType.DMA((2 + chips,)),
            single(*keep.shape),
            single(*keep.shape),
            single(4, half, size),
            single(*shape),
            single(*shape),
        ],
        compiler_params=params,
        cost_estimate=brief,
        name="chip_sums",
    )(place, keep, got, pair)


def join_kernel(chips, place, keep, got, pair, far, *refs):
    news = refs[:chips - 1]
    mine, theirs, sems, keep_v, got_v, pair_v, far_v, news_v, mine_v, theirs_v = refs[chips - 1:]
    copies = Copies(sems)
    chip = place[0] // 2
    upper = place[0] % 2 == 0
    half = keep_v.shape[3]
    here = pl.ds(pl.multiple_of((place[0] % 2) * half, ROWS), half)
    ready = [copies.start(keep, keep_v), copies.start(got, got_v), copies.start(pair.at[:, here], pair_v), copies.start(far.at[:, here], far_v)]
    ready += [copies.start(news[i], news_v.at[i]) for i in range(chips - 1)]
    for copy in ready:
        copy.wait()
    for a in range(2):
        for ri in range(2):
            first, second = (keep_v, got_v), (got_v, keep_v)
            pick = lambda refs, way: jnp.where(upper, refs[0][a, way, ri], refs[1][a, way, ri])
            down = jnp.zeros((half, keep_v.shape[4]), jnp.float32)
            up = down
            for apart in range(1, chips):
                term = far_v[apart - 1] * news_v[apart - 1, a, ri]
                down = down + jnp.where(chip >= apart, term, 0.0)
                up = up + jnp.where(chip >= apart, 0.0, term)
            inner_up = pick(second, 1) + pair_v[3] * up
            inner_down = pick(first, 0) + pair_v[0] * down
            mine_v[a, 0, ri] = jnp.where(upper, down, inner_down)
            mine_v[a, 1, ri] = jnp.where(upper, inner_up, up)
            theirs_v[a, 0, ri] = jnp.where(upper, inner_down, down)
            theirs_v[a, 1, ri] = jnp.where(upper, up, inner_up)
    for copy in [copies.start(theirs_v, theirs), copies.start(mine_v, mine)]:
        copy.wait()


def join(place, keep, got, pair, far, news):
    chips = len(news) + 1
    _, _, _, half, size = keep.shape
    single = lambda *shape: pltpu.VMEM(shape, jnp.float32)
    return pl.pallas_call(
        functools.partial(join_kernel, chips),
        in_specs=[in_smem] + [in_hbm] * (3 + chips),
        out_specs=[in_hbm] * 2,
        out_shape=[jax.ShapeDtypeStruct(keep.shape, jnp.float32)] * 2,
        scratch_shapes=[
            pltpu.SemaphoreType.DMA((5 + chips,)),
            single(*keep.shape),
            single(*keep.shape),
            single(4, half, size),
            single(chips - 1, half, size),
            single(chips - 1, 2, 2, half, size),
            single(*keep.shape),
            single(*keep.shape),
        ],
        compiler_params=params,
        cost_estimate=lengthy,
        name="join",
    )(place, keep, got, pair, far, *news)


def inverse_kernel(per, thick, face, lam, out, m_all, f_all, g_all):
    total = f_all.shape[0]
    rows = lam.shape[0]
    classes = out.shape[0]
    shift = lam[...]
    one = jnp.ones_like(shift)
    zero = jnp.zeros_like(shift)

    def step(j, state):
        f, r, phi, s = state
        m = face[j] * r
        f = shift * thick[j] + m * f
        r = 1.0 / (face[j + 1] + f)
        m_all[j] = m
        f_all[j] = f
        i = total - 1 - j
        u = face[i + 1] * s * phi
        phi = shift * thick[i] + u
        s = 1.0 / (face[i] + phi)
        g_all[i] = u
        return f, r, phi, s

    lax.fori_loop(0, total, step, (one, one, zero, zero))

    def centre(j, _):
        g_all[j] = 1.0 / (f_all[j] + g_all[j])
        return 0

    lax.fori_loop(0, total, centre, 0)
    wide = out.shape[2]
    sub = lax.broadcasted_iota(jnp.int32, (ROWS, LANES), 0)
    lane = lax.broadcasted_iota(jnp.int32, (ROWS, wide), 1)
    row = lax.broadcasted_iota(jnp.int32, (ROWS, wide), 0)
    line = lambda ref, j, t: jnp.broadcast_to(ref[j, t:t + 1, :], (ROWS, LANES))

    def put(j, z, sums):
        new = []
        for c in range(classes):
            tiles = z[c * per:(c + 1) * per]
            total_tile = tiles[0]
            for tile in tiles[1:]:
                total_tile = total_tile + tile
            value = jnp.sum(total_tile, axis=1, keepdims=True)
            new.append(jnp.where(lane == j, value, sums[c]))
        return new

    for base in range(0, total, ROWS):
        z = [jnp.zeros((ROWS, LANES), jnp.float32)] * (classes * per)
        sums = [jnp.zeros((ROWS, wide), jnp.float32)] * classes
        for i in range(ROWS - 1, -1, -1):
            j = base + i
            for t in range(classes * per):
                moved = z[t] * line(m_all, j + 1, t) if i < ROWS - 1 else z[t]
                z[t] = jnp.where(sub == i, line(g_all, j, t), moved)
            sums = put(j, z, sums)

        def above(back, state):
            z, sums = state
            for i in range(ROWS):
                j = base - 1 - back * ROWS - i
                z = [z[t] * line(m_all, j + 1, t) for t in range(classes * per)]
                sums = put(j, z, sums)
            return z, sums

        if base:
            z, sums = lax.fori_loop(0, base // ROWS, above, (z, sums))
        for c in range(classes):
            out[c, base:base + ROWS, :] = sums[c] * jnp.where(lane == base + row, 0.5, 1.0)


def inverse_sums(thick, face, lam, per):
    total = thick.shape[0]
    classes = lam.shape[0] // per
    wide = -(-total // LANES) * LANES
    spare = -lam.shape[0] % ROWS
    lam = jnp.pad(lam, ((0, spare), (0, 0)), constant_values=1.0) if spare else lam
    return pl.pallas_call(
        functools.partial(inverse_kernel, per),
        in_specs=[in_smem, in_smem, in_vmem],
        out_shape=jax.ShapeDtypeStruct((classes, total, wide), jnp.float32),
        scratch_shapes=[pltpu.VMEM((total,) + lam.shape, jnp.float32)] * 3,
        compiler_params=params,
        cost_estimate=lengthy,
        name="inverse_sums",
    )(thick, face, lam)


def interface_kernel(waves, matrices, edges, inverse, out):
    devices, _, wide = edges.shape
    total = wide // 2
    rows = 4 * waves
    lines = []
    for w in range(waves):
        line = edges[w]
        for d in range(1, devices // waves):
            line = line + edges[d * waves + w]
        lines.append(line)
    lines = jnp.concatenate(lines, 0)
    near, far = exact_dot(matrices[0], lines, NN), exact_dot(matrices[1], lines, NN)
    mixed = near[:, :total] + far[:, total:]
    result = jnp.zeros((2 * rows, total), jnp.float32)
    for c in range(inverse.shape[0]):
        part = mixed[c * 2 * rows:(c + 1) * 2 * rows]
        square = inverse[c][:, :total]
        result = result + (exact_dot(part, square, NN) + exact_dot(part, square, NT))
    result = jnp.concatenate([result[:rows], result[rows:]], 1)
    for w in range(waves):
        line = result[4 * w:4 * w + 4]
        for d in range(devices // waves):
            out[d * waves + w] = line


def interface(edges, inverse, waves, size):
    return pl.pallas_call(
        functools.partial(interface_kernel, waves),
        in_specs=[in_vmem] * 3,
        out_specs=in_vmem,
        out_shape=jax.ShapeDtypeStruct(edges.shape, jnp.float32),
        compiler_params=params,
        name="interface",
    )(interface_matrices(waves, size), edges, inverse)


def back_kernel(levels, total, place, thick, values, spread, t, mine, theirs, sines, b, r, m, end, odd_top, odd_rest, even_top, even_rest, out0, out1, sems, values_v, spread_v, t_v, ends, sines_v, b_v, r_v, m_v, end_v, ot, orest, et, er, picked, u_all, q_all, out_v):
    _, _, _, ky, size = b_v.shape
    first = place[0] * levels
    half = size // 2
    many = half // LANES
    core = place[0] % 2
    copies = Copies(sems)
    early = [copies.start(values.at[pl.ds(0, ky)], values_v), copies.start(spread, spread_v)]
    table = copies.start(t, t_v)
    both = []
    for source, start in ((mine, core), (theirs, 1 - core)):
        here = pl.ds(pl.multiple_of(start * (ky // 2), ROWS), ky // 2)
        both.append(copies.start(source, ends.at[:, :, :, here]))
    both.append(copies.start(sines, sines_v))
    rest = [copies.start(source, target) for source, target in ((r, r_v), (m, m_v), (end, end_v), (b, b_v), (odd_top, ot), (odd_rest, orest), (even_top, et), (even_rest, er))]
    for copy in early:
        copy.wait()
    lane = lax.broadcasted_iota(jnp.int32, (ky, 2 * total), 1)
    for f in range(4):
        parts = [part.astype(jnp.float32) for part in split(values_v[:, f, :])]
        for j in range(total):
            spot = (lane == j) | (lane == total + j)
            for p in range(2):
                picked[p, j * ky:(j + 1) * ky, :] = jnp.where(spot, parts[p], 0.0).astype(jnp.bfloat16)
        u_all[f] = (real_dot(picked[0], spread_v[...]) + real_dot(picked[1], spread_v[...])).reshape(total, ky, 2 * LANES)
    table.wait()
    for copy in both:
        copy.wait()

    def source(f, j, here):
        pair = u_all[f, j, here] * thick[j]
        return jnp.concatenate([pair[:, :LANES]] * many + [pair[:, LANES:]] * many, 1)

    def sweep(g, _):
        here = pl.ds(pl.multiple_of(g * ROWS, ROWS), ROWS)

        def from_above(block, y):
            for i in range(levels):
                j = block * levels + i
                step = t_v[j, here]
                y = [step * y[f] + source(f, j, here) for f in range(4)]
            return y

        def from_below(block, y):
            for i in range(levels):
                j = total - 1 - block * levels - i
                step = t_v[j + 1, here]
                y = [step * y[f] + source(f, j, here) for f in range(4)]
            return y

        zero = [jnp.zeros((ROWS, size), jnp.float32)] * 4
        wave = sines_v[...]
        for way, y in (
            (0, lax.fori_loop(0, place[0], from_above, zero)),
            (1, lax.fori_loop(0, total // levels - 1 - place[0], from_below, zero)),
        ):
            for f in range(4):
                ends[f // 2, way, f % 2, here] += wave * y[f]
        return 0

    lax.fori_loop(0, ky // ROWS, sweep, 0)
    for copy in rest:
        copy.wait()
    rows = levels * ky
    lane = lax.broadcasted_iota(jnp.int32, (ky, LANES), 1)
    outs = []
    for f in range(4):
        a, ri = f // 2, f % 2

        def tile(g, _):
            here = pl.ds(pl.multiple_of(g * ROWS, ROWS), ROWS)
            wave = sines_v[...]
            y = ends[a, 0, ri, here]
            ys = []
            for j in range(levels):
                y = b_v[a, ri, j, here] + wave * source(f, first + j, here) + m_v[j, here] * y
                ys.append(y)
            value = (y + end_v[0, here] * ends[a, 1, ri, here]) * end_v[1, here]
            q_all[levels - 1, here] = value
            for j in range(levels - 2, -1, -1):
                value = r_v[j, here] * ys[j] + m_v[j + 1, here] * value
                q_all[j, here] = value
            return 0

        lax.fori_loop(0, ky // ROWS, tile, 0)
        low, high = to_cells(
            q_all[:, :, :half].reshape(rows, half), q_all[:, :, half:].reshape(rows, half), ot, orest, et, er
        )
        for j in range(levels):
            height = thick[first + j] if a else 1.0
            scale = (2.0 / size) * height
            here = slice(j * ky, (j + 1) * ky)
            u = (u_all[f, first + j, :, :LANES] + u_all[f, first + j, :, LANES:]) * (0.5 * height)
            if many > 1:
                out_v[f, j, :, LANES:half] = low[here, LANES:] * scale
            out_v[f, j, :, :LANES] = jnp.where(lane == 0, u, low[here, :LANES] * scale)
            out_v[f, j, :, half:] = high[here] * scale
        outs.append(copies.start(out_v.at[f], (out0, out1)[a].at[ri]))
    for copy in outs:
        copy.wait()


def back(place, thick, values, sines, t, r, m, end, b, mine, theirs):
    _, _, levels, ky, size = b.shape
    total = t.shape[0] - 1
    half = size // 2
    single = lambda *shape: pltpu.VMEM(shape, jnp.float32)
    return pl.pallas_call(
        functools.partial(back_kernel, levels, total),
        in_specs=[in_smem] * 2 + [in_hbm] * 14,
        out_specs=[in_hbm] * 2,
        out_shape=[jax.ShapeDtypeStruct((2, levels, ky, size), jnp.float32)] * 2,
        scratch_shapes=[
            pltpu.SemaphoreType.DMA((18,)),
            single(ky, 4, 2 * total),
            pltpu.VMEM((2 * total, 2 * LANES), jnp.bfloat16),
            single(*t.shape),
            single(2, 2, 2, ky, size),
            single(ROWS, size),
            single(*b.shape),
            single(*r.shape),
            single(*m.shape),
            single(*end.shape),
            *[pltpu.VMEM((half, half), jnp.bfloat16)] * 4,
            pltpu.VMEM((2, total * ky, 2 * total), jnp.bfloat16),
            single(4, total, ky, 2 * LANES),
            single(levels, ky, size),
            single(4, levels, ky, size),
        ],
        compiler_params=params,
        name="back",
    )(place, thick, values, spread_matrix(total), t, mine, theirs, sines, b, r, m, end, *half_sines(size, True))


def shards(rhs, cotangent, thickness, ky_shift):
    waves = lax.axis_size("wave")
    count = lax.axis_size("depth")
    depth_pos = lax.axis_index("depth")
    wave_pos = lax.axis_index("wave")
    _, levels, ky, size = rhs.shape
    full = waves * size
    devices = waves * count
    chips = count // 2
    place = depth_pos.astype(jnp.int32).reshape(1)

    def across(a):
        return lax.ppermute(a, "depth", [(d, d ^ 1) for d in range(count)])

    def along(a, apart):
        return lax.ppermute(a, "depth", [(d, (d + 2 * apart) % count) for d in range(count)])

    def everywhere(a):
        return lax.all_to_all(a, ("depth", "wave"), split_axis=0, concat_axis=0, tiled=True)

    def horizontal(wavenumber, length):
        return (aspect_ratio * 4.0 * np.sin(math.pi * wavenumber / length) ** 2).astype(np.float32)

    inner_face = 2.0 / (thickness[:-1] + thickness[1:])
    face = jnp.concatenate([2.0 / thickness[:1], inner_face, jnp.zeros((1,), jnp.float32)])
    order = wave_order(size)
    sines = np.broadcast_to(np.sin(np.pi * order / size)[None, :], (ROWS, size)).astype(np.float32)
    across_k = horizontal(order, 2 * size)[None, :]
    t, r, m, end, pair, far, b, keep, give, edges = front(
        place, thickness, face, ky_shift, across_k, sines, rhs, cotangent, devices
    )

    classes = waves // 2 + 1
    wavenumber = (np.arange(classes)[:, None] + waves * np.arange(size)[None, :]).reshape(-1, LANES)
    shifts = jnp.pad(ky_shift, (0, devices - ky), constant_values=1.0) if devices > ky else ky_shift
    my_shift = lax.dynamic_slice_in_dim(shifts, depth_pos * waves + wave_pos, 1)

    got = across(give)
    edges = everywhere(edges)
    sums = chip_sums(place, keep, got, pair, chips)
    news = [along(sums[apart - 1], apart) for apart in range(1, chips)]
    inverse = inverse_sums(thickness, face, my_shift + horizontal(wavenumber, full), size // LANES)
    values = interface(edges, inverse, waves, size)
    values = everywhere(values)
    news, _ = lax.optimization_barrier((news, values))
    mine, theirs = join(place, keep, got, pair, far, news)
    return back(place, thickness, values, sines, t, r, m, end, b, mine, across(theirs))


def solution(mesh):
    spec = P(None, "depth", None, "wave")
    return jax.shard_map(shards, mesh=mesh, in_specs=(spec, spec, P(), P()), out_specs=(spec, spec), check_vma=False)
```

```python
import functools
import math

import jax
import jax.numpy as jnp
import numpy as np
from jax import lax
from jax.experimental import pallas as pl
from jax.experimental.pallas import tpu as pltpu
from jax.sharding import PartitionSpec as P

aspect_ratio = 1.0
LANES = 128
ROWS = 8
VMEM_BYTES = 60 * 1024 * 1024
real_dot = functools.partial(jnp.dot, preferred_element_type=jnp.float32)
exact_dot = functools.partial(lax.dot_general, precision=lax.Precision.HIGHEST, preferred_element_type=jnp.float32)
NN = (((1,), (0,)), ((), ()))
NT = (((1,), (1,)), ((), ()))
in_smem = pl.BlockSpec(memory_space=pltpu.SMEM)
in_hbm = pl.BlockSpec(memory_space=pl.ANY)
in_vmem = pl.BlockSpec(memory_space=pltpu.VMEM)
params = pltpu.CompilerParams(vmem_limit_bytes=VMEM_BYTES)
brief = pl.CostEstimate(flops=1, bytes_accessed=1, transcendentals=0)
lengthy = pl.CostEstimate(flops=20_000_000_000, bytes_accessed=40_000_000, transcendentals=0)


def wave_order(size):
    return np.concatenate([np.arange(1, size, 2), np.arange(0, size, 2)])


def half_sines(size, back=False):
    half = size // 2
    place = np.arange(half)
    place[0] = half
    parts = []
    for waves in (np.arange(1, size, 2), np.arange(0, size, 2)):
        matrix = np.sin(np.pi * (np.outer(place, waves) % (2 * size)) / size)
        if waves[0] == 0:
            matrix[0] = 0.0
            matrix[:, 0] = 0.0
        matrix = (matrix.T if back else matrix).astype(np.float32)
        top = matrix.astype(jnp.bfloat16)
        parts += [top, (matrix - top.astype(np.float32)).astype(jnp.bfloat16)]
    return parts


def edge_matrix(size, total):
    matrix = np.full((2 * LANES, 2 * total), 2.0 / size, np.float32)
    matrix[LANES:, total:] = -2.0 / size
    return matrix.astype(jnp.bfloat16)


def spread_matrix(total):
    matrix = np.ones((2 * total, 2 * LANES), np.float32)
    matrix[total:, LANES:] = -1.0
    return matrix.astype(jnp.bfloat16)


def interface_matrices(waves, size):
    classes = waves // 2 + 1
    matrix = np.zeros((2, classes, 2, waves, 4, waves, 4))
    for c in range(classes):
        weight = (1.0 if c in (0, waves // 2) else 2.0) / (size * waves)
        for w in range(waves):
            for e in range(2):
                for v in range(waves):
                    for g in range(2):
                        value = weight * math.cos(2.0 * math.pi * (c * (w + e - v - g) % waves) / waves)
                        for f in range(4):
                            matrix[g, c, e, w, f, v, f] = value
    return matrix.reshape(2, classes * 2 * waves * 4, waves * 4).astype(np.float32)


def split(values):
    high = values.astype(jnp.bfloat16)
    return high, (values - high.astype(jnp.float32)).astype(jnp.bfloat16)


def product(values, top, rest):
    high, low = split(values)
    return real_dot(high, top[...]) + (real_dot(low, top[...]) + real_dot(high, rest[...]))


def mirror(values):
    rows = values.shape[0]
    lane = lax.broadcasted_iota(jnp.int32, (rows, LANES), 1)
    back = (LANES - lane) % LANES
    tiles = [values[:, a * LANES:(a + 1) * LANES] for a in range(values.shape[1] // LANES)]
    many = len(tiles)
    out = []
    for a in range(many):
        turned = jnp.take_along_axis(tiles[many - 1 - a], back, axis=1)
        out.append(jnp.where(lane == 0, tiles[(many - a) % many], turned))
    return jnp.concatenate(out, 1) if many > 1 else out[0]


def to_waves(values, odd_top, odd_rest, even_top, even_rest):
    half = values.shape[1] // 2
    low, high = values[:, :half], mirror(values[:, half:])
    lane = lax.broadcasted_iota(jnp.int32, low.shape, 1)
    low = jnp.where(lane == 0, 0.0, low)
    return product(low + high, odd_top, odd_rest), product(low - high, even_top, even_rest)


def to_cells(odd, even, odd_top, odd_rest, even_top, even_rest):
    p, m = product(odd, odd_top, odd_rest), product(even, even_top, even_rest)
    return p + m, mirror(p - m)


def horizontal(wavenumber, length):
    return (aspect_ratio * 4.0 * np.sin(math.pi * wavenumber / length) ** 2).astype(np.float32)


def set_faces(thick, faces):
    total = faces.shape[0] - 1
    two = jnp.full((ROWS, LANES), 2.0, jnp.float32)
    faces[0] = two / (two * 0.0 + thick[0])
    faces[total] = two * 0.0

    def one(j, _):
        faces[j] = two / (two * 0.0 + (thick[j - 1] + thick[j]))
        return 0

    lax.fori_loop(1, total, one, 0, unroll=3)


def spread_face(tile, like):
    rows, lanes = like.shape
    wide = jnp.concatenate([tile] * (lanes // LANES), 1) if lanes > LANES else tile
    return jnp.concatenate([wide] * (rows // ROWS), 0) if rows > ROWS else wide


class Copies:
    def __init__(self, sems):
        self.sems, self.used = sems, 0

    def start(self, source, target):
        copy = pltpu.make_async_copy(source, target, self.sems.at[self.used])
        self.used += 1
        copy.start()
        return copy


def coefficients(levels, total, group, place, thick, faces, shifts, across, t_out, m_out, end_out, pair_out, far_out, lam, m_chip, f_chip, n_chip, u_chip, down_all, up_all):
    ky = lam.shape[0]
    span = 2 * levels
    chips = total // span
    chip = place[0] // 2
    start = chip * span
    upper = place[0] % 2 == 0
    own = (place[0] % 2) * levels
    for row in range(ky):
        lam[row:row + 1, :] = across[...] + shifts[row]

    def down_step(shift, j, f, r):
        m = spread_face(faces[j], r) * r
        f = shift * thick[j] + m * f
        return m, f, 1.0 / (spread_face(faces[j + 1], f) + f)

    def up_step(shift, j, phi, s):
        n = spread_face(faces[j + 1], s) * s
        u = n * phi
        phi = shift * thick[j] + u
        return n, u, phi, 1.0 / (spread_face(faces[j], phi) + phi)

    def part(g, _):
        here = pl.ds(pl.multiple_of(g * group, group), group)
        shift = lam[here]
        one = jnp.ones_like(shift)
        zero = jnp.zeros_like(shift)

        def down_chip(c, state):
            f, r = state
            product = one
            for i in range(span):
                m, f, r = down_step(shift, c * span + i, f, r)
                t_out[c * span + i, here] = m
                product = product * m
            down_all[c] = product
            return f, r

        def up_chip(back, state):
            phi, s = state
            c = chips - 1 - back
            product = one
            for i in range(span - 1, -1, -1):
                n, _, phi, s = up_step(shift, c * span + i, phi, s)
                t_out[c * span + i + 1, here] = n
                product = product * n
            up_all[c] = product
            return phi, s

        f, r = lax.fori_loop(0, chip, down_chip, (one, one))
        for i in range(span):
            m, f, r = down_step(shift, start + i, f, r)
            m_chip[i], f_chip[i] = m, f
        phi, s = lax.fori_loop(0, chips - 1 - chip, up_chip, (zero, zero))
        for i in range(span - 1, -1, -1):
            n, u, phi, s = up_step(shift, start + i, phi, s)
            n_chip[i], u_chip[i] = n, u

        for i in range(levels):
            t_out[start + i, here] = m_chip[i]
            t_out[start + levels + 1 + i, here] = n_chip[levels + i]
        t_out[start + levels, here] = jnp.where(upper, n_chip[levels - 1], m_chip[levels])
        for i in range(levels):
            m_out[i, here] = m_chip[own + i]
        last = own + levels - 1
        end_out[0, here] = n_chip[last]
        end_out[1, here] = 1.0 / (f_chip[last] + u_chip[last])
        end_out[2, here] = f_chip[own] + u_chip[own]
        for core in range(2):
            down, up = m_chip[core * levels], n_chip[core * levels]
            for i in range(1, levels):
                down = down * m_chip[core * levels + i]
                up = up * n_chip[core * levels + i]
            pair_out[core, here] = down
            pair_out[2 + core, here] = up
        above, below = [one], [one]
        for apart in range(1, chips - 1):
            above.append(above[-1] * jnp.where(chip >= apart, down_all[jnp.maximum(chip - apart, 0)], one))
            below.append(below[-1] * jnp.where(chip + apart < chips, up_all[jnp.minimum(chip + apart, chips - 1)], one))
        for apart in range(1, chips):
            far_out[apart - 1, here] = jnp.where(chip >= apart, above[apart - 1], below[chips - apart - 1])
        return 0

    lax.fori_loop(0, ky // group, part, 0)


def lane_sum(values):
    tiles = [values[:, t * LANES:(t + 1) * LANES] for t in range(values.shape[1] // LANES)]
    while len(tiles) > 1:
        tiles = [a + b for a, b in zip(tiles[0::2], tiles[1::2])] + tiles[len(tiles) // 2 * 2:]
    return tiles[0]


def front_kernel(levels, total, group, place, thick, shifts, across, sines, edge_mix, x0, x1, odd_top, odd_rest, even_top, even_rest, t_out, m_out, end_out, pair_out, far_out, b_out, keep_out, give_out, edge_out, sems, *scratch):
    across_v, sines_v, mix_v, x, ot, orest, et, er, t, m, end, pair, far, b, c_all, z_all, sums, edges, faces, lam, *work = scratch
    _, _, _, ky, size = x.shape
    first = place[0] * levels
    half = size // 2
    copies = Copies(sems)
    early = [copies.start(across, across_v)]
    fields = [copies.start(x0, x.at[0])]
    mats = [copies.start(source, target) for source, target in ((odd_top, ot), (odd_rest, orest), (even_top, et), (even_rest, er))]
    mats += [copies.start(sines, sines_v)]
    fields += [copies.start(x1, x.at[1])]
    late = [copies.start(edge_mix, mix_v)]
    set_faces(thick, faces)
    for copy in early:
        copy.wait()
    coefficients(levels, total, group, place, thick, faces, shifts, across_v, t, m, end, pair, far, lam, *work)
    outs = [copies.start(source, target) for source, target in ((pair, pair_out), (far, far_out))]
    outs += [copies.start(source, target) for source, target in ((t, t_out), (m, m_out), (end, end_out))]
    for copy in mats:
        copy.wait()
    lane = lax.broadcasted_iota(jnp.int32, (ROWS, LANES), 1)
    spot = jnp.where(lane == 0, size / 4.0, 0.0)
    core = place[0] % 2

    def put(f, j, here, values, height, own=None):
        odd, even = lane_sum(values[:, :half]) * height, lane_sum(values[:, half:]) * height
        if own is not None:
            odd, even = odd + own, even + own
        sums[f, 0, j, here] = odd
        sums[f, 1, j, here] = even

    for a in range(2):
        fields[a].wait()
        odd, even = to_waves(x[a].reshape(2 * levels * ky, size), ot, orest, et, er)
        for ri in range(2):
            for j in range(levels):
                rows = slice((ri * levels + j) * ky, (ri * levels + j + 1) * ky)
                scale = thick[first + j] if a == 0 else 1.0
                b[a, ri, j, :, :half] = odd[rows] * scale
                b[a, ri, j, :, half:] = even[rows] * scale
        outs.append(copies.start(b.at[a], b_out.at[a]))
        for ri in range(2):
            f = 2 * a + ri

            def tile(g, _):
                here = pl.ds(pl.multiple_of(g * ROWS, ROWS), ROWS)
                wave = sines_v[...]
                y = b[a, ri, 0, here]
                ys = [y]
                for j in range(1, levels):
                    y = b[a, ri, j, here] + m[j, here] * y
                    ys.append(y)
                c_all[a, 0, ri, here] = y
                value = y * end[1, here]
                z_all[1, f, here] = value * wave
                for j in range(levels - 1, -1, -1):
                    if j < levels - 1:
                        value = m[j + 1, here] * (ys[j] * (0.5 * (thick[first + j] + thick[first + j + 1])) + value)
                    height = thick[first + j]
                    own = jnp.broadcast_to(x[a, ri, j, here, 0:1], (ROWS, LANES)) * (spot * height if a == 0 else spot)
                    put(f, first + j, here, value * wave, height, own)
                z_all[0, f, here] = value * wave
                c_all[a, 1, ri, here] = value * end[2, here]
                return 0

            lax.fori_loop(0, ky // ROWS, tile, 0)
        for start, out in ((core, keep_out), (1 - core, give_out)):
            here = pl.ds(pl.multiple_of(start * (ky // 2), ROWS), ky // 2)
            outs.append(copies.start(c_all.at[a, :, :, here], out.at[a]))

    def reach(g, _):
        here = pl.ds(pl.multiple_of(g * ROWS, ROWS), ROWS)

        def up(block, z):
            for i in range(levels):
                j = first - 1 - block * levels - i
                step = t[j + 1, here]
                z = [step * one for one in z]
                for f in range(4):
                    put(f, j, here, z[f], thick[j])
            return z

        def down(block, z):
            for i in range(levels):
                j = first + levels + block * levels + i
                step = t[j, here]
                z = [step * one for one in z]
                for f in range(4):
                    put(f, j, here, z[f], thick[j])
            return z

        lax.fori_loop(0, place[0], up, [z_all[0, f, here] for f in range(4)])
        lax.fori_loop(0, total // levels - 1 - place[0], down, [z_all[1, f, here] for f in range(4)])
        return 0

    lax.fori_loop(0, ky // ROWS, reach, 0)
    for copy in late:
        copy.wait()
    if edges.shape[0] > ky:
        edges[...] = jnp.zeros_like(edges)
    wide = 2 * total
    lane = lax.broadcasted_iota(jnp.int32, (ky, wide), 1) % total
    for f in range(4):
        both = [sums[f, way].reshape(total * ky, LANES) for way in range(2)]
        high, low = split(jnp.concatenate(both, 1))
        spread = (real_dot(high, mix_v[...]) + real_dot(low, mix_v[...])).reshape(total, ky, wide)
        line = spread[0]
        for j in range(1, total):
            line = jnp.where(lane == j, spread[j], line)
        edges[:ky, f, :] = line
    outs.append(copies.start(edges, edge_out))
    for copy in outs:
        copy.wait()


def front(place, thick, shifts, across, sines, rhs, cotangent, devices):
    _, levels, ky, size = rhs.shape
    total = thick.shape[0]
    chips = total // (2 * levels)
    group = min(2 * ROWS, ky)
    half = size // 2
    wide = 2 * total
    single = lambda *shape: pltpu.VMEM(shape, jnp.float32)
    tables = [(n, ky, size) for n in (total + 1, levels, 3, 4, chips - 1)]
    shapes = tables + [(2, 2, levels, ky, size), (2, 2, 2, ky // 2, size), (2, 2, 2, ky // 2, size), (devices, 4, wide)]
    return pl.pallas_call(
        functools.partial(front_kernel, levels, total, group),
        in_specs=[in_smem] * 3 + [in_hbm] * 9,
        out_specs=[in_hbm] * len(shapes),
        out_shape=[jax.ShapeDtypeStruct(shape, jnp.float32) for shape in shapes],
        scratch_shapes=[
            pltpu.SemaphoreType.DMA((22,)),
            single(1, size),
            single(ROWS, size),
            pltpu.VMEM((2 * LANES, wide), jnp.bfloat16),
            single(2, 2, levels, ky, size),
            *[pltpu.VMEM((half, half), jnp.bfloat16)] * 4,
            *[single(*shape) for shape in tables],
            single(2, 2, levels, ky, size),
            single(2, 2, 2, ky, size),
            single(2, 4, ky, size),
            single(4, 2, total, ky, LANES),
            single(devices, 4, wide),
            single(total + 1, ROWS, LANES),
            single(ky, size),
            *[single(2 * levels, group, size)] * 4,
            *[single(chips, group, size)] * 2,
        ],
        compiler_params=params,
        name="front",
    )(place, thick, shifts, across, sines, edge_matrix(size, total), rhs, cotangent, *half_sines(size))


def chip_kernel(chips, place, keep, got, pair, *refs):
    outs = refs[:chips - 1]
    sems, keep_v, got_v, pair_v, down_v, up_v = refs[chips - 1:]
    copies = Copies(sems)
    chip = place[0] // 2
    upper = place[0] % 2 == 0
    half = keep_v.shape[3]
    here = pl.ds(pl.multiple_of((place[0] % 2) * half, ROWS), half)
    for copy in [copies.start(keep, keep_v), copies.start(got, got_v), copies.start(pair.at[:, here], pair_v)]:
        copy.wait()
    for a in range(2):
        first, second = jnp.where(upper, keep_v[a], got_v[a]), jnp.where(upper, got_v[a], keep_v[a])
        down_v[a] = second[0] + pair_v[1] * first[0]
        up_v[a] = first[1] + pair_v[2] * second[1]
    for apart in range(1, chips):
        goes_down = chip + apart < chips
        sem = sems.at[2 + apart]

        @pl.when(goes_down)
        def _():
            pltpu.make_async_copy(down_v, outs[apart - 1], sem).start()

        @pl.when(jnp.logical_not(goes_down))
        def _():
            pltpu.make_async_copy(up_v, outs[apart - 1], sem).start()

    for apart in range(1, chips):
        pltpu.make_async_copy(down_v, outs[apart - 1], sems.at[2 + apart]).wait()


def chip_sums(place, keep, got, pair, chips):
    _, _, _, half, size = keep.shape
    single = lambda *shape: pltpu.VMEM(shape, jnp.float32)
    shape = (2, 2, half, size)
    return pl.pallas_call(
        functools.partial(chip_kernel, chips),
        in_specs=[in_smem] + [in_hbm] * 3,
        out_specs=[in_hbm] * (chips - 1),
        out_shape=[jax.ShapeDtypeStruct(shape, jnp.float32)] * (chips - 1),
        scratch_shapes=[
            pltpu.SemaphoreType.DMA((2 + chips,)),
            single(*keep.shape),
            single(*keep.shape),
            single(4, half, size),
            single(*shape),
            single(*shape),
        ],
        compiler_params=params,
        cost_estimate=brief,
        name="chip_sums",
    )(place, keep, got, pair)


def join_kernel(chips, place, keep, got, pair, far, *refs):
    news = refs[:chips - 1]
    mine, theirs, sems, keep_v, got_v, pair_v, far_v, news_v, mine_v, theirs_v = refs[chips - 1:]
    copies = Copies(sems)
    chip = place[0] // 2
    upper = place[0] % 2 == 0
    half = keep_v.shape[3]
    here = pl.ds(pl.multiple_of((place[0] % 2) * half, ROWS), half)
    ready = [copies.start(keep, keep_v), copies.start(got, got_v), copies.start(pair.at[:, here], pair_v), copies.start(far.at[:, here], far_v)]
    ready += [copies.start(news[i], news_v.at[i]) for i in range(chips - 1)]
    for copy in ready:
        copy.wait()
    for a in range(2):
        for ri in range(2):
            first, second = (keep_v, got_v), (got_v, keep_v)
            pick = lambda refs, way: jnp.where(upper, refs[0][a, way, ri], refs[1][a, way, ri])
            down = jnp.zeros((half, keep_v.shape[4]), jnp.float32)
            up = down
            for apart in range(1, chips):
                term = far_v[apart - 1] * news_v[apart - 1, a, ri]
                down = down + jnp.where(chip >= apart, term, 0.0)
                up = up + jnp.where(chip >= apart, 0.0, term)
            inner_up = pick(second, 1) + pair_v[3] * up
            inner_down = pick(first, 0) + pair_v[0] * down
            mine_v[a, 0, ri] = jnp.where(upper, down, inner_down)
            mine_v[a, 1, ri] = jnp.where(upper, inner_up, up)
            theirs_v[a, 0, ri] = jnp.where(upper, inner_down, down)
            theirs_v[a, 1, ri] = jnp.where(upper, up, inner_up)
    for copy in [copies.start(theirs_v, theirs), copies.start(mine_v, mine)]:
        copy.wait()


def join(place, keep, got, pair, far, news):
    chips = len(news) + 1
    _, _, _, half, size = keep.shape
    single = lambda *shape: pltpu.VMEM(shape, jnp.float32)
    return pl.pallas_call(
        functools.partial(join_kernel, chips),
        in_specs=[in_smem] + [in_hbm] * (3 + chips),
        out_specs=[in_hbm] * 2,
        out_shape=[jax.ShapeDtypeStruct(keep.shape, jnp.float32)] * 2,
        scratch_shapes=[
            pltpu.SemaphoreType.DMA((5 + chips,)),
            single(*keep.shape),
            single(*keep.shape),
            single(4, half, size),
            single(chips - 1, half, size),
            single(chips - 1, 2, 2, half, size),
            single(*keep.shape),
            single(*keep.shape),
        ],
        compiler_params=params,
        cost_estimate=lengthy,
        name="join",
    )(place, keep, got, pair, far, *news)


def inverse_kernel(counts, my, thick, shifts, across, weights, out, faces, m_all, f_all, g_all):
    total = f_all.shape[0]
    classes = out.shape[0]
    ky = shifts.shape[0]
    starts = [sum(counts[:c]) for c in range(classes + 1)]
    set_faces(thick, faces)
    shift = across[...] + jnp.where(my[0] < ky, shifts[jnp.minimum(my[0], ky - 1)], 1.0)
    one = jnp.ones_like(shift)
    zero = jnp.zeros_like(shift)

    def step(j, state):
        f, r, phi, s = state
        m = spread_face(faces[j], r) * r
        f = shift * thick[j] + m * f
        r = 1.0 / (spread_face(faces[j + 1], f) + f)
        m_all[j] = m
        f_all[j] = f
        i = total - 1 - j
        u = spread_face(faces[i + 1], s) * s * phi
        phi = shift * thick[i] + u
        s = 1.0 / (spread_face(faces[i], phi) + phi)
        g_all[i] = u
        return f, r, phi, s

    lax.fori_loop(0, total, step, (one, one, zero, zero), unroll=4)
    weight = weights[...]

    def centre(j, _):
        g_all[j] = weight / (f_all[j] + g_all[j])
        return 0

    lax.fori_loop(0, total, centre, 0, unroll=8)
    wide = out.shape[2]
    sub = lax.broadcasted_iota(jnp.int32, (ROWS, LANES), 0)
    lane = lax.broadcasted_iota(jnp.int32, (ROWS, wide), 1)
    row = lax.broadcasted_iota(jnp.int32, (ROWS, wide), 0)
    line = lambda ref, j, t: jnp.broadcast_to(ref[j, t:t + 1, :], (ROWS, LANES))

    def put(j, z, sums):
        new = []
        for c in range(classes):
            tiles = z[starts[c]:starts[c + 1]]
            total_tile = tiles[0]
            for tile in tiles[1:]:
                total_tile = total_tile + tile
            value = jnp.sum(total_tile, axis=1, keepdims=True)
            new.append(jnp.where(lane == j, value, sums[c]))
        return new

    for base in range(0, total, ROWS):
        z = [jnp.zeros((ROWS, LANES), jnp.float32)] * (starts[-1])
        sums = [jnp.zeros((ROWS, wide), jnp.float32)] * classes
        for i in range(ROWS - 1, -1, -1):
            j = base + i
            for t in range(starts[-1]):
                moved = z[t] * line(m_all, j + 1, t) if i < ROWS - 1 else z[t]
                z[t] = jnp.where(sub == i, line(g_all, j, t), moved)
            sums = put(j, z, sums)

        def above(back, state):
            z, sums = state
            for i in range(ROWS):
                j = base - 1 - back * ROWS - i
                z = [z[t] * line(m_all, j + 1, t) for t in range(starts[-1])]
                sums = put(j, z, sums)
            return z, sums

        if base:
            z, sums = lax.fori_loop(0, base // ROWS, above, (z, sums))
        for c in range(classes):
            out[c, base:base + ROWS, :] = sums[c] * jnp.where(lane == base + row, 0.5, 1.0)


def inverse_sums(my, thick, shifts, waves, size):
    total = thick.shape[0]
    classes = waves // 2 + 1
    lines, weights, counts = [], [], []
    for c in range(classes):
        k = c + waves * np.arange(size)
        weight = np.ones(size)
        if c in (0, waves // 2):
            partner = (waves * size - k) % (waves * size)
            weight = np.where(k < partner, 2.0, 1.0)[k <= partner]
            k = k[k <= partner]
        spare = -len(k) % LANES
        counts.append((len(k) + spare) // LANES)
        lines.append(np.pad(k, (0, spare)))
        weights.append(np.pad(weight, (0, spare)))
    spare = -sum(counts) % ROWS * LANES
    k = np.pad(np.concatenate(lines), (0, spare)).reshape(-1, LANES)
    weight = np.pad(np.concatenate(weights), (0, spare)).reshape(-1, LANES).astype(np.float32)
    across = horizontal(k, waves * size)
    wide = -(-total // LANES) * LANES
    return pl.pallas_call(
        functools.partial(inverse_kernel, counts),
        in_specs=[in_smem] * 3 + [in_vmem] * 2,
        out_shape=jax.ShapeDtypeStruct((classes, total, wide), jnp.float32),
        scratch_shapes=[pltpu.VMEM((total + 1, ROWS, LANES), jnp.float32)] + [pltpu.VMEM((total,) + across.shape, jnp.float32)] * 3,
        compiler_params=params,
        cost_estimate=lengthy,
        name="inverse_sums",
    )(my, thick, shifts, across, weight)


def interface_kernel(waves, matrices, edges, inverse, out):
    devices, _, wide = edges.shape
    total = wide // 2
    rows = 4 * waves
    lines = []
    for w in range(waves):
        line = edges[w]
        for d in range(1, devices // waves):
            line = line + edges[d * waves + w]
        lines.append(line)
    lines = jnp.concatenate(lines, 0)
    near, far = exact_dot(matrices[0], lines, NN), exact_dot(matrices[1], lines, NN)
    mixed = near[:, :total] + far[:, total:]
    result = jnp.zeros((2 * rows, total), jnp.float32)
    for c in range(inverse.shape[0]):
        part = mixed[c * 2 * rows:(c + 1) * 2 * rows]
        square = inverse[c][:, :total]
        result = result + (exact_dot(part, square, NN) + exact_dot(part, square, NT))
    result = jnp.concatenate([result[:rows], result[rows:]], 1)
    for w in range(waves):
        line = result[4 * w:4 * w + 4]
        for d in range(devices // waves):
            out[d * waves + w] = line


def interface(edges, inverse, waves, size):
    return pl.pallas_call(
        functools.partial(interface_kernel, waves),
        in_specs=[in_vmem] * 3,
        out_specs=in_vmem,
        out_shape=jax.ShapeDtypeStruct(edges.shape, jnp.float32),
        compiler_params=params,
        name="interface",
    )(interface_matrices(waves, size), edges, inverse)


def back_kernel(levels, total, place, thick, values, spread, t, mine, theirs, sines, b, m, end, odd_top, odd_rest, even_top, even_rest, out0, out1, sems, values_v, spread_v, t_v, ends, sines_v, b_v, m_v, end_v, ot, orest, et, er, picked, u_all, q_all, out_v):
    _, _, _, ky, size = b_v.shape
    first = place[0] * levels
    half = size // 2
    many = half // LANES
    core = place[0] % 2
    copies = Copies(sems)
    early = [copies.start(values.at[pl.ds(0, ky)], values_v), copies.start(spread, spread_v)]
    table = copies.start(t, t_v)
    both = []
    for source, start in ((mine, core), (theirs, 1 - core)):
        here = pl.ds(pl.multiple_of(start * (ky // 2), ROWS), ky // 2)
        both.append(copies.start(source, ends.at[:, :, :, here]))
    both.append(copies.start(sines, sines_v))
    rest = [copies.start(source, target) for source, target in ((m, m_v), (end, end_v), (odd_top, ot), (odd_rest, orest), (even_top, et), (even_rest, er))]
    fields = [copies.start(b.at[f // 2, f % 2], b_v.at[f // 2, f % 2]) for f in range(4)]
    for copy in early:
        copy.wait()
    lane = lax.broadcasted_iota(jnp.int32, (ky, 2 * total), 1)
    for f in range(4):
        parts = [part.astype(jnp.float32) for part in split(values_v[:, f, :])]
        for j in range(total):
            spot = (lane == j) | (lane == total + j)
            for p in range(2):
                picked[p, j * ky:(j + 1) * ky, :] = jnp.where(spot, parts[p], 0.0).astype(jnp.bfloat16)
        u_all[f] = (real_dot(picked[0], spread_v[...]) + real_dot(picked[1], spread_v[...])).reshape(total, ky, 2 * LANES)
    table.wait()
    for copy in both:
        copy.wait()

    def source(f, j, here):
        pair = u_all[f, j, here] * thick[j]
        return jnp.concatenate([pair[:, :LANES]] * many + [pair[:, LANES:]] * many, 1)

    def sweep(g, _):
        here = pl.ds(pl.multiple_of(g * ROWS, ROWS), ROWS)

        def from_above(block, y):
            for i in range(levels):
                j = block * levels + i
                step = t_v[j, here]
                y = [step * y[f] + source(f, j, here) for f in range(4)]
            return y

        def from_below(block, y):
            for i in range(levels):
                j = total - 1 - block * levels - i
                step = t_v[j + 1, here]
                y = [step * y[f] + source(f, j, here) for f in range(4)]
            return y

        zero = [jnp.zeros((ROWS, size), jnp.float32)] * 4
        wave = sines_v[...]
        for way, y in (
            (0, lax.fori_loop(0, place[0], from_above, zero)),
            (1, lax.fori_loop(0, total // levels - 1 - place[0], from_below, zero)),
        ):
            for f in range(4):
                ends[f // 2, way, f % 2, here] += wave * y[f]
        return 0

    lax.fori_loop(0, ky // ROWS, sweep, 0)
    for copy in rest:
        copy.wait()
    rows = levels * ky
    lane = lax.broadcasted_iota(jnp.int32, (ky, LANES), 1)
    outs = []
    for f in range(4):
        a, ri = f // 2, f % 2
        fields[f].wait()

        def tile(g, _):
            here = pl.ds(pl.multiple_of(g * ROWS, ROWS), ROWS)
            wave = sines_v[...]
            y = ends[a, 0, ri, here]
            ys = []
            for j in range(levels):
                y = b_v[a, ri, j, here] + wave * source(f, first + j, here) + m_v[j, here] * y
                ys.append(y)
            value = (y + end_v[0, here] * ends[a, 1, ri, here]) * end_v[1, here]
            q_all[levels - 1, here] = value
            for j in range(levels - 2, -1, -1):
                value = m_v[j + 1, here] * (ys[j] * (0.5 * (thick[first + j] + thick[first + j + 1])) + value)
                q_all[j, here] = value
            return 0

        lax.fori_loop(0, ky // ROWS, tile, 0)
        low, high = to_cells(
            q_all[:, :, :half].reshape(rows, half), q_all[:, :, half:].reshape(rows, half), ot, orest, et, er
        )
        for j in range(levels):
            height = thick[first + j] if a else 1.0
            scale = (2.0 / size) * height
            here = slice(j * ky, (j + 1) * ky)
            u = (u_all[f, first + j, :, :LANES] + u_all[f, first + j, :, LANES:]) * (0.5 * height)
            if many > 1:
                out_v[f, j, :, LANES:half] = low[here, LANES:] * scale
            out_v[f, j, :, :LANES] = jnp.where(lane == 0, u, low[here, :LANES] * scale)
            out_v[f, j, :, half:] = high[here] * scale
        outs.append(copies.start(out_v.at[f], (out0, out1)[a].at[ri]))
    for copy in outs:
        copy.wait()


def back(place, thick, values, sines, t, m, end, b, mine, theirs):
    _, _, levels, ky, size = b.shape
    total = t.shape[0] - 1
    half = size // 2
    single = lambda *shape: pltpu.VMEM(shape, jnp.float32)
    return pl.pallas_call(
        functools.partial(back_kernel, levels, total),
        in_specs=[in_smem] * 2 + [in_hbm] * 13,
        out_specs=[in_hbm] * 2,
        out_shape=[jax.ShapeDtypeStruct((2, levels, ky, size), jnp.float32)] * 2,
        scratch_shapes=[
            pltpu.SemaphoreType.DMA((20,)),
            single(ky, 4, 2 * total),
            pltpu.VMEM((2 * total, 2 * LANES), jnp.bfloat16),
            single(*t.shape),
            single(2, 2, 2, ky, size),
            single(ROWS, size),
            single(*b.shape),
            single(*m.shape),
            single(*end.shape),
            *[pltpu.VMEM((half, half), jnp.bfloat16)] * 4,
            pltpu.VMEM((2, total * ky, 2 * total), jnp.bfloat16),
            single(4, total, ky, 2 * LANES),
            single(levels, ky, size),
            single(4, levels, ky, size),
        ],
        compiler_params=params,
        name="back",
    )(place, thick, values, spread_matrix(total), t, mine, theirs, sines, b, m, end, *half_sines(size, True))


def shards(rhs, cotangent, thickness, ky_shift):
    waves = lax.axis_size("wave")
    count = lax.axis_size("depth")
    depth_pos = lax.axis_index("depth")
    wave_pos = lax.axis_index("wave")
    _, levels, ky, size = rhs.shape
    devices = waves * count
    chips = count // 2
    place = depth_pos.astype(jnp.int32).reshape(1)

    def across(a):
        return lax.ppermute(a, "depth", [(d, d ^ 1) for d in range(count)])

    def along(a, apart):
        return lax.ppermute(a, "depth", [(d, (d + 2 * apart) % count) for d in range(count)])

    def everywhere(a):
        return lax.all_to_all(a, ("depth", "wave"), split_axis=0, concat_axis=0, tiled=True)

    order = wave_order(size)
    sines = np.broadcast_to(np.sin(np.pi * order / size)[None, :], (ROWS, size)).astype(np.float32)
    across_k = horizontal(order, 2 * size)[None, :]
    t, m, end, pair, far, b, keep, give, edges = front(
        place, thickness, ky_shift, across_k, sines, rhs, cotangent, devices
    )

    my = (depth_pos * waves + wave_pos).astype(jnp.int32).reshape(1)
    got = across(give)
    edges = everywhere(edges)
    sums = chip_sums(place, keep, got, pair, chips)
    news = [along(sums[apart - 1], apart) for apart in range(1, chips)]
    inverse = inverse_sums(my, thickness, ky_shift, waves, size)
    values = interface(edges, inverse, waves, size)
    values = everywhere(values)
    news, _ = lax.optimization_barrier((news, values))
    mine, theirs = join(place, keep, got, pair, far, news)
    return back(place, thickness, values, sines, t, m, end, b, mine, across(theirs))


def solution(mesh):
    spec = P(None, "depth", None, "wave")
    return jax.shard_map(shards, mesh=mesh, in_specs=(spec, spec, P(), P()), out_specs=(spec, spec), check_vma=False)
```

```python
import functools
import math

import jax
import jax.numpy as jnp
import numpy as np
from jax import lax
from jax.experimental import pallas as pl
from jax.experimental.pallas import tpu as pltpu
from jax.sharding import PartitionSpec as P

aspect_ratio = 1.0
LANES = 128
ROWS = 8
VMEM_BYTES = 56 * 1024 * 1024
real_dot = functools.partial(jnp.dot, preferred_element_type=jnp.float32)
exact_dot = functools.partial(lax.dot_general, precision=lax.Precision.HIGHEST, preferred_element_type=jnp.float32)
NN = (((1,), (0,)), ((), ()))
NT = (((1,), (1,)), ((), ()))
in_smem = pl.BlockSpec(memory_space=pltpu.SMEM)
in_hbm = pl.BlockSpec(memory_space=pl.ANY)
in_vmem = pl.BlockSpec(memory_space=pltpu.VMEM)
params = pltpu.CompilerParams(vmem_limit_bytes=VMEM_BYTES)
small = pltpu.CompilerParams(vmem_limit_bytes=12 * 1024 * 1024)
medium = pltpu.CompilerParams(vmem_limit_bytes=30 * 1024 * 1024)
brief = pl.CostEstimate(flops=1, bytes_accessed=1, transcendentals=0)
lengthy = pl.CostEstimate(flops=20_000_000_000, bytes_accessed=40_000_000, transcendentals=0)


def wave_order(size):
    return np.concatenate([np.arange(1, size, 2), np.arange(0, size, 2)])


def half_sines(size, back=False, scale=1.0):
    half = size // 2
    place = np.arange(half)
    place[0] = half
    parts = []
    for waves in (np.arange(1, size, 2), np.arange(0, size, 2)):
        matrix = np.sin(np.pi * (np.outer(place, waves) % (2 * size)) / size)
        if waves[0] == 0:
            matrix[0] = 0.0
            matrix[:, 0] = 0.0
        matrix = (matrix.T if back else matrix).astype(np.float32) * np.float32(scale)
        top = matrix.astype(jnp.bfloat16)
        parts += [top, (matrix - top.astype(np.float32)).astype(jnp.bfloat16)]
    return parts


def edge_matrix(size, total):
    matrix = np.full((2 * LANES, 2 * total), 2.0 / size, np.float32)
    matrix[LANES:, total:] = -2.0 / size
    return matrix.astype(jnp.bfloat16)


def spread_matrix(total):
    matrix = np.ones((2 * total, 2 * LANES), np.float32)
    matrix[total:, LANES:] = -1.0
    return matrix.astype(jnp.bfloat16)


def interface_matrices(waves, size):
    classes = waves // 2 + 1
    matrix = np.zeros((2, classes, 2, waves, 4, waves, 4))
    for c in range(classes):
        weight = (1.0 if c in (0, waves // 2) else 2.0) / (size * waves)
        for w in range(waves):
            for e in range(2):
                for v in range(waves):
                    for g in range(2):
                        value = weight * math.cos(2.0 * math.pi * (c * (w + e - v - g) % waves) / waves)
                        for f in range(4):
                            matrix[g, c, e, w, f, v, f] = value
    matrix = matrix.reshape(2, classes * 2 * waves * 4, waves * 4)
    return np.concatenate([matrix[0], matrix[1]], 1).astype(np.float32)


def split(values):
    high = values.astype(jnp.bfloat16)
    return high, (values - high.astype(jnp.float32)).astype(jnp.bfloat16)


def product(values, top, rest):
    high, low = split(values)
    return real_dot(high, top[...]) + (real_dot(low, top[...]) + real_dot(high, rest[...]))


def mirror(values):
    rows = values.shape[0]
    lane = lax.broadcasted_iota(jnp.int32, (rows, LANES), 1)
    back = (LANES - lane) % LANES
    tiles = [values[:, a * LANES:(a + 1) * LANES] for a in range(values.shape[1] // LANES)]
    many = len(tiles)
    out = []
    for a in range(many):
        turned = jnp.take_along_axis(tiles[many - 1 - a], back, axis=1)
        out.append(jnp.where(lane == 0, tiles[(many - a) % many], turned))
    return jnp.concatenate(out, 1) if many > 1 else out[0]


def to_waves(values, odd_top, odd_rest, even_top, even_rest):
    half = values.shape[1] // 2
    low, high = values[:, :half], mirror(values[:, half:])
    lane = lax.broadcasted_iota(jnp.int32, low.shape, 1)
    low = jnp.where(lane == 0, 0.0, low)
    return product(low + high, odd_top, odd_rest), product(low - high, even_top, even_rest)


def to_cells(odd, even, odd_top, odd_rest, even_top, even_rest):
    p, m = product(odd, odd_top, odd_rest), product(even, even_top, even_rest)
    return p + m, mirror(p - m)


def horizontal(wavenumber, length):
    return (aspect_ratio * 4.0 * np.sin(math.pi * wavenumber / length) ** 2).astype(np.float32)


def set_faces(thick, faces):
    total = faces.shape[0] - 1
    two = jnp.full((ROWS, LANES), 2.0, jnp.float32)
    faces[0] = two / (two * 0.0 + thick[0])
    faces[total] = two * 0.0

    def one(j, _):
        faces[j] = two / (two * 0.0 + (thick[j - 1] + thick[j]))
        return 0

    lax.fori_loop(1, total, one, 0, unroll=3)


def spread_face(tile, like):
    rows, lanes = like.shape
    wide = jnp.concatenate([tile] * (lanes // LANES), 1) if lanes > LANES else tile
    return jnp.concatenate([wide] * (rows // ROWS), 0) if rows > ROWS else wide


class Copies:
    def __init__(self, sems):
        self.sems, self.used = sems, 0

    def start(self, source, target):
        copy = pltpu.make_async_copy(source, target, self.sems.at[self.used])
        self.used += 1
        copy.start()
        return copy


def coefficients(levels, total, group, place, thick, faces, shifts, across, t_out, m_out, end_out, pair_out, far_out, lam, m_chip, f_chip, n_chip, u_chip, down_all, up_all):
    ky = lam.shape[0]
    span = 2 * levels
    chips = total // span
    chip = place[0] // 2
    start = chip * span
    upper = place[0] % 2 == 0
    own = (place[0] % 2) * levels
    for row in range(ky):
        lam[row:row + 1, :] = across[...] + shifts[row]

    def down_step(shift, j, f, r):
        m = spread_face(faces[j], r) * r
        f = shift * thick[j] + m * f
        return m, f, 1.0 / (spread_face(faces[j + 1], f) + f)

    def up_step(shift, j, phi, s):
        n = spread_face(faces[j + 1], s) * s
        u = n * phi
        phi = shift * thick[j] + u
        return n, u, phi, 1.0 / (spread_face(faces[j], phi) + phi)

    def part(g, _):
        here = pl.ds(pl.multiple_of(g * group, group), group)
        shift = lam[here]
        one = jnp.ones_like(shift)
        zero = jnp.zeros_like(shift)

        def down_chip(c, state):
            f, r = state
            product = one
            for i in range(span):
                m, f, r = down_step(shift, c * span + i, f, r)
                t_out[c * span + i, here] = m
                product = product * m
            down_all[c] = product
            return f, r

        def up_chip(back, state):
            phi, s = state
            c = chips - 1 - back
            product = one
            for i in range(span - 1, -1, -1):
                n, _, phi, s = up_step(shift, c * span + i, phi, s)
                t_out[c * span + i + 1, here] = n
                product = product * n
            up_all[c] = product
            return phi, s

        f, r = lax.fori_loop(0, chip, down_chip, (one, one))
        for i in range(span):
            m, f, r = down_step(shift, start + i, f, r)
            m_chip[i], f_chip[i] = m, f
        phi, s = lax.fori_loop(0, chips - 1 - chip, up_chip, (zero, zero))
        for i in range(span - 1, -1, -1):
            n, u, phi, s = up_step(shift, start + i, phi, s)
            n_chip[i], u_chip[i] = n, u

        for i in range(levels):
            t_out[start + i, here] = m_chip[i]
            t_out[start + levels + 1 + i, here] = n_chip[levels + i]
        t_out[start + levels, here] = jnp.where(upper, n_chip[levels - 1], m_chip[levels])
        for i in range(levels):
            m_out[i, here] = m_chip[own + i]
        last = own + levels - 1
        end_out[0, here] = n_chip[last]
        end_out[1, here] = 1.0 / (f_chip[last] + u_chip[last])
        end_out[2, here] = f_chip[own] + u_chip[own]
        for core in range(2):
            down, up = m_chip[core * levels], n_chip[core * levels]
            for i in range(1, levels):
                down = down * m_chip[core * levels + i]
                up = up * n_chip[core * levels + i]
            pair_out[core, here] = down
            pair_out[2 + core, here] = up
        above, below = [one], [one]
        for apart in range(1, chips - 1):
            above.append(above[-1] * jnp.where(chip >= apart, down_all[jnp.maximum(chip - apart, 0)], one))
            below.append(below[-1] * jnp.where(chip + apart < chips, up_all[jnp.minimum(chip + apart, chips - 1)], one))
        for apart in range(1, chips):
            far_out[apart - 1, here] = jnp.where(chip >= apart, above[apart - 1], below[chips - apart - 1])
        return 0

    lax.fori_loop(0, ky // group, part, 0)


def lane_sum(values):
    tiles = [values[:, t * LANES:(t + 1) * LANES] for t in range(values.shape[1] // LANES)]
    while len(tiles) > 1:
        tiles = [a + b for a, b in zip(tiles[0::2], tiles[1::2])] + tiles[len(tiles) // 2 * 2:]
    return tiles[0]


def front_kernel(levels, total, group, place, thick, shifts, across, sines, edge_mix, x0, x1, odd_top, odd_rest, even_top, even_rest, t_out, m_out, end_out, pair_out, far_out, b_out, keep_out, give_out, edge_out, sems, *scratch):
    across_v, sines_v, mix_v, x, ot, orest, et, er, t, m, end, pair, far, b, c_all, z_all, sums, edges, faces, lam, *work = scratch
    _, _, _, ky, size = x.shape
    first = place[0] * levels
    half = size // 2
    copies = Copies(sems)
    early = [copies.start(across, across_v)]
    fields = [copies.start(x0, x.at[0])]
    mats = [copies.start(source, target) for source, target in ((odd_top, ot), (odd_rest, orest), (even_top, et), (even_rest, er))]
    mats += [copies.start(sines, sines_v)]
    fields += [copies.start(x1, x.at[1])]
    late = [copies.start(edge_mix, mix_v)]
    set_faces(thick, faces)
    for copy in early:
        copy.wait()
    coefficients(levels, total, group, place, thick, faces, shifts, across_v, t, m, end, pair, far, lam, *work)
    outs = [copies.start(source, target) for source, target in ((pair, pair_out), (far, far_out))]
    outs += [copies.start(source, target) for source, target in ((t, t_out), (m, m_out), (end, end_out))]
    for copy in mats:
        copy.wait()
    lane = lax.broadcasted_iota(jnp.int32, (ROWS, LANES), 1)
    spot = jnp.where(lane == 0, size / 4.0, 0.0)
    core = place[0] % 2

    def put(f, j, here, values, height, own=None):
        odd, even = lane_sum(values[:, :half]) * height, lane_sum(values[:, half:]) * height
        if own is not None:
            odd, even = odd + own, even + own
        sums[f, 0, j, here] = odd
        sums[f, 1, j, here] = even

    for a in range(2):
        fields[a].wait()
        odd, even = to_waves(x[a].reshape(2 * levels * ky, size), ot, orest, et, er)
        for ri in range(2):
            for j in range(levels):
                rows = slice((ri * levels + j) * ky, (ri * levels + j + 1) * ky)
                scale = thick[first + j] if a == 0 else 1.0
                b[a, ri, j, :, :half] = odd[rows] * scale
                b[a, ri, j, :, half:] = even[rows] * scale
        outs.append(copies.start(b.at[a], b_out.at[a]))
        for ri in range(2):
            f = 2 * a + ri

            def tile(g, _):
                here = pl.ds(pl.multiple_of(g * ROWS, ROWS), ROWS)
                wave = sines_v[...]
                y = b[a, ri, 0, here]
                ys = [y]
                for j in range(1, levels):
                    y = b[a, ri, j, here] + m[j, here] * y
                    ys.append(y)
                c_all[a, 0, ri, here] = y
                value = y * end[1, here]
                z_all[1, f, here] = value * wave
                for j in range(levels - 1, -1, -1):
                    if j < levels - 1:
                        value = m[j + 1, here] * (ys[j] * (0.5 * (thick[first + j] + thick[first + j + 1])) + value)
                    height = thick[first + j]
                    own = jnp.broadcast_to(x[a, ri, j, here, 0:1], (ROWS, LANES)) * (spot * height if a == 0 else spot)
                    put(f, first + j, here, value * wave, height, own)
                z_all[0, f, here] = value * wave
                c_all[a, 1, ri, here] = value * end[2, here]
                return 0

            lax.fori_loop(0, ky // ROWS, tile, 0)
        for start, out in ((core, keep_out), (1 - core, give_out)):
            here = pl.ds(pl.multiple_of(start * (ky // 2), ROWS), ky // 2)
            outs.append(copies.start(c_all.at[a, :, :, here], out.at[a]))

    def reach(g, _):
        here = pl.ds(pl.multiple_of(g * ROWS, ROWS), ROWS)

        def up(block, z):
            for i in range(levels):
                j = first - 1 - block * levels - i
                step = t[j + 1, here]
                z = [step * one for one in z]
                for f in range(4):
                    put(f, j, here, z[f], thick[j])
            return z

        def down(block, z):
            for i in range(levels):
                j = first + levels + block * levels + i
                step = t[j, here]
                z = [step * one for one in z]
                for f in range(4):
                    put(f, j, here, z[f], thick[j])
            return z

        lax.fori_loop(0, place[0], up, [z_all[0, f, here] for f in range(4)])
        lax.fori_loop(0, total // levels - 1 - place[0], down, [z_all[1, f, here] for f in range(4)])
        return 0

    lax.fori_loop(0, ky // ROWS, reach, 0)
    for copy in late:
        copy.wait()
    if edges.shape[0] > ky:
        edges[...] = jnp.zeros_like(edges)
    wide = 2 * total
    lane = lax.broadcasted_iota(jnp.int32, (ky, wide), 1) % total
    for f in range(4):
        both = [sums[f, way].reshape(total * ky, LANES) for way in range(2)]
        high, low = split(jnp.concatenate(both, 1))
        spread = (real_dot(high, mix_v[...]) + real_dot(low, mix_v[...])).reshape(total, ky, wide)
        line = spread[0]
        for j in range(1, total):
            line = jnp.where(lane == j, spread[j], line)
        edges[:ky, f, :] = line
    outs.append(copies.start(edges, edge_out))
    for copy in outs:
        copy.wait()


def front(place, thick, shifts, across, sines, rhs, cotangent, devices):
    _, levels, ky, size = rhs.shape
    total = thick.shape[0]
    chips = total // (2 * levels)
    group = min(2 * ROWS, ky)
    half = size // 2
    wide = 2 * total
    single = lambda *shape: pltpu.VMEM(shape, jnp.float32)
    tables = [(n, ky, size) for n in (total + 1, levels, 3, 4, chips - 1)]
    shapes = tables + [(2, 2, levels, ky, size), (2, 2, 2, ky // 2, size), (2, 2, 2, ky // 2, size), (devices, 4, wide)]
    return pl.pallas_call(
        functools.partial(front_kernel, levels, total, group),
        in_specs=[in_smem] * 3 + [in_hbm] * 9,
        out_specs=[in_hbm] * len(shapes),
        out_shape=[jax.ShapeDtypeStruct(shape, jnp.float32) for shape in shapes],
        scratch_shapes=[
            pltpu.SemaphoreType.DMA((22,)),
            single(1, size),
            single(ROWS, size),
            pltpu.VMEM((2 * LANES, wide), jnp.bfloat16),
            single(2, 2, levels, ky, size),
            *[pltpu.VMEM((half, half), jnp.bfloat16)] * 4,
            *[single(*shape) for shape in tables],
            single(2, 2, levels, ky, size),
            single(2, 2, 2, ky, size),
            single(2, 4, ky, size),
            single(4, 2, total, ky, LANES),
            single(devices, 4, wide),
            single(total + 1, ROWS, LANES),
            single(ky, size),
            *[single(2 * levels, group, size)] * 4,
            *[single(chips, group, size)] * 2,
        ],
        compiler_params=params,
        name="front",
    )(place, thick, shifts, across, sines, edge_matrix(size, total), rhs, cotangent, *half_sines(size))


def chip_kernel(chips, place, keep, got_v, pair, *refs):
    outs = refs[:chips - 1]
    sems, keep_v, pair_v, down_v, up_v = refs[chips - 1:]
    copies = Copies(sems)
    chip = place[0] // 2
    upper = place[0] % 2 == 0
    half = keep_v.shape[3]
    here = pl.ds(pl.multiple_of((place[0] % 2) * half, ROWS), half)
    for copy in [copies.start(keep, keep_v), copies.start(pair.at[:, here], pair_v)]:
        copy.wait()
    for a in range(2):
        first, second = jnp.where(upper, keep_v[a], got_v[a]), jnp.where(upper, got_v[a], keep_v[a])
        down_v[a] = second[0] + pair_v[1] * first[0]
        up_v[a] = first[1] + pair_v[2] * second[1]
    for apart in range(1, chips):
        goes_down = chip + apart < chips
        sem = sems.at[1 + apart]

        @pl.when(goes_down)
        def _():
            pltpu.make_async_copy(down_v, outs[apart - 1], sem).start()

        @pl.when(jnp.logical_not(goes_down))
        def _():
            pltpu.make_async_copy(up_v, outs[apart - 1], sem).start()

    for apart in range(1, chips):
        pltpu.make_async_copy(down_v, outs[apart - 1], sems.at[1 + apart]).wait()


def chip_sums(place, keep, got, pair, chips):
    _, _, _, half, size = keep.shape
    single = lambda *shape: pltpu.VMEM(shape, jnp.float32)
    shape = (2, 2, half, size)
    return pl.pallas_call(
        functools.partial(chip_kernel, chips),
        in_specs=[in_smem, in_hbm, in_vmem, in_hbm],
        out_specs=[in_hbm] * (chips - 1),
        out_shape=[jax.ShapeDtypeStruct(shape, jnp.float32)] * (chips - 1),
        scratch_shapes=[
            pltpu.SemaphoreType.DMA((1 + chips,)),
            single(*keep.shape),
            single(4, half, size),
            single(*shape),
            single(*shape),
        ],
        compiler_params=small,
        cost_estimate=brief,
        name="chip_sums",
    )(place, keep, got, pair)


def join_kernel(chips, place, keep, got, pair, far, *refs):
    news = refs[:chips - 1]
    mine, theirs, sems, keep_v, got_v, pair_v, far_v, mine_v, theirs_v = refs[chips - 1:]
    copies = Copies(sems)
    chip = place[0] // 2
    upper = place[0] % 2 == 0
    half = keep_v.shape[3]
    here = pl.ds(pl.multiple_of((place[0] % 2) * half, ROWS), half)
    ready = [copies.start(keep, keep_v), copies.start(got, got_v), copies.start(pair.at[:, here], pair_v), copies.start(far.at[:, here], far_v)]
    for copy in ready:
        copy.wait()
    for a in range(2):
        for ri in range(2):
            first, second = (keep_v, got_v), (got_v, keep_v)
            pick = lambda refs, way: jnp.where(upper, refs[0][a, way, ri], refs[1][a, way, ri])
            down = jnp.zeros((half, keep_v.shape[4]), jnp.float32)
            up = down
            for apart in range(1, chips):
                term = far_v[apart - 1] * news[apart - 1][a, ri]
                down = down + jnp.where(chip >= apart, term, 0.0)
                up = up + jnp.where(chip >= apart, 0.0, term)
            inner_up = pick(second, 1) + pair_v[3] * up
            inner_down = pick(first, 0) + pair_v[0] * down
            mine_v[a, 0, ri] = jnp.where(upper, down, inner_down)
            mine_v[a, 1, ri] = jnp.where(upper, inner_up, up)
            theirs_v[a, 0, ri] = jnp.where(upper, inner_down, down)
            theirs_v[a, 1, ri] = jnp.where(upper, up, inner_up)
    for copy in [copies.start(theirs_v, theirs), copies.start(mine_v, mine)]:
        copy.wait()


def join(place, keep, got, pair, far, news):
    chips = len(news) + 1
    _, _, _, half, size = keep.shape
    single = lambda *shape: pltpu.VMEM(shape, jnp.float32)
    return pl.pallas_call(
        functools.partial(join_kernel, chips),
        in_specs=[in_smem] + [in_hbm] * 4 + [in_vmem] * (chips - 1),
        out_specs=[in_hbm] * 2,
        out_shape=[jax.ShapeDtypeStruct(keep.shape, jnp.float32)] * 2,
        scratch_shapes=[
            pltpu.SemaphoreType.DMA((6,)),
            single(*keep.shape),
            single(*keep.shape),
            single(4, half, size),
            single(chips - 1, half, size),
            single(*keep.shape),
            single(*keep.shape),
        ],
        compiler_params=small,
        cost_estimate=lengthy,
        name="join",
    )(place, keep, got, pair, far, *news)


def inverse_kernel(counts, my, thick, shifts, across, weights, out, faces, m_all, f_all, g_all):
    total = f_all.shape[0]
    classes = out.shape[0]
    ky = shifts.shape[0]
    starts = [sum(counts[:c]) for c in range(classes + 1)]
    set_faces(thick, faces)
    shift = across[...] + jnp.where(my[0] < ky, shifts[jnp.minimum(my[0], ky - 1)], 1.0)
    one = jnp.ones_like(shift)
    zero = jnp.zeros_like(shift)

    def step(j, state):
        f, r, phi, s = state
        m = spread_face(faces[j], r) * r
        f = shift * thick[j] + m * f
        r = 1.0 / (spread_face(faces[j + 1], f) + f)
        m_all[j] = m
        f_all[j] = f
        i = total - 1 - j
        u = spread_face(faces[i + 1], s) * s * phi
        phi = shift * thick[i] + u
        s = 1.0 / (spread_face(faces[i], phi) + phi)
        g_all[i] = u
        return f, r, phi, s

    lax.fori_loop(0, total, step, (one, one, zero, zero), unroll=4)
    weight = weights[...]

    def centre(j, _):
        g_all[j] = weight / (f_all[j] + g_all[j])
        return 0

    lax.fori_loop(0, total, centre, 0, unroll=8)
    wide = out.shape[2]
    sub = lax.broadcasted_iota(jnp.int32, (ROWS, LANES), 0)
    lane = lax.broadcasted_iota(jnp.int32, (ROWS, wide), 1)
    row = lax.broadcasted_iota(jnp.int32, (ROWS, wide), 0)
    line = lambda ref, j, t: jnp.broadcast_to(ref[j, t:t + 1, :], (ROWS, LANES))

    def put(j, z, sums):
        new = []
        for c in range(classes):
            tiles = z[starts[c]:starts[c + 1]]
            total_tile = tiles[0]
            for tile in tiles[1:]:
                total_tile = total_tile + tile
            value = jnp.sum(total_tile, axis=1, keepdims=True)
            new.append(jnp.where(lane == j, value, sums[c]))
        return new

    for base in range(0, total, ROWS):
        z = [jnp.zeros((ROWS, LANES), jnp.float32)] * (starts[-1])
        sums = [jnp.zeros((ROWS, wide), jnp.float32)] * classes
        for i in range(ROWS - 1, -1, -1):
            j = base + i
            for t in range(starts[-1]):
                moved = z[t] * line(m_all, j + 1, t) if i < ROWS - 1 else z[t]
                z[t] = jnp.where(sub == i, line(g_all, j, t), moved)
            sums = put(j, z, sums)

        def above(back, state):
            z, sums = state
            for i in range(ROWS):
                j = base - 1 - back * ROWS - i
                z = [z[t] * line(m_all, j + 1, t) for t in range(starts[-1])]
                sums = put(j, z, sums)
            return z, sums

        if base:
            z, sums = lax.fori_loop(0, base // ROWS, above, (z, sums))
        for c in range(classes):
            out[c, base:base + ROWS, :] = sums[c] * jnp.where(lane == base + row, 0.5, 1.0)


def inverse_sums(my, thick, shifts, waves, size):
    total = thick.shape[0]
    classes = waves // 2 + 1
    lines, weights, counts = [], [], []
    for c in range(classes):
        k = c + waves * np.arange(size)
        weight = np.ones(size)
        if c in (0, waves // 2):
            partner = (waves * size - k) % (waves * size)
            weight = np.where(k < partner, 2.0, 1.0)[k <= partner]
            k = k[k <= partner]
        spare = -len(k) % LANES
        counts.append((len(k) + spare) // LANES)
        lines.append(np.pad(k, (0, spare)))
        weights.append(np.pad(weight, (0, spare)))
    spare = -sum(counts) % ROWS * LANES
    k = np.pad(np.concatenate(lines), (0, spare)).reshape(-1, LANES)
    weight = np.pad(np.concatenate(weights), (0, spare)).reshape(-1, LANES).astype(np.float32)
    across = horizontal(k, waves * size)
    wide = -(-total // LANES) * LANES
    return pl.pallas_call(
        functools.partial(inverse_kernel, counts),
        in_specs=[in_smem] * 3 + [in_vmem] * 2,
        out_shape=jax.ShapeDtypeStruct((classes, total, wide), jnp.float32),
        scratch_shapes=[pltpu.VMEM((total + 1, ROWS, LANES), jnp.float32)] + [pltpu.VMEM((total,) + across.shape, jnp.float32)] * 3,
        compiler_params=small,
        cost_estimate=lengthy,
        name="inverse_sums",
    )(my, thick, shifts, across, weight)


def interface_kernel(waves, matrices, edges, inverse, out):
    devices, _, wide = edges.shape
    total = wide // 2
    rows = 4 * waves
    lines = []
    for w in range(waves):
        line = edges[w]
        for d in range(1, devices // waves):
            line = line + edges[d * waves + w]
        lines.append(line)
    lines = jnp.concatenate(lines, 0)
    lines = jnp.concatenate([lines[:, :total], lines[:, total:]], 0)
    mixed = exact_dot(matrices[...], lines, NN)
    classes = inverse.shape[0]
    parts = jnp.concatenate([mixed[c * 2 * rows:(c + 1) * 2 * rows] for c in range(classes)], 1)
    squares = [inverse[c][:, :total] for c in range(classes)]
    result = exact_dot(parts, jnp.concatenate(squares, 0), NN) + exact_dot(parts, jnp.concatenate(squares, 1), NT)
    result = jnp.concatenate([result[:rows], result[rows:]], 1)
    for w in range(waves):
        line = result[4 * w:4 * w + 4]
        for d in range(devices // waves):
            out[d * waves + w] = line


def interface(edges, inverse, waves, size):
    return pl.pallas_call(
        functools.partial(interface_kernel, waves),
        in_specs=[in_vmem] * 3,
        out_specs=in_vmem,
        out_shape=jax.ShapeDtypeStruct(edges.shape, jnp.float32),
        compiler_params=small,
        name="interface",
    )(interface_matrices(waves, size), edges, inverse)


def back_kernel(levels, total, place, thick, values_v, spread_v, t_v, mine, theirs, sines_v, b_v, m_v, end_v, ot, orest, et, er, out0, out1, sems, ends, picked, u_all, q_all, out_v):
    _, _, _, ky, size = b_v.shape
    first = place[0] * levels
    half = size // 2
    many = half // LANES
    core = place[0] % 2
    copies = Copies(sems)
    here, there = (pl.ds(pl.multiple_of(start * (ky // 2), ROWS), ky // 2) for start in (core, 1 - core))
    lane = lax.broadcasted_iota(jnp.int32, (ky, 2 * total), 1)
    for f in range(4):
        parts = [part.astype(jnp.float32) for part in split(values_v[:ky, f, :])]
        for j in range(total):
            spot = (lane == j) | (lane == total + j)
            for p in range(2):
                picked[p, j * ky:(j + 1) * ky, :] = jnp.where(spot, parts[p], 0.0).astype(jnp.bfloat16)
        u_all[f] = (real_dot(picked[0], spread_v[...]) + real_dot(picked[1], spread_v[...])).reshape(total, ky, 2 * LANES)
    ends[:, :, :, here] = mine[...]
    ends[:, :, :, there] = theirs[...]

    def source(f, j, here):
        pair = u_all[f, j, here] * thick[j]
        return jnp.concatenate([pair[:, :LANES]] * many + [pair[:, LANES:]] * many, 1)

    def sweep(g, _):
        here = pl.ds(pl.multiple_of(g * ROWS, ROWS), ROWS)

        def from_above(block, y):
            for i in range(levels):
                j = block * levels + i
                step = t_v[j, here]
                y = [step * y[f] + source(f, j, here) for f in range(4)]
            return y

        def from_below(block, y):
            for i in range(levels):
                j = total - 1 - block * levels - i
                step = t_v[j + 1, here]
                y = [step * y[f] + source(f, j, here) for f in range(4)]
            return y

        zero = [jnp.zeros((ROWS, size), jnp.float32)] * 4
        wave = sines_v[...]
        for way, y in (
            (0, lax.fori_loop(0, place[0], from_above, zero)),
            (1, lax.fori_loop(0, total // levels - 1 - place[0], from_below, zero)),
        ):
            for f in range(4):
                ends[f // 2, way, f % 2, here] += wave * y[f]
        return 0

    lax.fori_loop(0, ky // ROWS, sweep, 0)
    rows = 2 * levels * ky
    lane = lax.broadcasted_iota(jnp.int32, (ky, LANES), 1)
    outs = []
    for a in range(2):
        def tile(g, _):
            here = pl.ds(pl.multiple_of(g * ROWS, ROWS), ROWS)
            wave = sines_v[...]
            for ri in range(2):
                y = ends[a, 0, ri, here]
                ys = []
                for j in range(levels):
                    y = b_v[a, ri, j, here] + wave * source(2 * a + ri, first + j, here) + m_v[j, here] * y
                    ys.append(y)
                value = (y + end_v[0, here] * ends[a, 1, ri, here]) * end_v[1, here]
                q_all[ri, levels - 1, here] = value
                for j in range(levels - 2, -1, -1):
                    value = m_v[j + 1, here] * (ys[j] * (0.5 * (thick[first + j] + thick[first + j + 1])) + value)
                    q_all[ri, j, here] = value
            return 0

        lax.fori_loop(0, ky // ROWS, tile, 0)
        low, high = to_cells(
            q_all[:, :, :, :half].reshape(rows, half), q_all[:, :, :, half:].reshape(rows, half), ot, orest, et, er
        )
        for ri in range(2):
            for j in range(levels):
                height = thick[first + j] if a else 1.0
                here = slice((ri * levels + j) * ky, (ri * levels + j + 1) * ky)
                u = u_all[2 * a + ri, first + j]
                u = (u[:, :LANES] + u[:, LANES:]) * (0.5 * height)
                if many > 1:
                    out_v[a, ri, j, :, LANES:half] = low[here, LANES:] * height
                out_v[a, ri, j, :, :LANES] = jnp.where(lane == 0, u, low[here, :LANES] * height)
                out_v[a, ri, j, :, half:] = high[here] * height
            outs.append(copies.start(out_v.at[a, ri], (out0, out1)[a].at[ri]))
    for copy in outs:
        copy.wait()


def back(place, thick, values, sines, t, m, end, b, mine, theirs):
    _, _, levels, ky, size = b.shape
    total = t.shape[0] - 1
    half = size // 2
    single = lambda *shape: pltpu.VMEM(shape, jnp.float32)
    return pl.pallas_call(
        functools.partial(back_kernel, levels, total),
        in_specs=[in_smem] * 2 + [in_vmem] * 13,
        out_specs=[in_hbm] * 2,
        out_shape=[jax.ShapeDtypeStruct((2, levels, ky, size), jnp.float32)] * 2,
        scratch_shapes=[
            pltpu.SemaphoreType.DMA((4,)),
            single(2, 2, 2, ky, size),
            pltpu.VMEM((2, total * ky, 2 * total), jnp.bfloat16),
            single(4, total, ky, 2 * LANES),
            single(2, levels, ky, size),
            single(2, 2, levels, ky, size),
        ],
        compiler_params=medium,
        name="back",
    )(place, thick, values, spread_matrix(total), t, mine, theirs, sines, b, m, end, *half_sines(size, True, 2.0 / size))


def shards(rhs, cotangent, thickness, ky_shift):
    waves = lax.axis_size("wave")
    count = lax.axis_size("depth")
    depth_pos = lax.axis_index("depth")
    wave_pos = lax.axis_index("wave")
    _, levels, ky, size = rhs.shape
    devices = waves * count
    chips = count // 2
    place = depth_pos.astype(jnp.int32).reshape(1)

    def across(a):
        return lax.ppermute(a, "depth", [(d, d ^ 1) for d in range(count)])

    def along(a, apart):
        return lax.ppermute(a, "depth", [(d, (d + 2 * apart) % count) for d in range(count)])

    def everywhere(a):
        return lax.all_to_all(a, ("depth", "wave"), split_axis=0, concat_axis=0, tiled=True)

    order = wave_order(size)
    sines = np.broadcast_to(np.sin(np.pi * order / size)[None, :], (ROWS, size)).astype(np.float32)
    across_k = horizontal(order, 2 * size)[None, :]
    t, m, end, pair, far, b, keep, give, edges = front(
        place, thickness, ky_shift, across_k, sines, rhs, cotangent, devices
    )

    my = (depth_pos * waves + wave_pos).astype(jnp.int32).reshape(1)
    got = across(give)
    edges = everywhere(edges)
    sums = chip_sums(place, keep, got, pair, chips)
    news = [along(sums[apart - 1], apart) for apart in range(1, chips)]
    inverse = inverse_sums(my, thickness, ky_shift, waves, size)
    values = interface(edges, inverse, waves, size)
    values = everywhere(values)
    news, _ = lax.optimization_barrier((news, values))
    mine, theirs = join(place, keep, got, pair, far, news)
    return back(place, thickness, values, sines, t, m, end, b, mine, across(theirs))


def solution(mesh):
    spec = P(None, "depth", None, "wave")
    return jax.shard_map(shards, mesh=mesh, in_specs=(spec, spec, P(), P()), out_specs=(spec, spec), check_vma=False)
```

```python
import functools
import math

import jax
import jax.numpy as jnp
import numpy as np
from jax import lax
from jax.experimental import pallas as pl
from jax.experimental.pallas import tpu as pltpu
from jax.sharding import PartitionSpec as P

aspect_ratio = 1.0
LANES = 128
ROWS = 8
VMEM_BYTES = 56 * 1024 * 1024
real_dot = functools.partial(jnp.dot, preferred_element_type=jnp.float32)
exact_dot = functools.partial(lax.dot_general, precision=lax.Precision.HIGHEST, preferred_element_type=jnp.float32)
NN = (((1,), (0,)), ((), ()))
NT = (((1,), (1,)), ((), ()))
in_smem = pl.BlockSpec(memory_space=pltpu.SMEM)
in_hbm = pl.BlockSpec(memory_space=pl.ANY)
in_vmem = pl.BlockSpec(memory_space=pltpu.VMEM)
params = pltpu.CompilerParams(vmem_limit_bytes=VMEM_BYTES)
small = pltpu.CompilerParams(vmem_limit_bytes=12 * 1024 * 1024)
medium = pltpu.CompilerParams(vmem_limit_bytes=46 * 1024 * 1024)
brief = pl.CostEstimate(flops=1, bytes_accessed=1, transcendentals=0)
lengthy = pl.CostEstimate(flops=20_000_000_000, bytes_accessed=40_000_000, transcendentals=0)


def wave_order(size):
    return np.concatenate([np.arange(1, size, 2), np.arange(0, size, 2)])


def half_sines(size, back=False, scale=1.0):
    half = size // 2
    place = np.arange(half)
    place[0] = half
    parts = []
    for waves in (np.arange(1, size, 2), np.arange(0, size, 2)):
        matrix = np.sin(np.pi * (np.outer(place, waves) % (2 * size)) / size)
        if waves[0] == 0:
            matrix[0] = 0.0
            matrix[:, 0] = 0.0
        matrix = (matrix.T if back else matrix).astype(np.float32) * np.float32(scale)
        top = matrix.astype(jnp.bfloat16)
        parts += [top, (matrix - top.astype(np.float32)).astype(jnp.bfloat16)]
    return parts


def edge_matrix(size, total):
    matrix = np.full((2 * LANES, 2 * total), 2.0 / size, np.float32)
    matrix[LANES:, total:] = -2.0 / size
    return matrix.astype(jnp.bfloat16)


def spread_matrix(total):
    matrix = np.ones((2 * total, 2 * LANES), np.float32)
    matrix[total:, LANES:] = -1.0
    return matrix.astype(jnp.bfloat16)


def interface_matrices(waves, size):
    classes = waves // 2 + 1
    matrix = np.zeros((2, classes, 2, waves, 4, waves, 4))
    for c in range(classes):
        weight = (1.0 if c in (0, waves // 2) else 2.0) / (size * waves)
        for w in range(waves):
            for e in range(2):
                for v in range(waves):
                    for g in range(2):
                        value = weight * math.cos(2.0 * math.pi * (c * (w + e - v - g) % waves) / waves)
                        for f in range(4):
                            matrix[g, c, e, w, f, v, f] = value
    matrix = matrix.reshape(2, classes * 2 * waves * 4, waves * 4)
    return np.concatenate([matrix[0], matrix[1]], 1).astype(np.float32)


def split(values):
    high = values.astype(jnp.bfloat16)
    return high, (values - high.astype(jnp.float32)).astype(jnp.bfloat16)


def product(values, top, rest):
    high, low = split(values)
    return real_dot(high, top[...]) + (real_dot(low, top[...]) + real_dot(high, rest[...]))


def mirror(values):
    rows = values.shape[0]
    lane = lax.broadcasted_iota(jnp.int32, (rows, LANES), 1)
    back = (LANES - lane) % LANES
    tiles = [values[:, a * LANES:(a + 1) * LANES] for a in range(values.shape[1] // LANES)]
    many = len(tiles)
    out = []
    for a in range(many):
        turned = jnp.take_along_axis(tiles[many - 1 - a], back, axis=1)
        out.append(jnp.where(lane == 0, tiles[(many - a) % many], turned))
    return jnp.concatenate(out, 1) if many > 1 else out[0]


def to_waves(values, odd_top, odd_rest, even_top, even_rest):
    half = values.shape[1] // 2
    low, high = values[:, :half], mirror(values[:, half:])
    lane = lax.broadcasted_iota(jnp.int32, low.shape, 1)
    low = jnp.where(lane == 0, 0.0, low)
    return product(low + high, odd_top, odd_rest), product(low - high, even_top, even_rest)


def to_cells(odd, even, odd_top, odd_rest, even_top, even_rest):
    p, m = product(odd, odd_top, odd_rest), product(even, even_top, even_rest)
    return p + m, mirror(p - m)


def horizontal(wavenumber, length):
    return (aspect_ratio * 4.0 * np.sin(math.pi * wavenumber / length) ** 2).astype(np.float32)


def set_faces(thick, faces):
    total = faces.shape[0] - 1
    two = jnp.full((ROWS, LANES), 2.0, jnp.float32)
    faces[0] = two / (two * 0.0 + thick[0])
    faces[total] = two * 0.0

    def one(j, _):
        faces[j] = two / (two * 0.0 + (thick[j - 1] + thick[j]))
        return 0

    lax.fori_loop(1, total, one, 0, unroll=3)


def spread_face(tile, like):
    rows, lanes = like.shape
    wide = jnp.concatenate([tile] * (lanes // LANES), 1) if lanes > LANES else tile
    return jnp.concatenate([wide] * (rows // ROWS), 0) if rows > ROWS else wide


class Copies:
    def __init__(self, sems):
        self.sems, self.used = sems, 0

    def start(self, source, target):
        copy = pltpu.make_async_copy(source, target, self.sems.at[self.used])
        self.used += 1
        copy.start()
        return copy


def coefficients(levels, total, group, place, thick, faces, shifts, across, t_out, m_out, end_out, pair_out, far_out, lam, m_chip, f_chip, n_chip, u_chip, down_all, up_all):
    ky = lam.shape[0]
    span = 2 * levels
    chips = total // span
    chip = place[0] // 2
    start = chip * span
    upper = place[0] % 2 == 0
    own = (place[0] % 2) * levels
    for row in range(ky):
        lam[row:row + 1, :] = across[...] + shifts[row]

    def down_step(shift, j, f, r):
        m = spread_face(faces[j], r) * r
        f = shift * thick[j] + m * f
        return m, f, 1.0 / (spread_face(faces[j + 1], f) + f)

    def up_step(shift, j, phi, s):
        n = spread_face(faces[j + 1], s) * s
        u = n * phi
        phi = shift * thick[j] + u
        return n, u, phi, 1.0 / (spread_face(faces[j], phi) + phi)

    def part(g, _):
        here = pl.ds(pl.multiple_of(g * group, group), group)
        shift = lam[here]
        one = jnp.ones_like(shift)
        zero = jnp.zeros_like(shift)

        def down_chip(c, state):
            f, r = state
            product = one
            for i in range(span):
                m, f, r = down_step(shift, c * span + i, f, r)
                t_out[c * span + i, here] = m
                product = product * m
            down_all[c] = product
            return f, r

        def up_chip(back, state):
            phi, s = state
            c = chips - 1 - back
            product = one
            for i in range(span - 1, -1, -1):
                n, _, phi, s = up_step(shift, c * span + i, phi, s)
                t_out[c * span + i + 1, here] = n
                product = product * n
            up_all[c] = product
            return phi, s

        f, r = lax.fori_loop(0, chip, down_chip, (one, one))
        for i in range(span):
            m, f, r = down_step(shift, start + i, f, r)
            m_chip[i], f_chip[i] = m, f
        phi, s = lax.fori_loop(0, chips - 1 - chip, up_chip, (zero, zero))
        for i in range(span - 1, -1, -1):
            n, u, phi, s = up_step(shift, start + i, phi, s)
            n_chip[i], u_chip[i] = n, u

        for i in range(levels):
            t_out[start + i, here] = m_chip[i]
            t_out[start + levels + 1 + i, here] = n_chip[levels + i]
        t_out[start + levels, here] = jnp.where(upper, n_chip[levels - 1], m_chip[levels])
        for i in range(levels):
            m_out[i, here] = m_chip[own + i]
        last = own + levels - 1
        end_out[0, here] = n_chip[last]
        end_out[1, here] = 1.0 / (f_chip[last] + u_chip[last])
        end_out[2, here] = f_chip[own] + u_chip[own]
        for core in range(2):
            down, up = m_chip[core * levels], n_chip[core * levels]
            for i in range(1, levels):
                down = down * m_chip[core * levels + i]
                up = up * n_chip[core * levels + i]
            pair_out[core, here] = down
            pair_out[2 + core, here] = up
        above, below = [one], [one]
        for apart in range(1, chips - 1):
            above.append(above[-1] * jnp.where(chip >= apart, down_all[jnp.maximum(chip - apart, 0)], one))
            below.append(below[-1] * jnp.where(chip + apart < chips, up_all[jnp.minimum(chip + apart, chips - 1)], one))
        for apart in range(1, chips):
            far_out[apart - 1, here] = jnp.where(chip >= apart, above[apart - 1], below[chips - apart - 1])
        return 0

    lax.fori_loop(0, ky // group, part, 0)


def lane_sum(values):
    tiles = [values[:, t * LANES:(t + 1) * LANES] for t in range(values.shape[1] // LANES)]
    while len(tiles) > 1:
        tiles = [a + b for a, b in zip(tiles[0::2], tiles[1::2])] + tiles[len(tiles) // 2 * 2:]
    return tiles[0]


def front_kernel(levels, total, group, place, thick, shifts, across, sines, edge_mix, x0, x1, odd_top, odd_rest, even_top, even_rest, t_out, m_out, end_out, b_out, local_out, give_out, edge_out, sems, *scratch):
    across_v, sines_v, mix_v, x, ot, orest, et, er, t, m, end, pair, far, b, c_all, z_all, sums, edges, faces, lam, *work = scratch
    _, _, _, ky, size = x.shape
    first = place[0] * levels
    half = size // 2
    copies = Copies(sems)
    early = [copies.start(across, across_v)]
    fields = [copies.start(x0, x.at[0])]
    mats = [copies.start(source, target) for source, target in ((odd_top, ot), (odd_rest, orest), (even_top, et), (even_rest, er))]
    mats += [copies.start(sines, sines_v)]
    fields += [copies.start(x1, x.at[1])]
    late = [copies.start(edge_mix, mix_v)]
    set_faces(thick, faces)
    for copy in early:
        copy.wait()
    coefficients(levels, total, group, place, thick, faces, shifts, across_v, t, m, end, pair, far, lam, *work)
    outs = [copies.start(source, target) for source, target in ((t, t_out), (m, m_out), (end, end_out))]
    for copy in mats:
        copy.wait()
    lane = lax.broadcasted_iota(jnp.int32, (ROWS, LANES), 1)
    spot = jnp.where(lane == 0, size / 4.0, 0.0)
    core = place[0] % 2
    mine, other = (pl.ds(pl.multiple_of(start * (ky // 2), ROWS), ky // 2) for start in (core, 1 - core))
    outs.append(copies.start(pair.at[:, mine], local_out.at[pl.ds(8, 4)]))
    outs.append(copies.start(far.at[:, mine], local_out.at[pl.ds(12, far.shape[0])]))

    def put(f, j, here, values, height, own=None):
        odd, even = lane_sum(values[:, :half]) * height, lane_sum(values[:, half:]) * height
        if own is not None:
            odd, even = odd + own, even + own
        sums[f, 0, j, here] = odd
        sums[f, 1, j, here] = even

    for a in range(2):
        fields[a].wait()
        odd, even = to_waves(x[a].reshape(2 * levels * ky, size), ot, orest, et, er)
        for ri in range(2):
            for j in range(levels):
                rows = slice((ri * levels + j) * ky, (ri * levels + j + 1) * ky)
                scale = thick[first + j] if a == 0 else 1.0
                b[a, ri, j, :, :half] = odd[rows] * scale
                b[a, ri, j, :, half:] = even[rows] * scale
        outs.append(copies.start(b.at[a], b_out.at[a]))
        for ri in range(2):
            f = 2 * a + ri

            def tile(g, _):
                here = pl.ds(pl.multiple_of(g * ROWS, ROWS), ROWS)
                wave = sines_v[...]
                y = b[a, ri, 0, here]
                ys = [y]
                for j in range(1, levels):
                    y = b[a, ri, j, here] + m[j, here] * y
                    ys.append(y)
                c_all[a, ri, here] = y
                value = y * end[1, here]
                z_all[1, f, here] = value * wave
                for j in range(levels - 1, -1, -1):
                    if j < levels - 1:
                        value = m[j + 1, here] * (ys[j] * (0.5 * (thick[first + j] + thick[first + j + 1])) + value)
                    height = thick[first + j]
                    own = jnp.broadcast_to(x[a, ri, j, here, 0:1], (ROWS, LANES)) * (spot * height if a == 0 else spot)
                    put(f, first + j, here, value * wave, height, own)
                z_all[0, f, here] = value * wave
                c_all[a, 2 + ri, here] = value * end[2, here]
                return 0

            lax.fori_loop(0, ky // ROWS, tile, 0)
        outs.append(copies.start(c_all.at[a, :, mine], local_out.at[pl.ds(4 * a, 4)]))
        outs.append(copies.start(c_all.at[a, :, other], give_out.at[a]))

    def reach(g, _):
        here = pl.ds(pl.multiple_of(g * ROWS, ROWS), ROWS)

        def up(block, z):
            for i in range(levels):
                j = first - 1 - block * levels - i
                step = t[j + 1, here]
                z = [step * one for one in z]
                for f in range(4):
                    put(f, j, here, z[f], thick[j])
            return z

        def down(block, z):
            for i in range(levels):
                j = first + levels + block * levels + i
                step = t[j, here]
                z = [step * one for one in z]
                for f in range(4):
                    put(f, j, here, z[f], thick[j])
            return z

        lax.fori_loop(0, place[0], up, [z_all[0, f, here] for f in range(4)])
        lax.fori_loop(0, total // levels - 1 - place[0], down, [z_all[1, f, here] for f in range(4)])
        return 0

    lax.fori_loop(0, ky // ROWS, reach, 0)
    for copy in late:
        copy.wait()
    if edges.shape[0] > ky:
        edges[...] = jnp.zeros_like(edges)
    wide = 2 * total
    lane = lax.broadcasted_iota(jnp.int32, (ky, wide), 1) % total
    for f in range(4):
        both = [sums[f, way].reshape(total * ky, LANES) for way in range(2)]
        high, low = split(jnp.concatenate(both, 1))
        spread = (real_dot(high, mix_v[...]) + real_dot(low, mix_v[...])).reshape(total, ky, wide)
        line = spread[0]
        for j in range(1, total):
            line = jnp.where(lane == j, spread[j], line)
        edges[:ky, f, :] = line
    outs.append(copies.start(edges, edge_out))
    for copy in outs:
        copy.wait()


def front(place, thick, shifts, across, sines, rhs, cotangent, devices):
    _, levels, ky, size = rhs.shape
    total = thick.shape[0]
    chips = total // (2 * levels)
    group = min(2 * ROWS, ky)
    half = size // 2
    wide = 2 * total
    single = lambda *shape: pltpu.VMEM(shape, jnp.float32)
    tables = [(n, ky, size) for n in (total + 1, levels, 3, 4, chips - 1)]
    shapes = tables[:3] + [(2, 2, levels, ky, size), (11 + chips, ky // 2, size), (2, 4, ky // 2, size), (devices, 4, wide)]
    return pl.pallas_call(
        functools.partial(front_kernel, levels, total, group),
        in_specs=[in_smem] * 3 + [in_hbm] * 9,
        out_specs=[in_hbm] * len(shapes),
        out_shape=[jax.ShapeDtypeStruct(shape, jnp.float32) for shape in shapes],
        scratch_shapes=[
            pltpu.SemaphoreType.DMA((22,)),
            single(1, size),
            single(ROWS, size),
            pltpu.VMEM((2 * LANES, wide), jnp.bfloat16),
            single(2, 2, levels, ky, size),
            *[pltpu.VMEM((half, half), jnp.bfloat16)] * 4,
            *[single(*shape) for shape in tables],
            single(2, 2, levels, ky, size),
            single(2, 4, ky, size),
            single(2, 4, ky, size),
            single(4, 2, total, ky, LANES),
            single(devices, 4, wide),
            single(total + 1, ROWS, LANES),
            single(ky, size),
            *[single(2 * levels, group, size)] * 4,
            *[single(chips, group, size)] * 2,
        ],
        compiler_params=params,
        name="front",
    )(place, thick, shifts, across, sines, edge_matrix(size, total), rhs, cotangent, *half_sines(size))


def chip_kernel(chips, place, local, got, *refs):
    outs = refs[:chips - 1]
    sems, down_v, up_v = refs[chips - 1:]
    chip = place[0] // 2
    upper = place[0] % 2 == 0
    for a in range(2):
        for ri in range(2):
            sums = [(local[4 * a + 2 * way + ri], got[a, 2 * way + ri]) for way in range(2)]
            first, second = ([jnp.where(upper, *one[::turn]) for one in sums] for turn in (1, -1))
            down_v[2 * a + ri] = second[0] + local[9] * first[0]
            up_v[2 * a + ri] = first[1] + local[10] * second[1]
    for apart in range(1, chips):
        goes_down = chip + apart < chips
        sem = sems.at[apart - 1]

        @pl.when(goes_down)
        def _():
            pltpu.make_async_copy(down_v, outs[apart - 1], sem).start()

        @pl.when(jnp.logical_not(goes_down))
        def _():
            pltpu.make_async_copy(up_v, outs[apart - 1], sem).start()

    for apart in range(1, chips):
        pltpu.make_async_copy(down_v, outs[apart - 1], sems.at[apart - 1]).wait()


def chip_sums(place, local, got, chips):
    _, half, size = local.shape
    shape = (4, half, size)
    return pl.pallas_call(
        functools.partial(chip_kernel, chips),
        in_specs=[in_smem] + [in_vmem] * 2,
        out_specs=[in_hbm] * (chips - 1),
        out_shape=[jax.ShapeDtypeStruct(shape, jnp.float32)] * (chips - 1),
        scratch_shapes=[
            pltpu.SemaphoreType.DMA((chips - 1,)),
            pltpu.VMEM(shape, jnp.float32),
            pltpu.VMEM(shape, jnp.float32),
        ],
        compiler_params=small,
        cost_estimate=brief,
        name="chip_sums",
    )(place, local, got)


def join_kernel(chips, place, local, got, *refs):
    news = refs[:chips - 1]
    mine, theirs = refs[chips - 1:]
    chip = place[0] // 2
    upper = place[0] % 2 == 0
    for a in range(2):
        for ri in range(2):
            sums = [(local[4 * a + 2 * way + ri], got[a, 2 * way + ri]) for way in range(2)]
            first, second = ([jnp.where(upper, *one[::turn]) for one in sums] for turn in (1, -1))
            down = jnp.zeros(local.shape[1:], jnp.float32)
            up = down
            for apart in range(1, chips):
                term = local[11 + apart] * news[apart - 1][2 * a + ri]
                down = down + jnp.where(chip >= apart, term, 0.0)
                up = up + jnp.where(chip >= apart, 0.0, term)
            inner_up = second[1] + local[11] * up
            inner_down = first[0] + local[8] * down
            mine[a, 0, ri] = jnp.where(upper, down, inner_down)
            mine[a, 1, ri] = jnp.where(upper, inner_up, up)
            theirs[a, 0, ri] = jnp.where(upper, inner_down, down)
            theirs[a, 1, ri] = jnp.where(upper, up, inner_up)


def join(place, local, got, news):
    chips = len(news) + 1
    _, half, size = local.shape
    return pl.pallas_call(
        functools.partial(join_kernel, chips),
        in_specs=[in_smem] + [in_vmem] * (1 + chips),
        out_specs=[in_vmem] * 2,
        out_shape=[jax.ShapeDtypeStruct((2, 2, 2, half, size), jnp.float32)] * 2,
        compiler_params=small,
        cost_estimate=lengthy,
        name="join",
    )(place, local, got, *news)


def inverse_kernel(counts, my, thick, shifts, across, weights, out, faces, m_all, f_all, g_all):
    total = f_all.shape[0]
    classes = out.shape[0]
    ky = shifts.shape[0]
    starts = [sum(counts[:c]) for c in range(classes + 1)]
    set_faces(thick, faces)
    shift = across[...] + jnp.where(my[0] < ky, shifts[jnp.minimum(my[0], ky - 1)], 1.0)
    one = jnp.ones_like(shift)
    zero = jnp.zeros_like(shift)

    def step(j, state):
        f, r, phi, s = state
        m = spread_face(faces[j], r) * r
        f = shift * thick[j] + m * f
        r = 1.0 / (spread_face(faces[j + 1], f) + f)
        m_all[j] = m
        f_all[j] = f
        i = total - 1 - j
        u = spread_face(faces[i + 1], s) * s * phi
        phi = shift * thick[i] + u
        s = 1.0 / (spread_face(faces[i], phi) + phi)
        g_all[i] = u
        return f, r, phi, s

    lax.fori_loop(0, total, step, (one, one, zero, zero), unroll=4)
    weight = weights[...]

    def centre(j, _):
        g_all[j] = weight / (f_all[j] + g_all[j])
        return 0

    lax.fori_loop(0, total, centre, 0, unroll=8)
    wide = out.shape[2]
    sub = lax.broadcasted_iota(jnp.int32, (ROWS, LANES), 0)
    lane = lax.broadcasted_iota(jnp.int32, (ROWS, wide), 1)
    row = lax.broadcasted_iota(jnp.int32, (ROWS, wide), 0)
    line = lambda ref, j, t: jnp.broadcast_to(ref[j, t:t + 1, :], (ROWS, LANES))

    def put(j, z, sums):
        new = []
        for c in range(classes):
            tiles = z[starts[c]:starts[c + 1]]
            total_tile = tiles[0]
            for tile in tiles[1:]:
                total_tile = total_tile + tile
            value = jnp.sum(total_tile, axis=1, keepdims=True)
            new.append(jnp.where(lane == j, value, sums[c]))
        return new

    for base in range(0, total, ROWS):
        z = [jnp.zeros((ROWS, LANES), jnp.float32)] * (starts[-1])
        sums = [jnp.zeros((ROWS, wide), jnp.float32)] * classes
        for i in range(ROWS - 1, -1, -1):
            j = base + i
            for t in range(starts[-1]):
                moved = z[t] * line(m_all, j + 1, t) if i < ROWS - 1 else z[t]
                z[t] = jnp.where(sub == i, line(g_all, j, t), moved)
            sums = put(j, z, sums)

        def above(back, state):
            z, sums = state
            for i in range(ROWS):
                j = base - 1 - back * ROWS - i
                z = [z[t] * line(m_all, j + 1, t) for t in range(starts[-1])]
                sums = put(j, z, sums)
            return z, sums

        if base:
            z, sums = lax.fori_loop(0, base // ROWS, above, (z, sums))
        for c in range(classes):
            out[c, base:base + ROWS, :] = sums[c] * jnp.where(lane == base + row, 0.5, 1.0)


def inverse_sums(my, thick, shifts, waves, size):
    total = thick.shape[0]
    classes = waves // 2 + 1
    lines, weights, counts = [], [], []
    for c in range(classes):
        k = c + waves * np.arange(size)
        weight = np.ones(size)
        if c in (0, waves // 2):
            partner = (waves * size - k) % (waves * size)
            weight = np.where(k < partner, 2.0, 1.0)[k <= partner]
            k = k[k <= partner]
        spare = -len(k) % LANES
        counts.append((len(k) + spare) // LANES)
        lines.append(np.pad(k, (0, spare)))
        weights.append(np.pad(weight, (0, spare)))
    spare = -sum(counts) % ROWS * LANES
    k = np.pad(np.concatenate(lines), (0, spare)).reshape(-1, LANES)
    weight = np.pad(np.concatenate(weights), (0, spare)).reshape(-1, LANES).astype(np.float32)
    across = horizontal(k, waves * size)
    wide = -(-total // LANES) * LANES
    return pl.pallas_call(
        functools.partial(inverse_kernel, counts),
        in_specs=[in_smem] * 3 + [in_vmem] * 2,
        out_shape=jax.ShapeDtypeStruct((classes, total, wide), jnp.float32),
        scratch_shapes=[pltpu.VMEM((total + 1, ROWS, LANES), jnp.float32)] + [pltpu.VMEM((total,) + across.shape, jnp.float32)] * 3,
        compiler_params=small,
        cost_estimate=lengthy,
        name="inverse_sums",
    )(my, thick, shifts, across, weight)


def interface_kernel(waves, matrices, edges, inverse, out):
    devices, _, wide = edges.shape
    total = wide // 2
    rows = 4 * waves
    lines = []
    for w in range(waves):
        line = edges[w]
        for d in range(1, devices // waves):
            line = line + edges[d * waves + w]
        lines.append(line)
    lines = jnp.concatenate(lines, 0)
    lines = jnp.concatenate([lines[:, :total], lines[:, total:]], 0)
    mixed = exact_dot(matrices[...], lines, NN)
    classes = inverse.shape[0]
    parts = jnp.concatenate([mixed[c * 2 * rows:(c + 1) * 2 * rows] for c in range(classes)], 1)
    squares = [inverse[c][:, :total] for c in range(classes)]
    result = exact_dot(parts, jnp.concatenate(squares, 0), NN) + exact_dot(parts, jnp.concatenate(squares, 1), NT)
    result = jnp.concatenate([result[:rows], result[rows:]], 1)
    for w in range(waves):
        line = result[4 * w:4 * w + 4]
        for d in range(devices // waves):
            out[d * waves + w] = line


def interface(edges, inverse, waves, size):
    return pl.pallas_call(
        functools.partial(interface_kernel, waves),
        in_specs=[in_vmem] * 3,
        out_specs=in_vmem,
        out_shape=jax.ShapeDtypeStruct(edges.shape, jnp.float32),
        compiler_params=small,
        name="interface",
    )(interface_matrices(waves, size), edges, inverse)


def back_kernel(levels, total, place, thick, values_v, spread_v, t, mine, theirs, sines_v, b, m_v, end_v, ot, orest, et, er, out0, out1, sems, t_v, b_v, ends, picked, u_all, q_all, out_v):
    _, _, _, ky, size = b_v.shape
    first = place[0] * levels
    half = size // 2
    many = half // LANES
    core = place[0] % 2
    copies = Copies(sems)
    table = copies.start(t, t_v)
    fields = [copies.start(b.at[a], b_v.at[a]) for a in range(2)]
    here, there = (pl.ds(pl.multiple_of(start * (ky // 2), ROWS), ky // 2) for start in (core, 1 - core))
    lane = lax.broadcasted_iota(jnp.int32, (ky, 2 * total), 1)
    for f in range(4):
        parts = [part.astype(jnp.float32) for part in split(values_v[:ky, f, :])]
        for j in range(total):
            spot = (lane == j) | (lane == total + j)
            for p in range(2):
                picked[p, j * ky:(j + 1) * ky, :] = jnp.where(spot, parts[p], 0.0).astype(jnp.bfloat16)
        u_all[f] = (real_dot(picked[0], spread_v[...]) + real_dot(picked[1], spread_v[...])).reshape(total, ky, 2 * LANES)
    table.wait()
    ends[:, :, :, here] = mine[...]
    ends[:, :, :, there] = theirs[...]

    def source(f, j, here):
        pair = u_all[f, j, here] * thick[j]
        return jnp.concatenate([pair[:, :LANES]] * many + [pair[:, LANES:]] * many, 1)

    def sweep(g, _):
        here = pl.ds(pl.multiple_of(g * ROWS, ROWS), ROWS)

        def from_above(block, y):
            for i in range(levels):
                j = block * levels + i
                step = t_v[j, here]
                y = [step * y[f] + source(f, j, here) for f in range(4)]
            return y

        def from_below(block, y):
            for i in range(levels):
                j = total - 1 - block * levels - i
                step = t_v[j + 1, here]
                y = [step * y[f] + source(f, j, here) for f in range(4)]
            return y

        zero = [jnp.zeros((ROWS, size), jnp.float32)] * 4
        wave = sines_v[...]
        for way, y in (
            (0, lax.fori_loop(0, place[0], from_above, zero)),
            (1, lax.fori_loop(0, total // levels - 1 - place[0], from_below, zero)),
        ):
            for f in range(4):
                ends[f // 2, way, f % 2, here] += wave * y[f]
        return 0

    lax.fori_loop(0, ky // ROWS, sweep, 0)
    rows = 2 * levels * ky
    lane = lax.broadcasted_iota(jnp.int32, (ky, LANES), 1)
    outs = []
    for a in range(2):
        fields[a].wait()

        def tile(g, _):
            here = pl.ds(pl.multiple_of(g * ROWS, ROWS), ROWS)
            wave = sines_v[...]
            for ri in range(2):
                y = ends[a, 0, ri, here]
                ys = []
                for j in range(levels):
                    y = b_v[a, ri, j, here] + wave * source(2 * a + ri, first + j, here) + m_v[j, here] * y
                    ys.append(y)
                value = (y + end_v[0, here] * ends[a, 1, ri, here]) * end_v[1, here]
                q_all[ri, levels - 1, here] = value
                for j in range(levels - 2, -1, -1):
                    value = m_v[j + 1, here] * (ys[j] * (0.5 * (thick[first + j] + thick[first + j + 1])) + value)
                    q_all[ri, j, here] = value
            return 0

        lax.fori_loop(0, ky // ROWS, tile, 0)
        low, high = to_cells(
            q_all[:, :, :, :half].reshape(rows, half), q_all[:, :, :, half:].reshape(rows, half), ot, orest, et, er
        )
        for ri in range(2):
            for j in range(levels):
                height = thick[first + j] if a else 1.0
                here = slice((ri * levels + j) * ky, (ri * levels + j + 1) * ky)
                u = u_all[2 * a + ri, first + j]
                u = (u[:, :LANES] + u[:, LANES:]) * (0.5 * height)
                if many > 1:
                    out_v[a, ri, j, :, LANES:half] = low[here, LANES:] * height
                out_v[a, ri, j, :, :LANES] = jnp.where(lane == 0, u, low[here, :LANES] * height)
                out_v[a, ri, j, :, half:] = high[here] * height
            outs.append(copies.start(out_v.at[a, ri], (out0, out1)[a].at[ri]))
    for copy in outs:
        copy.wait()


def back(place, thick, values, sines, t, m, end, b, mine, theirs):
    _, _, levels, ky, size = b.shape
    total = t.shape[0] - 1
    half = size // 2
    single = lambda *shape: pltpu.VMEM(shape, jnp.float32)
    return pl.pallas_call(
        functools.partial(back_kernel, levels, total),
        in_specs=[in_smem] * 2 + [in_vmem] * 2 + [in_hbm] + [in_vmem] * 3 + [in_hbm] + [in_vmem] * 6,
        out_specs=[in_hbm] * 2,
        out_shape=[jax.ShapeDtypeStruct((2, levels, ky, size), jnp.float32)] * 2,
        scratch_shapes=[
            pltpu.SemaphoreType.DMA((7,)),
            single(*t.shape),
            single(*b.shape),
            single(2, 2, 2, ky, size),
            pltpu.VMEM((2, total * ky, 2 * total), jnp.bfloat16),
            single(4, total, ky, 2 * LANES),
            single(2, levels, ky, size),
            single(2, 2, levels, ky, size),
        ],
        compiler_params=medium,
        name="back",
    )(place, thick, values, spread_matrix(total), t, mine, theirs, sines, b, m, end, *half_sines(size, True, 2.0 / size))


def shards(rhs, cotangent, thickness, ky_shift):
    waves = lax.axis_size("wave")
    count = lax.axis_size("depth")
    depth_pos = lax.axis_index("depth")
    wave_pos = lax.axis_index("wave")
    _, levels, ky, size = rhs.shape
    devices = waves * count
    chips = count // 2
    place = depth_pos.astype(jnp.int32).reshape(1)

    def across(a):
        return lax.ppermute(a, "depth", [(d, d ^ 1) for d in range(count)])

    def along(a, apart):
        return lax.ppermute(a, "depth", [(d, (d + 2 * apart) % count) for d in range(count)])

    def everywhere(a):
        return lax.all_to_all(a, ("depth", "wave"), split_axis=0, concat_axis=0, tiled=True)

    order = wave_order(size)
    sines = np.broadcast_to(np.sin(np.pi * order / size)[None, :], (ROWS, size)).astype(np.float32)
    across_k = horizontal(order, 2 * size)[None, :]
    t, m, end, b, local, give, edges = front(
        place, thickness, ky_shift, across_k, sines, rhs, cotangent, devices
    )

    my = (depth_pos * waves + wave_pos).astype(jnp.int32).reshape(1)
    got = across(give)
    edges = everywhere(edges)
    sums = chip_sums(place, local, got, chips)
    news = [along(sums[apart - 1], apart) for apart in range(1, chips)]
    inverse = inverse_sums(my, thickness, ky_shift, waves, size)
    values = interface(edges, inverse, waves, size)
    values = everywhere(values)
    news, _ = lax.optimization_barrier((news, values))
    mine, theirs = join(place, local, got, news)
    return back(place, thickness, values, sines, t, m, end, b, mine, across(theirs))


def solution(mesh):
    spec = P(None, "depth", None, "wave")
    return jax.shard_map(shards, mesh=mesh, in_specs=(spec, spec, P(), P()), out_specs=(spec, spec), check_vma=False)
```

```python
import functools
import math

import jax
import jax.numpy as jnp
import numpy as np
from jax import lax
from jax.experimental import pallas as pl
from jax.experimental.pallas import tpu as pltpu
from jax.sharding import PartitionSpec as P

aspect_ratio = 1.0
LANES = 128
ROWS = 8
VMEM_BYTES = 56 * 1024 * 1024
real_dot = functools.partial(jnp.dot, preferred_element_type=jnp.float32)
exact_dot = functools.partial(lax.dot_general, precision=lax.Precision.HIGHEST, preferred_element_type=jnp.float32)
NN = (((1,), (0,)), ((), ()))
NT = (((1,), (1,)), ((), ()))
in_smem = pl.BlockSpec(memory_space=pltpu.SMEM)
in_hbm = pl.BlockSpec(memory_space=pl.ANY)
in_vmem = pl.BlockSpec(memory_space=pltpu.VMEM)
params = pltpu.CompilerParams(vmem_limit_bytes=VMEM_BYTES)
small = pltpu.CompilerParams(vmem_limit_bytes=12 * 1024 * 1024)
medium = pltpu.CompilerParams(vmem_limit_bytes=46 * 1024 * 1024)
brief = pl.CostEstimate(flops=1, bytes_accessed=1, transcendentals=0)
lengthy = pl.CostEstimate(flops=20_000_000_000, bytes_accessed=40_000_000, transcendentals=0)


def wave_order(size):
    return np.concatenate([np.arange(1, size, 2), np.arange(0, size, 2)])


def half_sines(size, back=False, scale=1.0):
    half = size // 2
    place = np.arange(half)
    place[0] = half
    parts = []
    for waves in (np.arange(1, size, 2), np.arange(0, size, 2)):
        matrix = np.sin(np.pi * (np.outer(place, waves) % (2 * size)) / size)
        if waves[0] == 0:
            matrix[0] = 0.0
            matrix[:, 0] = 0.0
        matrix = (matrix.T if back else matrix).astype(np.float32) * np.float32(scale)
        top = matrix.astype(jnp.bfloat16)
        parts += [top, (matrix - top.astype(np.float32)).astype(jnp.bfloat16)]
    return parts


def edge_matrix(size, total):
    matrix = np.full((2 * LANES, 2 * total), 2.0 / size, np.float32)
    matrix[LANES:, total:] = -2.0 / size
    return matrix.astype(jnp.bfloat16)


def spread_matrix(total):
    matrix = np.ones((2 * total, 2 * LANES), np.float32)
    matrix[total:, LANES:] = -1.0
    return matrix.astype(jnp.bfloat16)


def interface_matrices(waves, size):
    classes = waves // 2 + 1
    matrix = np.zeros((2, classes, 2, waves, 4, waves, 4))
    for c in range(classes):
        weight = (1.0 if c in (0, waves // 2) else 2.0) / (size * waves)
        for w in range(waves):
            for e in range(2):
                for v in range(waves):
                    for g in range(2):
                        value = weight * math.cos(2.0 * math.pi * (c * (w + e - v - g) % waves) / waves)
                        for f in range(4):
                            matrix[g, c, e, w, f, v, f] = value
    matrix = matrix.reshape(2, classes * 2 * waves * 4, waves * 4)
    return np.concatenate([matrix[0], matrix[1]], 1).astype(np.float32)


def split(values):
    high = values.astype(jnp.bfloat16)
    return high, (values - high.astype(jnp.float32)).astype(jnp.bfloat16)


def product(values, top, rest):
    high, low = split(values)
    return real_dot(high, top[...]) + (real_dot(low, top[...]) + real_dot(high, rest[...]))


def mirror(values):
    rows = values.shape[0]
    lane = lax.broadcasted_iota(jnp.int32, (rows, LANES), 1)
    back = (LANES - lane) % LANES
    tiles = [values[:, a * LANES:(a + 1) * LANES] for a in range(values.shape[1] // LANES)]
    many = len(tiles)
    out = []
    for a in range(many):
        turned = jnp.take_along_axis(tiles[many - 1 - a], back, axis=1)
        out.append(jnp.where(lane == 0, tiles[(many - a) % many], turned))
    return jnp.concatenate(out, 1) if many > 1 else out[0]


def to_waves(values, odd_top, odd_rest, even_top, even_rest):
    half = values.shape[1] // 2
    low, high = values[:, :half], mirror(values[:, half:])
    lane = lax.broadcasted_iota(jnp.int32, low.shape, 1)
    low = jnp.where(lane == 0, 0.0, low)
    return product(low + high, odd_top, odd_rest), product(low - high, even_top, even_rest)


def to_cells(odd, even, odd_top, odd_rest, even_top, even_rest):
    p, m = product(odd, odd_top, odd_rest), product(even, even_top, even_rest)
    return p + m, mirror(p - m)


def horizontal(wavenumber, length):
    return (aspect_ratio * 4.0 * np.sin(math.pi * wavenumber / length) ** 2).astype(np.float32)


def set_faces(thick, faces):
    total = faces.shape[0] - 1
    two = jnp.full((ROWS, LANES), 2.0, jnp.float32)
    faces[0] = two / (two * 0.0 + thick[0])
    faces[total] = two * 0.0

    def one(j, _):
        faces[j] = two / (two * 0.0 + (thick[j - 1] + thick[j]))
        return 0

    lax.fori_loop(1, total, one, 0, unroll=3)


def spread_face(tile, like):
    rows, lanes = like.shape
    wide = jnp.concatenate([tile] * (lanes // LANES), 1) if lanes > LANES else tile
    return jnp.concatenate([wide] * (rows // ROWS), 0) if rows > ROWS else wide


class Copies:
    def __init__(self, sems):
        self.sems, self.used = sems, 0

    def start(self, source, target):
        copy = pltpu.make_async_copy(source, target, self.sems.at[self.used])
        self.used += 1
        copy.start()
        return copy


def coefficients(levels, total, group, place, thick, faces, shifts, across, t_out, m_out, end_out, pair_out, far_out, lam, m_chip, f_chip, n_chip, u_chip, down_all, up_all):
    ky = lam.shape[0]
    span = 2 * levels
    chips = total // span
    chip = place[0] // 2
    start = chip * span
    upper = place[0] % 2 == 0
    own = (place[0] % 2) * levels
    for row in range(ky):
        lam[row:row + 1, :] = across[...] + shifts[row]

    def down_step(shift, j, f, r):
        m = spread_face(faces[j], r) * r
        f = shift * thick[j] + m * f
        return m, f, 1.0 / (spread_face(faces[j + 1], f) + f)

    def up_step(shift, j, phi, s):
        n = spread_face(faces[j + 1], s) * s
        u = n * phi
        phi = shift * thick[j] + u
        return n, u, phi, 1.0 / (spread_face(faces[j], phi) + phi)

    def part(g, _):
        here = pl.ds(pl.multiple_of(g * group, group), group)
        shift = lam[here]
        one = jnp.ones_like(shift)
        zero = jnp.zeros_like(shift)

        def down_chip(c, state):
            f, r = state
            product = one
            for i in range(span):
                m, f, r = down_step(shift, c * span + i, f, r)
                t_out[c * span + i, here] = m
                product = product * m
            down_all[c] = product
            return f, r

        def up_chip(back, state):
            phi, s = state
            c = chips - 1 - back
            product = one
            for i in range(span - 1, -1, -1):
                n, _, phi, s = up_step(shift, c * span + i, phi, s)
                t_out[c * span + i + 1, here] = n
                product = product * n
            up_all[c] = product
            return phi, s

        f, r = lax.fori_loop(0, chip, down_chip, (one, one))
        for i in range(span):
            m, f, r = down_step(shift, start + i, f, r)
            m_chip[i], f_chip[i] = m, f
        phi, s = lax.fori_loop(0, chips - 1 - chip, up_chip, (zero, zero))
        for i in range(span - 1, -1, -1):
            n, u, phi, s = up_step(shift, start + i, phi, s)
            n_chip[i], u_chip[i] = n, u

        for i in range(levels):
            t_out[start + i, here] = m_chip[i]
            t_out[start + levels + 1 + i, here] = n_chip[levels + i]
        t_out[start + levels, here] = jnp.where(upper, n_chip[levels - 1], m_chip[levels])
        for i in range(levels):
            m_out[i, here] = m_chip[own + i]
        last = own + levels - 1
        end_out[0, here] = n_chip[last]
        end_out[1, here] = 1.0 / (f_chip[last] + u_chip[last])
        end_out[2, here] = f_chip[own] + u_chip[own]
        for core in range(2):
            down, up = m_chip[core * levels], n_chip[core * levels]
            for i in range(1, levels):
                down = down * m_chip[core * levels + i]
                up = up * n_chip[core * levels + i]
            pair_out[core, here] = down
            pair_out[2 + core, here] = up
        above, below = [one], [one]
        for apart in range(1, chips - 1):
            above.append(above[-1] * jnp.where(chip >= apart, down_all[jnp.maximum(chip - apart, 0)], one))
            below.append(below[-1] * jnp.where(chip + apart < chips, up_all[jnp.minimum(chip + apart, chips - 1)], one))
        for apart in range(1, chips):
            far_out[apart - 1, here] = jnp.where(chip >= apart, above[apart - 1], below[chips - apart - 1])
        return 0

    lax.fori_loop(0, ky // group, part, 0)


def lane_sum(values):
    tiles = [values[:, t * LANES:(t + 1) * LANES] for t in range(values.shape[1] // LANES)]
    while len(tiles) > 1:
        tiles = [a + b for a, b in zip(tiles[0::2], tiles[1::2])] + tiles[len(tiles) // 2 * 2:]
    return tiles[0]


def front_kernel(levels, total, group, place, thick, shifts, across, sines, edge_mix, x0, x1, odd_top, odd_rest, even_top, even_rest, t_out, m_out, end_out, b_out, local_out, give_out, edge_out, sems, *scratch):
    across_v, sines_v, mix_v, x, ot, orest, et, er, t, m, end, pair, far, b, c_all, z_all, sums, edges, faces, lam, *work = scratch
    _, _, _, ky, size = x.shape
    first = place[0] * levels
    half = size // 2
    copies = Copies(sems)
    early = [copies.start(across, across_v)]
    fields = [copies.start(x0, x.at[0])]
    mats = [copies.start(source, target) for source, target in ((odd_top, ot), (odd_rest, orest), (even_top, et), (even_rest, er))]
    mats += [copies.start(sines, sines_v)]
    fields += [copies.start(x1, x.at[1])]
    late = [copies.start(edge_mix, mix_v)]
    set_faces(thick, faces)
    for copy in early:
        copy.wait()
    coefficients(levels, total, group, place, thick, faces, shifts, across_v, t, m, end, pair, far, lam, *work)
    outs = [copies.start(source, target) for source, target in ((t, t_out), (m, m_out), (end, end_out))]
    for copy in mats:
        copy.wait()
    lane = lax.broadcasted_iota(jnp.int32, (ROWS, LANES), 1)
    spot = jnp.where(lane == 0, size / 4.0, 0.0)
    core = place[0] % 2
    mine, other = (pl.ds(pl.multiple_of(start * (ky // 2), ROWS), ky // 2) for start in (core, 1 - core))
    outs.append(copies.start(pair.at[:, mine], local_out.at[pl.ds(8, 4)]))
    outs.append(copies.start(far.at[:, mine], local_out.at[pl.ds(12, far.shape[0])]))

    def put(f, j, here, values, height, own=None):
        odd, even = lane_sum(values[:, :half]) * height, lane_sum(values[:, half:]) * height
        if own is not None:
            odd, even = odd + own, even + own
        sums[f, 0, j, here] = odd
        sums[f, 1, j, here] = even

    for a in range(2):
        fields[a].wait()
        odd, even = to_waves(x[a].reshape(2 * levels * ky, size), ot, orest, et, er)
        for ri in range(2):
            for j in range(levels):
                rows = slice((ri * levels + j) * ky, (ri * levels + j + 1) * ky)
                scale = thick[first + j] if a == 0 else 1.0
                b[a, ri, j, :, :half] = odd[rows] * scale
                b[a, ri, j, :, half:] = even[rows] * scale
        outs.append(copies.start(b.at[a], b_out.at[a]))
        for ri in range(2):
            f = 2 * a + ri

            def tile(g, _):
                here = pl.ds(pl.multiple_of(g * ROWS, ROWS), ROWS)
                wave = sines_v[...]
                y = b[a, ri, 0, here]
                ys = [y]
                for j in range(1, levels):
                    y = b[a, ri, j, here] + m[j, here] * y
                    ys.append(y)
                c_all[a, ri, here] = y
                value = y * end[1, here]
                z_all[1, f, here] = value * wave
                for j in range(levels - 1, -1, -1):
                    if j < levels - 1:
                        value = m[j + 1, here] * (ys[j] * (0.5 * (thick[first + j] + thick[first + j + 1])) + value)
                    height = thick[first + j]
                    own = jnp.broadcast_to(x[a, ri, j, here, 0:1], (ROWS, LANES)) * (spot * height if a == 0 else spot)
                    put(f, first + j, here, value * wave, height, own)
                z_all[0, f, here] = value * wave
                c_all[a, 2 + ri, here] = value * end[2, here]
                return 0

            lax.fori_loop(0, ky // ROWS, tile, 0)
        outs.append(copies.start(c_all.at[a, :, mine], local_out.at[pl.ds(4 * a, 4)]))
        outs.append(copies.start(c_all.at[a, :, other], give_out.at[a]))

    def reach(g, _):
        here = pl.ds(pl.multiple_of(g * ROWS, ROWS), ROWS)

        def up(block, z):
            for i in range(levels):
                j = first - 1 - block * levels - i
                step = t[j + 1, here]
                z = [step * one for one in z]
                for f in range(4):
                    put(f, j, here, z[f], thick[j])
            return z

        def down(block, z):
            for i in range(levels):
                j = first + levels + block * levels + i
                step = t[j, here]
                z = [step * one for one in z]
                for f in range(4):
                    put(f, j, here, z[f], thick[j])
            return z

        lax.fori_loop(0, place[0], up, [z_all[0, f, here] for f in range(4)])
        lax.fori_loop(0, total // levels - 1 - place[0], down, [z_all[1, f, here] for f in range(4)])
        return 0

    lax.fori_loop(0, ky // ROWS, reach, 0)
    for copy in late:
        copy.wait()
    if edges.shape[0] > ky:
        edges[...] = jnp.zeros_like(edges)
    wide = 2 * total
    lane = lax.broadcasted_iota(jnp.int32, (ky, wide), 1) % total
    for f in range(4):
        both = [sums[f, way].reshape(total * ky, LANES) for way in range(2)]
        high, low = split(jnp.concatenate(both, 1))
        spread = (real_dot(high, mix_v[...]) + real_dot(low, mix_v[...])).reshape(total, ky, wide)
        line = spread[0]
        for j in range(1, total):
            line = jnp.where(lane == j, spread[j], line)
        edges[:ky, f, :] = line
    outs.append(copies.start(edges, edge_out))
    for copy in outs:
        copy.wait()


def front(place, thick, shifts, across, sines, rhs, cotangent, devices):
    _, levels, ky, size = rhs.shape
    total = thick.shape[0]
    chips = total // (2 * levels)
    group = min(2 * ROWS, ky)
    half = size // 2
    wide = 2 * total
    single = lambda *shape: pltpu.VMEM(shape, jnp.float32)
    tables = [(n, ky, size) for n in (total + 1, levels, 3, 4, chips - 1)]
    shapes = tables[:3] + [(2, 2, levels, ky, size), (11 + chips, ky // 2, size), (2, 4, ky // 2, size), (devices, 4, wide)]
    return pl.pallas_call(
        functools.partial(front_kernel, levels, total, group),
        in_specs=[in_smem] * 3 + [in_hbm] * 9,
        out_specs=[in_hbm] * len(shapes),
        out_shape=[jax.ShapeDtypeStruct(shape, jnp.float32) for shape in shapes],
        scratch_shapes=[
            pltpu.SemaphoreType.DMA((22,)),
            single(1, size),
            single(ROWS, size),
            pltpu.VMEM((2 * LANES, wide), jnp.bfloat16),
            single(2, 2, levels, ky, size),
            *[pltpu.VMEM((half, half), jnp.bfloat16)] * 4,
            *[single(*shape) for shape in tables],
            single(2, 2, levels, ky, size),
            single(2, 4, ky, size),
            single(2, 4, ky, size),
            single(4, 2, total, ky, LANES),
            single(devices, 4, wide),
            single(total + 1, ROWS, LANES),
            single(ky, size),
            *[single(2 * levels, group, size)] * 4,
            *[single(chips, group, size)] * 2,
        ],
        compiler_params=params,
        name="front",
    )(place, thick, shifts, across, sines, edge_matrix(size, total), rhs, cotangent, *half_sines(size))


def chip_kernel(chips, place, local, got, *refs):
    outs = refs[:chips - 1]
    sems, down_v, up_v = refs[chips - 1:]
    chip = place[0] // 2
    upper = place[0] % 2 == 0
    for a in range(2):
        for ri in range(2):
            sums = [(local[4 * a + 2 * way + ri], got[a, 2 * way + ri]) for way in range(2)]
            first, second = ([jnp.where(upper, *one[::turn]) for one in sums] for turn in (1, -1))
            down_v[2 * a + ri] = second[0] + local[9] * first[0]
            up_v[2 * a + ri] = first[1] + local[10] * second[1]
    for apart in range(1, chips):
        goes_down = chip + apart < chips
        sem = sems.at[apart - 1]

        @pl.when(goes_down)
        def _():
            pltpu.make_async_copy(down_v, outs[apart - 1], sem).start()

        @pl.when(jnp.logical_not(goes_down))
        def _():
            pltpu.make_async_copy(up_v, outs[apart - 1], sem).start()

    for apart in range(1, chips):
        pltpu.make_async_copy(down_v, outs[apart - 1], sems.at[apart - 1]).wait()


def chip_sums(place, local, got, chips):
    _, half, size = local.shape
    shape = (4, half, size)
    return pl.pallas_call(
        functools.partial(chip_kernel, chips),
        in_specs=[in_smem] + [in_vmem] * 2,
        out_specs=[in_hbm] * (chips - 1),
        out_shape=[jax.ShapeDtypeStruct(shape, jnp.float32)] * (chips - 1),
        scratch_shapes=[
            pltpu.SemaphoreType.DMA((chips - 1,)),
            pltpu.VMEM(shape, jnp.float32),
            pltpu.VMEM(shape, jnp.float32),
        ],
        compiler_params=small,
        cost_estimate=brief,
        name="chip_sums",
    )(place, local, got)


def pair_kernel(place, local, got, first_out, second_out):
    even = (place[0] // 2) % 2 == 0
    upper = place[0] % 2 == 0
    for a in range(2):
        for ri in range(2):
            sums = [(local[4 * a + 2 * way + ri], got[a, 2 * way + ri]) for way in range(2)]
            first, second = ([jnp.where(upper, *one[::turn]) for one in sums] for turn in (1, -1))
            down = second[0] + local[9] * first[0]
            up = first[1] + local[10] * second[1]
            first_out[2 * a + ri] = jnp.where(even, down, up)
            second_out[2 * a + ri] = jnp.where(even, up, down)


def pair_sums(place, local, got):
    shape = jax.ShapeDtypeStruct((4,) + local.shape[1:], jnp.float32)
    return pl.pallas_call(
        pair_kernel,
        in_specs=[in_smem] + [in_vmem] * 2,
        out_specs=[in_vmem] * 2,
        out_shape=[shape] * 2,
        compiler_params=small,
        cost_estimate=brief,
        name="pair_sums",
    )(place, local, got)


def grow_kernel(place, local, second, near, out):
    even = (place[0] // 2) % 2 == 0
    factor = jnp.where(even, local[10] * local[11], local[8] * local[9])
    for i in range(4):
        out[i] = second[i] + factor * near[i]


def grow(place, local, second, near):
    return pl.pallas_call(
        grow_kernel,
        in_specs=[in_smem] + [in_vmem] * 3,
        out_specs=in_vmem,
        out_shape=jax.ShapeDtypeStruct(second.shape, jnp.float32),
        compiler_params=small,
        cost_estimate=brief,
        name="grow",
    )(place, local, second, near)


def join_kernel(chips, place, local, got, *refs):
    news = refs[:chips - 1]
    mine, theirs = refs[chips - 1:]
    chip = place[0] // 2
    upper = place[0] % 2 == 0
    for a in range(2):
        for ri in range(2):
            sums = [(local[4 * a + 2 * way + ri], got[a, 2 * way + ri]) for way in range(2)]
            first, second = ([jnp.where(upper, *one[::turn]) for one in sums] for turn in (1, -1))
            down = jnp.zeros(local.shape[1:], jnp.float32)
            up = down
            if chips == 4:
                near, middle, outer = (one[2 * a + ri] for one in news)
                outer = near + local[13] * outer
                down = jnp.where(chip == 0, 0.0, jnp.where(chip == 1, near, jnp.where(chip == 2, middle, outer)))
                up = jnp.where(chip == 3, 0.0, jnp.where(chip == 2, near, jnp.where(chip == 1, middle, outer)))
            for apart in range(1, chips if chips != 4 else 0):
                term = local[11 + apart] * news[apart - 1][2 * a + ri]
                down = down + jnp.where(chip >= apart, term, 0.0)
                up = up + jnp.where(chip >= apart, 0.0, term)
            inner_up = second[1] + local[11] * up
            inner_down = first[0] + local[8] * down
            mine[a, 0, ri] = jnp.where(upper, down, inner_down)
            mine[a, 1, ri] = jnp.where(upper, inner_up, up)
            theirs[a, 0, ri] = jnp.where(upper, inner_down, down)
            theirs[a, 1, ri] = jnp.where(upper, up, inner_up)


def join(place, local, got, news):
    chips = len(news) + 1
    _, half, size = local.shape
    return pl.pallas_call(
        functools.partial(join_kernel, chips),
        in_specs=[in_smem] + [in_vmem] * (1 + chips),
        out_specs=[in_vmem] * 2,
        out_shape=[jax.ShapeDtypeStruct((2, 2, 2, half, size), jnp.float32)] * 2,
        compiler_params=small,
        cost_estimate=lengthy,
        name="join",
    )(place, local, got, *news)


def inverse_kernel(counts, my, thick, shifts, across, weights, out, faces, m_all, g_all, d_all, f_all, e_all):
    total = f_all.shape[0]
    classes = out.shape[0]
    ky = shifts.shape[0]
    starts = [sum(counts[:c]) for c in range(classes + 1)]
    set_faces(thick, faces)
    shift = across[...] + jnp.where(my[0] < ky, shifts[jnp.minimum(my[0], ky - 1)], 1.0)
    one = jnp.ones_like(shift)
    zero = jnp.zeros_like(shift)

    def steps(block, state):
        n, d, p, e = state
        for i in range(ROWS):
            j = block * ROWS + i
            q = spread_face(faces[j], n)
            a = q * d
            d = a + n
            n = (shift * thick[j]) * d + q * n
            m_all[j], d_all[j], f_all[j] = a, d, n
            j = total - 1 - j
            q = spread_face(faces[j + 1], p)
            w = q * p
            e = q * e + p
            p = (shift * thick[j]) * e + w
            g_all[j], e_all[j] = w, e
        one, two = pl.reciprocal(d, approx=True), pl.reciprocal(e, approx=True)
        return n * one, d * one, p * two, e * two

    lax.fori_loop(0, total // ROWS, steps, (one, zero, one, zero))
    weight = weights[...]

    def centre(j, _):
        d, e = d_all[j], e_all[j]
        m_all[j] = m_all[j] / d
        g_all[j] = weight * (d * e) / (f_all[j] * e + g_all[j] * d)
        return 0

    lax.fori_loop(0, total, centre, 0, unroll=8)
    wide = out.shape[2]
    sub = lax.broadcasted_iota(jnp.int32, (ROWS, LANES), 0)
    lane = lax.broadcasted_iota(jnp.int32, (ROWS, wide), 1)
    row = lax.broadcasted_iota(jnp.int32, (ROWS, wide), 0)
    line = lambda ref, j, t: jnp.broadcast_to(ref[j, t:t + 1, :], (ROWS, LANES))

    def put(j, z, sums):
        new = []
        for c in range(classes):
            tiles = z[starts[c]:starts[c + 1]]
            total_tile = tiles[0]
            for tile in tiles[1:]:
                total_tile = total_tile + tile
            value = jnp.sum(total_tile, axis=1, keepdims=True)
            new.append(jnp.where(lane == j, value, sums[c]))
        return new

    for base in range(0, total, ROWS):
        z = [jnp.zeros((ROWS, LANES), jnp.float32)] * (starts[-1])
        sums = [jnp.zeros((ROWS, wide), jnp.float32)] * classes
        for i in range(ROWS - 1, -1, -1):
            j = base + i
            for t in range(starts[-1]):
                moved = z[t] * line(m_all, j + 1, t) if i < ROWS - 1 else z[t]
                z[t] = jnp.where(sub == i, line(g_all, j, t), moved)
            sums = put(j, z, sums)

        def above(back, state):
            z, sums = state
            for i in range(ROWS):
                j = base - 1 - back * ROWS - i
                z = [z[t] * line(m_all, j + 1, t) for t in range(starts[-1])]
                sums = put(j, z, sums)
            return z, sums

        if base:
            z, sums = lax.fori_loop(0, base // ROWS, above, (z, sums))
        for c in range(classes):
            out[c, base:base + ROWS, :] = sums[c] * jnp.where(lane == base + row, 0.5, 1.0)


def inverse_sums(my, thick, shifts, waves, size):
    total = thick.shape[0]
    classes = waves // 2 + 1
    lines, weights, counts = [], [], []
    for c in range(classes):
        k = c + waves * np.arange(size)
        weight = np.ones(size)
        if c in (0, waves // 2):
            partner = (waves * size - k) % (waves * size)
            weight = np.where(k < partner, 2.0, 1.0)[k <= partner]
            k = k[k <= partner]
        spare = -len(k) % LANES
        counts.append((len(k) + spare) // LANES)
        lines.append(np.pad(k, (0, spare)))
        weights.append(np.pad(weight, (0, spare)))
    spare = -sum(counts) % ROWS * LANES
    k = np.pad(np.concatenate(lines), (0, spare)).reshape(-1, LANES)
    weight = np.pad(np.concatenate(weights), (0, spare)).reshape(-1, LANES).astype(np.float32)
    across = horizontal(k, waves * size)
    wide = -(-total // LANES) * LANES
    return pl.pallas_call(
        functools.partial(inverse_kernel, counts),
        in_specs=[in_smem] * 3 + [in_vmem] * 2,
        out_shape=jax.ShapeDtypeStruct((classes, total, wide), jnp.float32),
        scratch_shapes=[pltpu.VMEM((total + 1, ROWS, LANES), jnp.float32)] + [pltpu.VMEM((total,) + across.shape, jnp.float32)] * 5,
        compiler_params=small,
        cost_estimate=lengthy,
        name="inverse_sums",
    )(my, thick, shifts, across, weight)


def interface_kernel(waves, matrices, edges, inverse, out):
    devices, _, wide = edges.shape
    total = wide // 2
    rows = 4 * waves
    lines = []
    for w in range(waves):
        line = edges[w]
        for d in range(1, devices // waves):
            line = line + edges[d * waves + w]
        lines.append(line)
    lines = jnp.concatenate(lines, 0)
    lines = jnp.concatenate([lines[:, :total], lines[:, total:]], 0)
    mixed = exact_dot(matrices[...], lines, NN)
    classes = inverse.shape[0]
    parts = jnp.concatenate([mixed[c * 2 * rows:(c + 1) * 2 * rows] for c in range(classes)], 1)
    squares = [inverse[c][:, :total] for c in range(classes)]
    result = exact_dot(parts, jnp.concatenate(squares, 0), NN) + exact_dot(parts, jnp.concatenate(squares, 1), NT)
    result = jnp.concatenate([result[:rows], result[rows:]], 1)
    for w in range(waves):
        line = result[4 * w:4 * w + 4]
        for d in range(devices // waves):
            out[d * waves + w] = line


def interface(edges, inverse, waves, size):
    return pl.pallas_call(
        functools.partial(interface_kernel, waves),
        in_specs=[in_vmem] * 3,
        out_specs=in_vmem,
        out_shape=jax.ShapeDtypeStruct(edges.shape, jnp.float32),
        compiler_params=small,
        name="interface",
    )(interface_matrices(waves, size), edges, inverse)


def back_kernel(levels, total, place, thick, values_v, spread_v, t, mine, theirs, sines_v, b, m_v, end_v, ot, orest, et, er, out0, out1, sems, t_v, b_v, ends, picked, u_all, q_all, out_v):
    _, _, _, ky, size = b_v.shape
    first = place[0] * levels
    half = size // 2
    many = half // LANES
    core = place[0] % 2
    copies = Copies(sems)
    table = copies.start(t, t_v)
    fields = [copies.start(b.at[a], b_v.at[a]) for a in range(2)]
    here, there = (pl.ds(pl.multiple_of(start * (ky // 2), ROWS), ky // 2) for start in (core, 1 - core))
    lane = lax.broadcasted_iota(jnp.int32, (ky, 2 * total), 1)
    for f in range(4):
        parts = [part.astype(jnp.float32) for part in split(values_v[:ky, f, :])]
        for j in range(total):
            spot = (lane == j) | (lane == total + j)
            for p in range(2):
                picked[p, j * ky:(j + 1) * ky, :] = jnp.where(spot, parts[p], 0.0).astype(jnp.bfloat16)
        u_all[f] = (real_dot(picked[0], spread_v[...]) + real_dot(picked[1], spread_v[...])).reshape(total, ky, 2 * LANES)
    table.wait()
    ends[:, :, :, here] = mine[...]
    ends[:, :, :, there] = theirs[...]

    def source(f, j, here):
        pair = u_all[f, j, here] * thick[j]
        return jnp.concatenate([pair[:, :LANES]] * many + [pair[:, LANES:]] * many, 1)

    def sweep(g, _):
        here = pl.ds(pl.multiple_of(g * ROWS, ROWS), ROWS)

        def from_above(block, y):
            for i in range(levels):
                j = block * levels + i
                step = t_v[j, here]
                y = [step * y[f] + source(f, j, here) for f in range(4)]
            return y

        def from_below(block, y):
            for i in range(levels):
                j = total - 1 - block * levels - i
                step = t_v[j + 1, here]
                y = [step * y[f] + source(f, j, here) for f in range(4)]
            return y

        zero = [jnp.zeros((ROWS, size), jnp.float32)] * 4
        wave = sines_v[...]
        for way, y in (
            (0, lax.fori_loop(0, place[0], from_above, zero)),
            (1, lax.fori_loop(0, total // levels - 1 - place[0], from_below, zero)),
        ):
            for f in range(4):
                ends[f // 2, way, f % 2, here] += wave * y[f]
        return 0

    lax.fori_loop(0, ky // ROWS, sweep, 0)
    rows = 2 * levels * ky
    lane = lax.broadcasted_iota(jnp.int32, (ky, LANES), 1)
    outs = []
    for a in range(2):
        fields[a].wait()

        def tile(g, _):
            here = pl.ds(pl.multiple_of(g * ROWS, ROWS), ROWS)
            wave = sines_v[...]
            for ri in range(2):
                y = ends[a, 0, ri, here]
                ys = []
                for j in range(levels):
                    y = b_v[a, ri, j, here] + wave * source(2 * a + ri, first + j, here) + m_v[j, here] * y
                    ys.append(y)
                value = (y + end_v[0, here] * ends[a, 1, ri, here]) * end_v[1, here]
                q_all[ri, levels - 1, here] = value
                for j in range(levels - 2, -1, -1):
                    value = m_v[j + 1, here] * (ys[j] * (0.5 * (thick[first + j] + thick[first + j + 1])) + value)
                    q_all[ri, j, here] = value
            return 0

        lax.fori_loop(0, ky // ROWS, tile, 0)
        low, high = to_cells(
            q_all[:, :, :, :half].reshape(rows, half), q_all[:, :, :, half:].reshape(rows, half), ot, orest, et, er
        )
        for ri in range(2):
            for j in range(levels):
                height = thick[first + j] if a else 1.0
                here = slice((ri * levels + j) * ky, (ri * levels + j + 1) * ky)
                u = u_all[2 * a + ri, first + j]
                u = (u[:, :LANES] + u[:, LANES:]) * (0.5 * height)
                if many > 1:
                    out_v[a, ri, j, :, LANES:half] = low[here, LANES:] * height
                out_v[a, ri, j, :, :LANES] = jnp.where(lane == 0, u, low[here, :LANES] * height)
                out_v[a, ri, j, :, half:] = high[here] * height
            outs.append(copies.start(out_v.at[a, ri], (out0, out1)[a].at[ri]))
    for copy in outs:
        copy.wait()


def back(place, thick, values, sines, t, m, end, b, mine, theirs):
    _, _, levels, ky, size = b.shape
    total = t.shape[0] - 1
    half = size // 2
    single = lambda *shape: pltpu.VMEM(shape, jnp.float32)
    return pl.pallas_call(
        functools.partial(back_kernel, levels, total),
        in_specs=[in_smem] * 2 + [in_vmem] * 2 + [in_hbm] + [in_vmem] * 3 + [in_hbm] + [in_vmem] * 6,
        out_specs=[in_hbm] * 2,
        out_shape=[jax.ShapeDtypeStruct((2, levels, ky, size), jnp.float32)] * 2,
        scratch_shapes=[
            pltpu.SemaphoreType.DMA((7,)),
            single(*t.shape),
            single(*b.shape),
            single(2, 2, 2, ky, size),
            pltpu.VMEM((2, total * ky, 2 * total), jnp.bfloat16),
            single(4, total, ky, 2 * LANES),
            single(2, levels, ky, size),
            single(2, 2, levels, ky, size),
        ],
        compiler_params=medium,
        name="back",
    )(place, thick, values, spread_matrix(total), t, mine, theirs, sines, b, m, end, *half_sines(size, True, 2.0 / size))


def shards(rhs, cotangent, thickness, ky_shift):
    waves = lax.axis_size("wave")
    count = lax.axis_size("depth")
    depth_pos = lax.axis_index("depth")
    wave_pos = lax.axis_index("wave")
    _, levels, ky, size = rhs.shape
    devices = waves * count
    chips = count // 2
    place = depth_pos.astype(jnp.int32).reshape(1)

    def across(a):
        return lax.ppermute(a, "depth", [(d, d ^ 1) for d in range(count)])

    def along(a, apart):
        return lax.ppermute(a, "depth", [(d, (d + 2 * apart) % count) for d in range(count)])

    def everywhere(a):
        return lax.all_to_all(a, ("depth", "wave"), split_axis=0, concat_axis=0, tiled=True)

    order = wave_order(size)
    sines = np.broadcast_to(np.sin(np.pi * order / size)[None, :], (ROWS, size)).astype(np.float32)
    across_k = horizontal(order, 2 * size)[None, :]
    t, m, end, b, local, give, edges = front(
        place, thickness, ky_shift, across_k, sines, rhs, cotangent, devices
    )

    my = (depth_pos * waves + wave_pos).astype(jnp.int32).reshape(1)
    got = across(give)
    edges = everywhere(edges)
    inverse = inverse_sums(my, thickness, ky_shift, waves, size)
    if chips == 4:
        both = lambda moves: [(2 * a + core, 2 * b + core) for a, b in moves for core in range(2)]
        first, second = pair_sums(place, local, got)
        near = lax.ppermute(first, "depth", both(((0, 1), (1, 0), (2, 3), (3, 2))))
        near, _, _ = lax.optimization_barrier((near, inverse, edges))
        grown = grow(place, local, second, near)
        news = [near] + [lax.ppermute(grown, "depth", both(moves)) for moves in (((1, 2), (2, 1)), ((1, 3), (2, 0)))]
    else:
        sums = chip_sums(place, local, got, chips)
        news = [along(sums[apart - 1], apart) for apart in range(1, chips)]
    values = interface(edges, inverse, waves, size)
    values = everywhere(values)
    news, _ = lax.optimization_barrier((news, values))
    mine, theirs = join(place, local, got, news)
    return back(place, thickness, values, sines, t, m, end, b, mine, across(theirs))


def solution(mesh):
    spec = P(None, "depth", None, "wave")
    return jax.shard_map(shards, mesh=mesh, in_specs=(spec, spec, P(), P()), out_specs=(spec, spec), check_vma=False)
```

```python
import functools
import math

import jax
import jax.numpy as jnp
import numpy as np
from jax import lax
from jax.experimental import pallas as pl
from jax.experimental.pallas import tpu as pltpu
from jax.sharding import PartitionSpec as P

aspect_ratio = 1.0
LANES = 128
ROWS = 8
VMEM_BYTES = 56 * 1024 * 1024
real_dot = functools.partial(jnp.dot, preferred_element_type=jnp.float32)
exact_dot = functools.partial(lax.dot_general, precision=lax.Precision.HIGHEST, preferred_element_type=jnp.float32)
NN = (((1,), (0,)), ((), ()))
NT = (((1,), (1,)), ((), ()))
in_smem = pl.BlockSpec(memory_space=pltpu.SMEM)
in_hbm = pl.BlockSpec(memory_space=pl.ANY)
in_vmem = pl.BlockSpec(memory_space=pltpu.VMEM)
params = pltpu.CompilerParams(vmem_limit_bytes=VMEM_BYTES)
small = pltpu.CompilerParams(vmem_limit_bytes=12 * 1024 * 1024)
medium = pltpu.CompilerParams(vmem_limit_bytes=46 * 1024 * 1024)
brief = pl.CostEstimate(flops=1, bytes_accessed=1, transcendentals=0)
lengthy = pl.CostEstimate(flops=20_000_000_000, bytes_accessed=40_000_000, transcendentals=0)


def wave_order(size):
    return np.concatenate([np.arange(1, size, 2), np.arange(0, size, 2)])


def half_sines(size, back=False, scale=1.0):
    half = size // 2
    place = np.arange(half)
    place[0] = half
    parts = []
    for waves in (np.arange(1, size, 2), np.arange(0, size, 2)):
        matrix = np.sin(np.pi * (np.outer(place, waves) % (2 * size)) / size)
        if waves[0] == 0:
            matrix[0] = 0.0
            matrix[:, 0] = 0.0
        matrix = (matrix.T if back else matrix).astype(np.float32) * np.float32(scale)
        top = matrix.astype(jnp.bfloat16)
        parts += [top, (matrix - top.astype(np.float32)).astype(jnp.bfloat16)]
    return parts


def edge_matrix(size, total):
    matrix = np.full((2 * LANES, 2 * total), 2.0 / size, np.float32)
    matrix[LANES:, total:] = -2.0 / size
    return matrix.astype(jnp.bfloat16)


def spread_matrix(total):
    matrix = np.ones((2 * total, 2 * LANES), np.float32)
    matrix[total:, LANES:] = -1.0
    return matrix.astype(jnp.bfloat16)


def interface_matrices(waves, size):
    classes = waves // 2 + 1
    matrix = np.zeros((2, classes, 2, waves, 4, waves, 4))
    for c in range(classes):
        weight = (1.0 if c in (0, waves // 2) else 2.0) / (size * waves)
        for w in range(waves):
            for e in range(2):
                for v in range(waves):
                    for g in range(2):
                        value = weight * math.cos(2.0 * math.pi * (c * (w + e - v - g) % waves) / waves)
                        for f in range(4):
                            matrix[g, c, e, w, f, v, f] = value
    matrix = matrix.reshape(2, classes * 2 * waves * 4, waves * 4)
    return np.concatenate([matrix[0], matrix[1]], 1).astype(np.float32)


def split(values):
    high = values.astype(jnp.bfloat16)
    return high, (values - high.astype(jnp.float32)).astype(jnp.bfloat16)


def product(values, top, rest):
    high, low = split(values)
    return real_dot(high, top[...]) + (real_dot(low, top[...]) + real_dot(high, rest[...]))


def mirror(values):
    rows = values.shape[0]
    lane = lax.broadcasted_iota(jnp.int32, (rows, LANES), 1)
    back = (LANES - lane) % LANES
    tiles = [values[:, a * LANES:(a + 1) * LANES] for a in range(values.shape[1] // LANES)]
    many = len(tiles)
    out = []
    for a in range(many):
        turned = jnp.take_along_axis(tiles[many - 1 - a], back, axis=1)
        out.append(jnp.where(lane == 0, tiles[(many - a) % many], turned))
    return jnp.concatenate(out, 1) if many > 1 else out[0]


def to_waves(values, odd_top, odd_rest, even_top, even_rest):
    half = values.shape[1] // 2
    low, high = values[:, :half], mirror(values[:, half:])
    lane = lax.broadcasted_iota(jnp.int32, low.shape, 1)
    low = jnp.where(lane == 0, 0.0, low)
    return product(low + high, odd_top, odd_rest), product(low - high, even_top, even_rest)


def to_cells(odd, even, odd_top, odd_rest, even_top, even_rest):
    p, m = product(odd, odd_top, odd_rest), product(even, even_top, even_rest)
    return p + m, mirror(p - m)


def horizontal(wavenumber, length):
    return (aspect_ratio * 4.0 * np.sin(math.pi * wavenumber / length) ** 2).astype(np.float32)


def set_faces(thick, faces):
    total = faces.shape[0] - 1
    two = jnp.full((ROWS, LANES), 2.0, jnp.float32)
    faces[0] = two / (two * 0.0 + thick[0])
    faces[total] = two * 0.0

    def one(j, _):
        faces[j] = two / (two * 0.0 + (thick[j - 1] + thick[j]))
        return 0

    lax.fori_loop(1, total, one, 0, unroll=3)


def spread_face(tile, like):
    rows, lanes = like.shape
    wide = jnp.concatenate([tile] * (lanes // LANES), 1) if lanes > LANES else tile
    return jnp.concatenate([wide] * (rows // ROWS), 0) if rows > ROWS else wide


class Copies:
    def __init__(self, sems):
        self.sems, self.used = sems, 0

    def start(self, source, target):
        copy = pltpu.make_async_copy(source, target, self.sems.at[self.used])
        self.used += 1
        copy.start()
        return copy


def coefficients(levels, total, group, place, thick, faces, shifts, across, t_out, m_out, end_out, pair_out, far_out, lam, m_chip, f_chip, n_chip, u_chip, down_all, up_all):
    ky = lam.shape[0]
    span = 2 * levels
    chips = total // span
    chip = place[0] // 2
    start = chip * span
    upper = place[0] % 2 == 0
    own = (place[0] % 2) * levels
    for row in range(ky):
        lam[row:row + 1, :] = across[...] + shifts[row]

    def down_step(shift, j, f, r):
        m = spread_face(faces[j], r) * r
        f = shift * thick[j] + m * f
        return m, f, 1.0 / (spread_face(faces[j + 1], f) + f)

    def up_step(shift, j, phi, s):
        n = spread_face(faces[j + 1], s) * s
        u = n * phi
        phi = shift * thick[j] + u
        return n, u, phi, 1.0 / (spread_face(faces[j], phi) + phi)

    def part(g, _):
        here = pl.ds(pl.multiple_of(g * group, group), group)
        shift = lam[here]
        one = jnp.ones_like(shift)
        zero = jnp.zeros_like(shift)

        def down_chip(c, state):
            f, r = state
            product = one
            for i in range(span):
                m, f, r = down_step(shift, c * span + i, f, r)
                t_out[c * span + i, here] = m
                product = product * m
            down_all[c] = product
            return f, r

        def up_chip(back, state):
            phi, s = state
            c = chips - 1 - back
            product = one
            for i in range(span - 1, -1, -1):
                n, _, phi, s = up_step(shift, c * span + i, phi, s)
                t_out[c * span + i + 1, here] = n
                product = product * n
            up_all[c] = product
            return phi, s

        f, r = lax.fori_loop(0, chip, down_chip, (one, one))
        for i in range(span):
            m, f, r = down_step(shift, start + i, f, r)
            m_chip[i], f_chip[i] = m, f
        phi, s = lax.fori_loop(0, chips - 1 - chip, up_chip, (zero, zero))
        for i in range(span - 1, -1, -1):
            n, u, phi, s = up_step(shift, start + i, phi, s)
            n_chip[i], u_chip[i] = n, u

        for i in range(levels):
            t_out[start + i, here] = m_chip[i]
            t_out[start + levels + 1 + i, here] = n_chip[levels + i]
        t_out[start + levels, here] = jnp.where(upper, n_chip[levels - 1], m_chip[levels])
        for i in range(levels):
            m_out[i, here] = m_chip[own + i]
        last = own + levels - 1
        end_out[0, here] = n_chip[last]
        end_out[1, here] = 1.0 / (f_chip[last] + u_chip[last])
        end_out[2, here] = f_chip[own] + u_chip[own]
        for core in range(2):
            down, up = m_chip[core * levels], n_chip[core * levels]
            for i in range(1, levels):
                down = down * m_chip[core * levels + i]
                up = up * n_chip[core * levels + i]
            pair_out[core, here] = down
            pair_out[2 + core, here] = up
        above, below = [one], [one]
        for apart in range(1, chips - 1):
            above.append(above[-1] * jnp.where(chip >= apart, down_all[jnp.maximum(chip - apart, 0)], one))
            below.append(below[-1] * jnp.where(chip + apart < chips, up_all[jnp.minimum(chip + apart, chips - 1)], one))
        for apart in range(1, chips):
            far_out[apart - 1, here] = jnp.where(chip >= apart, above[apart - 1], below[chips - apart - 1])
        return 0

    lax.fori_loop(0, ky // group, part, 0)


def lane_sum(values):
    tiles = [values[:, t * LANES:(t + 1) * LANES] for t in range(values.shape[1] // LANES)]
    while len(tiles) > 1:
        tiles = [a + b for a, b in zip(tiles[0::2], tiles[1::2])] + tiles[len(tiles) // 2 * 2:]
    return tiles[0]


def front_kernel(levels, total, group, place, thick, shifts, across, sines, edge_mix, x0, x1, odd_top, odd_rest, even_top, even_rest, t_out, m_out, end_out, b_out, local_out, give_out, edge_out, sems, *scratch):
    across_v, sines_v, mix_v, x, ot, orest, et, er, t, m, end, pair, far, b, c_all, z_all, sums, edges, faces, lam, *work = scratch
    _, _, _, ky, size = x.shape
    first = place[0] * levels
    half = size // 2
    copies = Copies(sems)
    early = [copies.start(across, across_v)]
    fields = [copies.start(x0, x.at[0])]
    mats = [copies.start(source, target) for source, target in ((odd_top, ot), (odd_rest, orest), (even_top, et), (even_rest, er))]
    mats += [copies.start(sines, sines_v)]
    fields += [copies.start(x1, x.at[1])]
    late = [copies.start(edge_mix, mix_v)]
    set_faces(thick, faces)
    for copy in early:
        copy.wait()
    coefficients(levels, total, group, place, thick, faces, shifts, across_v, t, m, end, pair, far, lam, *work)
    outs = [copies.start(source, target) for source, target in ((t, t_out), (m, m_out), (end, end_out))]
    for copy in mats:
        copy.wait()
    lane = lax.broadcasted_iota(jnp.int32, (ROWS, LANES), 1)
    spot = jnp.where(lane == 0, size / 4.0, 0.0)
    core = place[0] % 2
    mine, other = (pl.ds(pl.multiple_of(start * (ky // 2), ROWS), ky // 2) for start in (core, 1 - core))
    outs.append(copies.start(pair.at[:, mine], local_out.at[pl.ds(8, 4)]))
    outs.append(copies.start(far.at[:, mine], local_out.at[pl.ds(12, far.shape[0])]))

    def put(f, j, here, values, height, own=None):
        odd, even = lane_sum(values[:, :half]) * height, lane_sum(values[:, half:]) * height
        if own is not None:
            odd, even = odd + own, even + own
        sums[f, 0, j, here] = odd
        sums[f, 1, j, here] = even

    for a in range(2):
        fields[a].wait()
        odd, even = to_waves(x[a].reshape(2 * levels * ky, size), ot, orest, et, er)
        for ri in range(2):
            for j in range(levels):
                rows = slice((ri * levels + j) * ky, (ri * levels + j + 1) * ky)
                scale = thick[first + j] if a == 0 else 1.0
                b[a, ri, j, :, :half] = odd[rows] * scale
                b[a, ri, j, :, half:] = even[rows] * scale
        outs.append(copies.start(b.at[a], b_out.at[a]))
        for ri in range(2):
            f = 2 * a + ri

            def tile(g, _):
                here = pl.ds(pl.multiple_of(g * ROWS, ROWS), ROWS)
                wave = sines_v[...]
                y = b[a, ri, 0, here]
                ys = [y]
                for j in range(1, levels):
                    y = b[a, ri, j, here] + m[j, here] * y
                    ys.append(y)
                c_all[a, ri, here] = y
                value = y * end[1, here]
                z_all[1, f, here] = value * wave
                for j in range(levels - 1, -1, -1):
                    if j < levels - 1:
                        value = m[j + 1, here] * (ys[j] * (0.5 * (thick[first + j] + thick[first + j + 1])) + value)
                    height = thick[first + j]
                    own = jnp.broadcast_to(x[a, ri, j, here, 0:1], (ROWS, LANES)) * (spot * height if a == 0 else spot)
                    put(f, first + j, here, value * wave, height, own)
                z_all[0, f, here] = value * wave
                c_all[a, 2 + ri, here] = value * end[2, here]
                return 0

            lax.fori_loop(0, ky // ROWS, tile, 0)
        outs.append(copies.start(c_all.at[a, :, mine], local_out.at[pl.ds(4 * a, 4)]))
        outs.append(copies.start(c_all.at[a, :, other], give_out.at[a]))

    def reach(g, _):
        here = pl.ds(pl.multiple_of(g * ROWS, ROWS), ROWS)

        def up(block, z):
            for i in range(levels):
                j = first - 1 - block * levels - i
                step = t[j + 1, here]
                z = [step * one for one in z]
                for f in range(4):
                    put(f, j, here, z[f], thick[j])
            return z

        def down(block, z):
            for i in range(levels):
                j = first + levels + block * levels + i
                step = t[j, here]
                z = [step * one for one in z]
                for f in range(4):
                    put(f, j, here, z[f], thick[j])
            return z

        lax.fori_loop(0, place[0], up, [z_all[0, f, here] for f in range(4)])
        lax.fori_loop(0, total // levels - 1 - place[0], down, [z_all[1, f, here] for f in range(4)])
        return 0

    lax.fori_loop(0, ky // ROWS, reach, 0)
    for copy in late:
        copy.wait()
    if edges.shape[0] > ky:
        edges[...] = jnp.zeros_like(edges)
    wide = 2 * total
    lane = lax.broadcasted_iota(jnp.int32, (ky, wide), 1) % total
    for f in range(4):
        both = [sums[f, way].reshape(total * ky, LANES) for way in range(2)]
        high, low = split(jnp.concatenate(both, 1))
        spread = (real_dot(high, mix_v[...]) + real_dot(low, mix_v[...])).reshape(total, ky, wide)
        line = spread[0]
        for j in range(1, total):
            line = jnp.where(lane == j, spread[j], line)
        edges[:ky, f, :] = line
    outs.append(copies.start(edges, edge_out))
    for copy in outs:
        copy.wait()


def front(place, thick, shifts, across, sines, rhs, cotangent, devices):
    _, levels, ky, size = rhs.shape
    total = thick.shape[0]
    chips = total // (2 * levels)
    group = min(2 * ROWS, ky)
    half = size // 2
    wide = 2 * total
    single = lambda *shape: pltpu.VMEM(shape, jnp.float32)
    tables = [(n, ky, size) for n in (total + 1, levels, 3, 4, chips - 1)]
    shapes = tables[:3] + [(2, 2, levels, ky, size), (11 + chips, ky // 2, size), (2, 4, ky // 2, size), (devices, 4, wide)]
    return pl.pallas_call(
        functools.partial(front_kernel, levels, total, group),
        in_specs=[in_smem] * 3 + [in_hbm] * 9,
        out_specs=[in_hbm] * len(shapes),
        out_shape=[jax.ShapeDtypeStruct(shape, jnp.float32) for shape in shapes],
        scratch_shapes=[
            pltpu.SemaphoreType.DMA((22,)),
            single(1, size),
            single(ROWS, size),
            pltpu.VMEM((2 * LANES, wide), jnp.bfloat16),
            single(2, 2, levels, ky, size),
            *[pltpu.VMEM((half, half), jnp.bfloat16)] * 4,
            *[single(*shape) for shape in tables],
            single(2, 2, levels, ky, size),
            single(2, 4, ky, size),
            single(2, 4, ky, size),
            single(4, 2, total, ky, LANES),
            single(devices, 4, wide),
            single(total + 1, ROWS, LANES),
            single(ky, size),
            *[single(2 * levels, group, size)] * 4,
            *[single(chips, group, size)] * 2,
        ],
        compiler_params=params,
        name="front",
    )(place, thick, shifts, across, sines, edge_matrix(size, total), rhs, cotangent, *half_sines(size))


def chip_kernel(chips, place, local, got, *refs):
    outs = refs[:chips - 1]
    sems, down_v, up_v = refs[chips - 1:]
    chip = place[0] // 2
    upper = place[0] % 2 == 0
    for a in range(2):
        for ri in range(2):
            sums = [(local[4 * a + 2 * way + ri], got[a, 2 * way + ri]) for way in range(2)]
            first, second = ([jnp.where(upper, *one[::turn]) for one in sums] for turn in (1, -1))
            down_v[2 * a + ri] = second[0] + local[9] * first[0]
            up_v[2 * a + ri] = first[1] + local[10] * second[1]
    for apart in range(1, chips):
        goes_down = chip + apart < chips
        sem = sems.at[apart - 1]

        @pl.when(goes_down)
        def _():
            pltpu.make_async_copy(down_v, outs[apart - 1], sem).start()

        @pl.when(jnp.logical_not(goes_down))
        def _():
            pltpu.make_async_copy(up_v, outs[apart - 1], sem).start()

    for apart in range(1, chips):
        pltpu.make_async_copy(down_v, outs[apart - 1], sems.at[apart - 1]).wait()


def chip_sums(place, local, got, chips):
    _, half, size = local.shape
    shape = (4, half, size)
    return pl.pallas_call(
        functools.partial(chip_kernel, chips),
        in_specs=[in_smem] + [in_vmem] * 2,
        out_specs=[in_hbm] * (chips - 1),
        out_shape=[jax.ShapeDtypeStruct(shape, jnp.float32)] * (chips - 1),
        scratch_shapes=[
            pltpu.SemaphoreType.DMA((chips - 1,)),
            pltpu.VMEM(shape, jnp.float32),
            pltpu.VMEM(shape, jnp.float32),
        ],
        compiler_params=small,
        cost_estimate=brief,
        name="chip_sums",
    )(place, local, got)


def pair_kernel(place, local, got, first_out, second_out):
    even = (place[0] // 2) % 2 == 0
    upper = place[0] % 2 == 0
    for a in range(2):
        for ri in range(2):
            sums = [(local[4 * a + 2 * way + ri], got[a, 2 * way + ri]) for way in range(2)]
            first, second = ([jnp.where(upper, *one[::turn]) for one in sums] for turn in (1, -1))
            down = second[0] + local[9] * first[0]
            up = first[1] + local[10] * second[1]
            first_out[2 * a + ri] = jnp.where(even, down, up)
            second_out[2 * a + ri] = jnp.where(even, up, down)


def pair_sums(place, local, got):
    shape = jax.ShapeDtypeStruct((4,) + local.shape[1:], jnp.float32)
    return pl.pallas_call(
        pair_kernel,
        in_specs=[in_smem] + [in_vmem] * 2,
        out_specs=[in_vmem] * 2,
        out_shape=[shape] * 2,
        compiler_params=small,
        cost_estimate=brief,
        name="pair_sums",
    )(place, local, got)


def grow_kernel(place, local, second, near, out):
    even = (place[0] // 2) % 2 == 0
    factor = jnp.where(even, local[10] * local[11], local[8] * local[9])
    for i in range(4):
        out[i] = second[i] + factor * near[i]


def grow(place, local, second, near):
    return pl.pallas_call(
        grow_kernel,
        in_specs=[in_smem] + [in_vmem] * 3,
        out_specs=in_vmem,
        out_shape=jax.ShapeDtypeStruct(second.shape, jnp.float32),
        compiler_params=small,
        cost_estimate=brief,
        name="grow",
    )(place, local, second, near)


def join_kernel(chips, place, local, got, *refs):
    news = refs[:chips - 1]
    mine, theirs = refs[chips - 1:]
    chip = place[0] // 2
    upper = place[0] % 2 == 0
    for a in range(2):
        for ri in range(2):
            sums = [(local[4 * a + 2 * way + ri], got[a, 2 * way + ri]) for way in range(2)]
            first, second = ([jnp.where(upper, *one[::turn]) for one in sums] for turn in (1, -1))
            down = jnp.zeros(local.shape[1:], jnp.float32)
            up = down
            if chips == 4:
                near, middle, outer = (one[2 * a + ri] for one in news)
                outer = near + local[13] * outer
                down = jnp.where(chip == 0, 0.0, jnp.where(chip == 1, near, jnp.where(chip == 2, middle, outer)))
                up = jnp.where(chip == 3, 0.0, jnp.where(chip == 2, near, jnp.where(chip == 1, middle, outer)))
            for apart in range(1, chips if chips != 4 else 0):
                term = local[11 + apart] * news[apart - 1][2 * a + ri]
                down = down + jnp.where(chip >= apart, term, 0.0)
                up = up + jnp.where(chip >= apart, 0.0, term)
            inner_up = second[1] + local[11] * up
            inner_down = first[0] + local[8] * down
            mine[a, 0, ri] = jnp.where(upper, down, inner_down)
            mine[a, 1, ri] = jnp.where(upper, inner_up, up)
            theirs[a, 0, ri] = jnp.where(upper, inner_down, down)
            theirs[a, 1, ri] = jnp.where(upper, up, inner_up)


def join(place, local, got, news):
    chips = len(news) + 1
    _, half, size = local.shape
    return pl.pallas_call(
        functools.partial(join_kernel, chips),
        in_specs=[in_smem] + [in_vmem] * (1 + chips),
        out_specs=[in_vmem] * 2,
        out_shape=[jax.ShapeDtypeStruct((2, 2, 2, half, size), jnp.float32)] * 2,
        compiler_params=small,
        cost_estimate=lengthy,
        name="join",
    )(place, local, got, *news)


def inverse_kernel(counts, my, thick, shifts, across, weights, out, faces, m_all, g_all, d_all, f_all, e_all):
    total = f_all.shape[0]
    classes = out.shape[0]
    ky = shifts.shape[0]
    starts = [sum(counts[:c]) for c in range(classes + 1)]
    set_faces(thick, faces)
    shift = across[...] + jnp.where(my[0] < ky, shifts[jnp.minimum(my[0], ky - 1)], 1.0)
    one = jnp.ones_like(shift)
    zero = jnp.zeros_like(shift)

    def steps(block, state):
        n, d, p, e = state
        for i in range(ROWS):
            j = block * ROWS + i
            q = spread_face(faces[j], n)
            a = q * d
            d = a + n
            n = (shift * thick[j]) * d + q * n
            m_all[j], d_all[j], f_all[j] = a, d, n
            j = total - 1 - j
            q = spread_face(faces[j + 1], p)
            w = q * p
            e = q * e + p
            p = (shift * thick[j]) * e + w
            g_all[j], e_all[j] = w, e
        one, two = pl.reciprocal(d, approx=True), pl.reciprocal(e, approx=True)
        return n * one, d * one, p * two, e * two

    lax.fori_loop(0, total // ROWS, steps, (one, zero, one, zero))
    weight = weights[...]

    def centre(j, _):
        d, e = d_all[j], e_all[j]
        m_all[j] = m_all[j] / d
        g_all[j] = weight * (d * e) / (f_all[j] * e + g_all[j] * d)
        return 0

    lax.fori_loop(0, total, centre, 0, unroll=8)
    wide = out.shape[2]
    sub = lax.broadcasted_iota(jnp.int32, (ROWS, LANES), 0)
    lane = lax.broadcasted_iota(jnp.int32, (ROWS, wide), 1)
    row = lax.broadcasted_iota(jnp.int32, (ROWS, wide), 0)
    line = lambda ref, j, t: jnp.broadcast_to(ref[j, t:t + 1, :], (ROWS, LANES))

    def put(j, z, sums):
        new = []
        for c in range(classes):
            tiles = z[starts[c]:starts[c + 1]]
            total_tile = tiles[0]
            for tile in tiles[1:]:
                total_tile = total_tile + tile
            value = jnp.sum(total_tile, axis=1, keepdims=True)
            new.append(jnp.where(lane == j, value, sums[c]))
        return new

    for base in range(0, total, ROWS):
        z = [jnp.zeros((ROWS, LANES), jnp.float32)] * (starts[-1])
        sums = [jnp.zeros((ROWS, wide), jnp.float32)] * classes
        for i in range(ROWS - 1, -1, -1):
            j = base + i
            for t in range(starts[-1]):
                moved = z[t] * line(m_all, j + 1, t) if i < ROWS - 1 else z[t]
                z[t] = jnp.where(sub == i, line(g_all, j, t), moved)
            sums = put(j, z, sums)

        def above(back, state):
            z, sums = state
            for i in range(ROWS):
                j = base - 1 - back * ROWS - i
                z = [z[t] * line(m_all, j + 1, t) for t in range(starts[-1])]
                sums = put(j, z, sums)
            return z, sums

        if base:
            z, sums = lax.fori_loop(0, base // ROWS, above, (z, sums))
        for c in range(classes):
            out[c, base:base + ROWS, :] = sums[c] * jnp.where(lane == base + row, 0.5, 1.0)


def inverse_sums(my, thick, shifts, waves, size):
    total = thick.shape[0]
    classes = waves // 2 + 1
    lines, weights, counts = [], [], []
    for c in range(classes):
        k = c + waves * np.arange(size)
        weight = np.ones(size)
        if c in (0, waves // 2):
            partner = (waves * size - k) % (waves * size)
            weight = np.where(k < partner, 2.0, 1.0)[k <= partner]
            k = k[k <= partner]
        spare = -len(k) % LANES
        counts.append((len(k) + spare) // LANES)
        lines.append(np.pad(k, (0, spare)))
        weights.append(np.pad(weight, (0, spare)))
    spare = -sum(counts) % ROWS * LANES
    k = np.pad(np.concatenate(lines), (0, spare)).reshape(-1, LANES)
    weight = np.pad(np.concatenate(weights), (0, spare)).reshape(-1, LANES).astype(np.float32)
    across = horizontal(k, waves * size)
    wide = -(-total // LANES) * LANES
    return pl.pallas_call(
        functools.partial(inverse_kernel, counts),
        in_specs=[in_smem] * 3 + [in_vmem] * 2,
        out_shape=jax.ShapeDtypeStruct((classes, total, wide), jnp.float32),
        scratch_shapes=[pltpu.VMEM((total + 1, ROWS, LANES), jnp.float32)] + [pltpu.VMEM((total,) + across.shape, jnp.float32)] * 5,
        compiler_params=small,
        cost_estimate=lengthy,
        name="inverse_sums",
    )(my, thick, shifts, across, weight)


def interface_kernel(waves, matrices, edges, inverse, out):
    devices, _, wide = edges.shape
    total = wide // 2
    rows = 4 * waves
    lines = []
    for w in range(waves):
        line = edges[w]
        for d in range(1, devices // waves):
            line = line + edges[d * waves + w]
        lines.append(line)
    lines = jnp.concatenate(lines, 0)
    lines = jnp.concatenate([lines[:, :total], lines[:, total:]], 0)
    mixed = exact_dot(matrices[...], lines, NN)
    classes = inverse.shape[0]
    parts = jnp.concatenate([mixed[c * 2 * rows:(c + 1) * 2 * rows] for c in range(classes)], 1)
    squares = [inverse[c][:, :total] for c in range(classes)]
    result = exact_dot(parts, jnp.concatenate(squares, 0), NN) + exact_dot(parts, jnp.concatenate(squares, 1), NT)
    result = jnp.concatenate([result[:rows], result[rows:]], 1)
    for w in range(waves):
        line = result[4 * w:4 * w + 4]
        for d in range(devices // waves):
            out[d * waves + w] = line


def interface(edges, inverse, waves, size):
    return pl.pallas_call(
        functools.partial(interface_kernel, waves),
        in_specs=[in_vmem] * 3,
        out_specs=in_vmem,
        out_shape=jax.ShapeDtypeStruct(edges.shape, jnp.float32),
        compiler_params=small,
        name="interface",
    )(interface_matrices(waves, size), edges, inverse)


def back_kernel(levels, total, place, thick, values_v, spread_v, t, mine, theirs, sines_v, b, m_v, end_v, ot, orest, et, er, out0, out1, sems, t_v, b_v, ends, picked, u_all, q_all, out_v):
    _, _, _, ky, size = b_v.shape
    first = place[0] * levels
    half = size // 2
    many = half // LANES
    core = place[0] % 2
    copies = Copies(sems)
    table = copies.start(t, t_v)
    fields = [copies.start(b.at[a], b_v.at[a]) for a in range(2)]
    here, there = (pl.ds(pl.multiple_of(start * (ky // 2), ROWS), ky // 2) for start in (core, 1 - core))
    lane = lax.broadcasted_iota(jnp.int32, (ky, 2 * total), 1)
    for f in range(4):
        parts = [part.astype(jnp.float32) for part in split(values_v[:ky, f, :])]
        for j in range(total):
            spot = (lane == j) | (lane == total + j)
            for p in range(2):
                picked[p, j * ky:(j + 1) * ky, :] = jnp.where(spot, parts[p], 0.0).astype(jnp.bfloat16)
        u_all[f] = (real_dot(picked[0], spread_v[...]) + real_dot(picked[1], spread_v[...])).reshape(total, ky, 2 * LANES)
    table.wait()
    ends[:, :, :, here] = mine[...]
    ends[:, :, :, there] = theirs[...]

    def source(f, j, here):
        pair = u_all[f, j, here] * thick[j]
        return jnp.concatenate([pair[:, :LANES]] * many + [pair[:, LANES:]] * many, 1)

    def sweep(g, _):
        here = pl.ds(pl.multiple_of(g * ROWS, ROWS), ROWS)

        def from_above(block, y):
            for i in range(levels):
                j = block * levels + i
                step = t_v[j, here]
                y = [step * y[f] + source(f, j, here) for f in range(4)]
            return y

        def from_below(block, y):
            for i in range(levels):
                j = total - 1 - block * levels - i
                step = t_v[j + 1, here]
                y = [step * y[f] + source(f, j, here) for f in range(4)]
            return y

        zero = [jnp.zeros((ROWS, size), jnp.float32)] * 4
        wave = sines_v[...]
        for way, y in (
            (0, lax.fori_loop(0, place[0], from_above, zero)),
            (1, lax.fori_loop(0, total // levels - 1 - place[0], from_below, zero)),
        ):
            for f in range(4):
                ends[f // 2, way, f % 2, here] += wave * y[f]
        return 0

    lax.fori_loop(0, ky // ROWS, sweep, 0)
    rows = 2 * levels * ky
    lane = lax.broadcasted_iota(jnp.int32, (ky, LANES), 1)
    outs = []
    for a in range(2):
        fields[a].wait()

        def tile(g, _):
            here = pl.ds(pl.multiple_of(g * ROWS, ROWS), ROWS)
            wave = sines_v[...]
            for ri in range(2):
                y = ends[a, 0, ri, here]
                ys = []
                for j in range(levels):
                    y = b_v[a, ri, j, here] + wave * source(2 * a + ri, first + j, here) + m_v[j, here] * y
                    ys.append(y)
                value = (y + end_v[0, here] * ends[a, 1, ri, here]) * end_v[1, here]
                q_all[ri, levels - 1, here] = value
                for j in range(levels - 2, -1, -1):
                    value = m_v[j + 1, here] * (ys[j] * (0.5 * (thick[first + j] + thick[first + j + 1])) + value)
                    q_all[ri, j, here] = value
            return 0

        lax.fori_loop(0, ky // ROWS, tile, 0)
        low, high = to_cells(
            q_all[:, :, :, :half].reshape(rows, half), q_all[:, :, :, half:].reshape(rows, half), ot, orest, et, er
        )
        for ri in range(2):
            for j in range(levels):
                height = thick[first + j] if a else 1.0
                here = slice((ri * levels + j) * ky, (ri * levels + j + 1) * ky)
                u = u_all[2 * a + ri, first + j]
                u = (u[:, :LANES] + u[:, LANES:]) * (0.5 * height)
                if many > 1:
                    out_v[a, ri, j, :, LANES:half] = low[here, LANES:] * height
                out_v[a, ri, j, :, :LANES] = jnp.where(lane == 0, u, low[here, :LANES] * height)
                out_v[a, ri, j, :, half:] = high[here] * height
            outs.append(copies.start(out_v.at[a, ri], (out0, out1)[a].at[ri]))
    for copy in outs:
        copy.wait()


def back(place, thick, values, sines, t, m, end, b, mine, theirs):
    _, _, levels, ky, size = b.shape
    total = t.shape[0] - 1
    half = size // 2
    single = lambda *shape: pltpu.VMEM(shape, jnp.float32)
    return pl.pallas_call(
        functools.partial(back_kernel, levels, total),
        in_specs=[in_smem] * 2 + [in_vmem] * 2 + [in_hbm] + [in_vmem] * 3 + [in_hbm] + [in_vmem] * 6,
        out_specs=[in_hbm] * 2,
        out_shape=[jax.ShapeDtypeStruct((2, levels, ky, size), jnp.float32)] * 2,
        scratch_shapes=[
            pltpu.SemaphoreType.DMA((7,)),
            single(*t.shape),
            single(*b.shape),
            single(2, 2, 2, ky, size),
            pltpu.VMEM((2, total * ky, 2 * total), jnp.bfloat16),
            single(4, total, ky, 2 * LANES),
            single(2, levels, ky, size),
            single(2, 2, levels, ky, size),
        ],
        compiler_params=medium,
        name="back",
    )(place, thick, values, spread_matrix(total), t, mine, theirs, sines, b, m, end, *half_sines(size, True, 2.0 / size))


def shards(rhs, cotangent, thickness, ky_shift):
    waves = lax.axis_size("wave")
    count = lax.axis_size("depth")
    depth_pos = lax.axis_index("depth")
    wave_pos = lax.axis_index("wave")
    _, levels, ky, size = rhs.shape
    devices = waves * count
    chips = count // 2
    place = depth_pos.astype(jnp.int32).reshape(1)

    def across(a):
        return lax.ppermute(a, "depth", [(d, d ^ 1) for d in range(count)])

    def along(a, apart):
        return lax.ppermute(a, "depth", [(d, (d + 2 * apart) % count) for d in range(count)])

    def everywhere(a):
        return lax.all_to_all(a, ("depth", "wave"), split_axis=0, concat_axis=0, tiled=True)

    order = wave_order(size)
    sines = np.broadcast_to(np.sin(np.pi * order / size)[None, :], (ROWS, size)).astype(np.float32)
    across_k = horizontal(order, 2 * size)[None, :]
    t, m, end, b, local, give, edges = front(
        place, thickness, ky_shift, across_k, sines, rhs, cotangent, devices
    )

    my = (depth_pos * waves + wave_pos).astype(jnp.int32).reshape(1)
    got = across(give)
    edges = everywhere(edges)
    inverse = inverse_sums(my, thickness, ky_shift, waves, size)
    if chips == 4:
        both = lambda moves: [(2 * a + core, 2 * b + core) for a, b in moves for core in range(2)]
        first, second = pair_sums(place, local, got)
        near = lax.ppermute(first, "depth", both(((0, 1), (1, 0), (2, 3), (3, 2))))
        values = interface(edges, inverse, waves, size)
        near, values = lax.optimization_barrier((near, values))
        grown = grow(place, local, second, near)
        grown, values = lax.optimization_barrier((grown, values))
        news = [near] + [lax.ppermute(grown, "depth", both(moves)) for moves in (((1, 2), (2, 1)), ((1, 3), (2, 0)))]
    else:
        sums = chip_sums(place, local, got, chips)
        news = [along(sums[apart - 1], apart) for apart in range(1, chips)]
    if chips != 4:
        values = interface(edges, inverse, waves, size)
    values = everywhere(values)
    news, _ = lax.optimization_barrier((news, values))
    mine, theirs = join(place, local, got, news)
    return back(place, thickness, values, sines, t, m, end, b, mine, across(theirs))


def solution(mesh):
    spec = P(None, "depth", None, "wave")
    return jax.shard_map(shards, mesh=mesh, in_specs=(spec, spec, P(), P()), out_specs=(spec, spec), check_vma=False)
```
